32 devices in a mesh: chan: 4 (over z), bfly: 2 (over x), samp: 4 (over y, core).
Axes of the slice: x: 2, y: 2, z: 4, core: 2. Of those that a mesh axis runs over, the one named last changes fastest.
Arguments:
- features: bfloat16 [65536, 2048], P(('chan', 'bfly'), 'samp'), may hold values from -6 to 6
- cotangent: bfloat16 [65536, 2048], P(('chan', 'bfly'), 'samp'), may hold values from -6 to 6
- right_factor: bfloat16 [2, 256, 256, 256], P(None, ('chan', 'bfly')), may hold values from -0.375 to 0.375
- left_factor: float32 [2, 256, 256, 256], P(None, ('chan', 'bfly')), may hold values from -0.375 to 0.375
- mixing: float32 [2, 2, 256, 256], P(None, None, ('chan', 'bfly')), may hold values from -1.2 to 1.2
Outputs:
- output: bfloat16 [65536, 2048], P(('chan', 'bfly'), 'samp')
- feature_grad: bfloat16 [65536, 2048], P(('chan', 'bfly'), 'samp')
- grad_right: float32 [2, 256, 256, 256], P(None, ('chan', 'bfly'))
- grad_left: float32 [2, 256, 256, 256], P(None, ('chan', 'bfly'))
- grad_mixing: float32 [2, 2, 256, 256], P(None, None, ('chan', 'bfly'))
The draws below stay inside these ranges and needn't reach their ends.
All inputs are finite; a program needn't handle non-finite values.
Results may differ from the reference program's by a relative error of at most 0.025.
Values may be sent and summed in bfloat16 or wider, within the bound.
No kernel may reach another device: no remote copies, remote signals or barrier semaphores. Data moves between devices by JAX's collectives and lax.ppermute only.
A program may use at most 320 MiB of HBM per device.

```python
import jax
import jax.numpy as jnp
from jax import lax

BLOCK = 256
LAYERS = 2
SAMP_DEV = 512
WIDTH = 65536
SAMPLES = 2048
BLK_DEV = 32


def shard_levels(key, dims, pieces, smallest, top_value):
    loudness = 1.0
    for dim, parts in pieces:
        draws = jax.random.uniform(jax.random.fold_in(jax.random.fold_in(key, 6), dim), (parts,), jnp.float32, smallest / len(pieces), top_value / len(pieces))
        loudness = loudness * jnp.repeat(jnp.exp(draws), dims[dim] // parts).reshape((-1,) + (1,) * (len(dims) - 1 - dim))
    return loudness


def centred(rng, dims, width, reach, split=(), kind=jnp.bfloat16):
    factor_of = shard_levels(rng, dims, split, -0.22, 0.18) if split else 1.0
    result = jax.random.normal(rng, dims, jnp.float32) * width * factor_of
    return jnp.minimum(jnp.maximum(result, -reach), reach).astype(kind)


def setup_inputs(seed: int = 0) -> dict:
    splits = jax.random.split(jax.random.key(seed), 6)
    return {
        "features": centred(splits[0], (WIDTH, SAMPLES), 1.0, 6.0, ((0, 8), (1, 4))),
        "cotangent": centred(splits[1], (WIDTH, SAMPLES), 1.0, 6.0, ((0, 8), (1, 4))),
        "right_factor": centred(splits[2], (LAYERS, BLOCK, BLOCK, BLOCK), BLOCK ** -0.5, 0.375, ((1, 8),)),
        "left_factor": centred(splits[3], (LAYERS, BLOCK, BLOCK, BLOCK), BLOCK ** -0.5, 0.375, ((1, 8),), jnp.float32),
        "mixing": jnp.clip(jax.random.uniform(splits[4], (LAYERS, 2, BLOCK, BLOCK), jnp.float32, -1.2, 1.2) * shard_levels(splits[4], (LAYERS, 2, BLOCK, BLOCK), ((2, 8),), -0.4, 0.0), -1.2, 1.2),
    }


def flip_pairs(values, span):
    shape = values.shape
    grouped = values.reshape((shape[0] // (2 * span), 2, span) + shape[1:])
    return grouped[:, ::-1].reshape(shape)


def run_block(features, cotangent, right_factor, left_factor, mixing):
    samples = features.shape[1]
    height = features.reshape(BLOCK, BLOCK, samples)
    saved = []
    for layer_index in range(LAYERS):
        right_full = right_factor[layer_index].astype(jnp.float32)
        left_full = left_factor[layer_index].astype(jnp.float32)
        self_gain = mixing[layer_index, 0][:, :, None]
        cross_gain = mixing[layer_index, 1][:, :, None]
        mixed_u = jnp.einsum('bis,bij->bjs', height.astype(jnp.float32), right_full).astype(jnp.bfloat16)
        partner = flip_pairs(mixed_u, BLK_DEV)
        mixed_v = (self_gain * mixed_u.astype(jnp.float32) + cross_gain * partner.astype(jnp.float32)).astype(jnp.bfloat16)
        outer = jnp.einsum('bjs,jbk->kjs', mixed_v.astype(jnp.float32), left_full).astype(jnp.bfloat16)
        saved.append((height, mixed_u, partner, mixed_v, outer))
        height = (height.astype(jnp.float32) + jax.nn.silu(outer.astype(jnp.float32))).astype(jnp.bfloat16)
    output = height.reshape(WIDTH, samples)
    grad = cotangent.reshape(BLOCK, BLOCK, samples)
    rights = [None] * LAYERS
    lefts = [None] * LAYERS
    mixes = [None] * LAYERS
    for layer_index in reversed(range(LAYERS)):
        height_in, mixed_u, partner, mixed_v, outer = saved[layer_index]
        right_full = right_factor[layer_index].astype(jnp.float32)
        left_full = left_factor[layer_index].astype(jnp.float32)
        self_gain = mixing[layer_index, 0][:, :, None]
        cross_gain = mixing[layer_index, 1][:, :, None]
        before = outer.astype(jnp.float32)
        logistic = jax.nn.sigmoid(before)
        error = (grad.astype(jnp.float32) * logistic * (1.0 + before * (1.0 - logistic))).astype(jnp.bfloat16)
        error_full = error.astype(jnp.float32)
        lefts[layer_index] = jnp.einsum('bjs,kjs->jbk', mixed_v.astype(jnp.float32), error_full)
        grad_v = jnp.einsum('jbk,kjs->bjs', left_full, error_full).astype(jnp.bfloat16)
        grad_vf = grad_v.astype(jnp.float32)
        mixes[layer_index] = jnp.stack([jnp.sum(grad_vf * mixed_u.astype(jnp.float32), axis=2), jnp.sum(grad_vf * partner.astype(jnp.float32), axis=2)])
        carried = lax.optimization_barrier((cross_gain * grad_vf).astype(jnp.bfloat16))
        grad_u = (self_gain * grad_vf + flip_pairs(carried, BLK_DEV).astype(jnp.float32)).astype(jnp.bfloat16)
        grad_uf = grad_u.astype(jnp.float32)
        rights[layer_index] = jnp.einsum('bis,bjs->bij', height_in.astype(jnp.float32), grad_uf)
        grad = (grad.astype(jnp.float32) + jnp.einsum('bij,bjs->bis', right_full, grad_uf)).astype(jnp.bfloat16)
    return output, grad.reshape(WIDTH, samples), (jnp.stack(rights), jnp.stack(lefts), jnp.stack(mixes))


def reference(features, cotangent, right_factor, left_factor, mixing):
    count = features.shape[1] // SAMP_DEV

    def one_block(carry, index):
        start = (index * SAMP_DEV).astype(jnp.int32)
        feat_block = lax.dynamic_slice_in_dim(features, start, SAMP_DEV, 1)
        cot_block = lax.dynamic_slice_in_dim(cotangent, start, SAMP_DEV, 1)
        out_block, grad_block, grads = run_block(feat_block, cot_block, right_factor, left_factor, mixing)
        carry = (carry[0] + grads[0], carry[1] + grads[1], carry[2] + grads[2])
        return carry, (out_block, grad_block)

    start_sums = (jnp.zeros((LAYERS, BLOCK, BLOCK, BLOCK), jnp.float32), jnp.zeros((LAYERS, BLOCK, BLOCK, BLOCK), jnp.float32), jnp.zeros((LAYERS, 2, BLOCK, BLOCK), jnp.float32))
    sums, stacked = lax.scan(one_block, start_sums, jnp.arange(count, dtype=jnp.int32))
    output = jnp.transpose(stacked[0], (1, 0, 2)).reshape(WIDTH, count * SAMP_DEV)
    feature_grad = jnp.transpose(stacked[1], (1, 0, 2)).reshape(WIDTH, count * SAMP_DEV)
    return output, feature_grad, sums[0], sums[1], sums[2]
```

```python
import jax
import jax.numpy as jnp
from jax import lax
from jax.sharding import PartitionSpec as P

BLOCK = 256
LAYERS = 2
ROW_AXES = ("chan", "bfly")


def to_columns(values):
    return lax.all_to_all(values, ROW_AXES, split_axis=1, concat_axis=0, tiled=True)


def to_rows(values):
    return lax.all_to_all(values, ROW_AXES, split_axis=0, concat_axis=1, tiled=True)


def local(features, cotangent, right_factor, left_factor, mixing):
    blocks = right_factor.shape[1]
    samples = features.shape[1]
    pairs = lax.axis_size("bfly")

    def flip(values):
        grouped = values.reshape((-1, pairs // 2, 2, blocks) + values.shape[1:])
        return grouped[:, :, ::-1].reshape(values.shape)

    left_bf = left_factor.astype(jnp.bfloat16)
    gains = lax.all_to_all(mixing, ROW_AXES, split_axis=3, concat_axis=2, tiled=True)
    height = features.reshape(blocks, BLOCK, samples)
    saved = []
    for layer in range(LAYERS):
        self_gain = gains[layer, 0][:, :, None]
        cross_gain = gains[layer, 1][:, :, None]
        mixed_u = to_columns(
            jnp.einsum(
                "bis,bij->bjs", height, right_factor[layer], preferred_element_type=jnp.float32
            ).astype(jnp.bfloat16)
        )
        mixed_v = (
            self_gain * mixed_u.astype(jnp.float32) + cross_gain * flip(mixed_u).astype(jnp.float32)
        ).astype(jnp.bfloat16)
        outer = jnp.einsum(
            "bjs,jbk->kjs", mixed_v, left_bf[layer], preferred_element_type=jnp.float32
        ).astype(jnp.bfloat16)
        activation = to_rows(outer)
        saved.append((height, mixed_u, mixed_v, activation))
        height = (height.astype(jnp.float32) + jax.nn.silu(activation.astype(jnp.float32))).astype(
            jnp.bfloat16
        )
    output = height.reshape(blocks * BLOCK, samples)
    grad = cotangent.reshape(blocks, BLOCK, samples)
    rights = [None] * LAYERS
    lefts = [None] * LAYERS
    mixes = [None] * LAYERS
    for layer in reversed(range(LAYERS)):
        height_in, mixed_u, mixed_v, activation = saved[layer]
        self_gain = gains[layer, 0][:, :, None]
        cross_gain = gains[layer, 1][:, :, None]
        before = activation.astype(jnp.float32)
        logistic = jax.nn.sigmoid(before)
        error = (grad.astype(jnp.float32) * logistic * (1.0 + before * (1.0 - logistic))).astype(
            jnp.bfloat16
        )
        error_cols = to_columns(error)
        grad_v = jnp.einsum(
            "jbk,kjs->bjs", left_bf[layer], error_cols, preferred_element_type=jnp.float32
        ).astype(jnp.bfloat16)
        grad_vf = grad_v.astype(jnp.float32)
        carried = (cross_gain * grad_vf).astype(jnp.bfloat16)
        grad_u = to_rows(
            (self_gain * grad_vf + flip(carried).astype(jnp.float32)).astype(jnp.bfloat16)
        )
        lefts[layer] = jnp.einsum(
            "bjs,kjs->jbk", mixed_v, error_cols, preferred_element_type=jnp.float32
        )
        mixes[layer] = jnp.stack(
            [
                jnp.sum(grad_vf * mixed_u.astype(jnp.float32), axis=2),
                jnp.sum(grad_vf * flip(mixed_u).astype(jnp.float32), axis=2),
            ]
        )
        rights[layer] = jnp.einsum(
            "bis,bjs->bij", height_in, grad_u, preferred_element_type=jnp.float32
        )
        back_term = jnp.einsum(
            "bij,bjs->bis", right_factor[layer], grad_u, preferred_element_type=jnp.float32
        )
        grad = (grad.astype(jnp.float32) + back_term).astype(jnp.bfloat16)
    all_mix = lax.psum(jnp.stack(mixes), "samp")
    all_mix = lax.all_to_all(all_mix, ROW_AXES, split_axis=2, concat_axis=3, tiled=True)
    all_right = jnp.stack(
        [lax.psum(part.astype(jnp.bfloat16), "samp").astype(jnp.float32) for part in rights]
    )
    all_left = jnp.stack(
        [lax.psum(part.astype(jnp.bfloat16), "samp").astype(jnp.float32) for part in lefts]
    )
    return (output, grad.reshape(blocks * BLOCK, samples), all_right, all_left, all_mix)


def solution(mesh):
    in_specs = (
        P(("chan", "bfly"), "samp"),
        P(("chan", "bfly"), "samp"),
        P(None, ("chan", "bfly"), None, None),
        P(None, ("chan", "bfly"), None, None),
        P(None, None, ("chan", "bfly"), None),
    )
    out_specs = (
        P(("chan", "bfly"), "samp"),
        P(("chan", "bfly"), "samp"),
        P(None, ("chan", "bfly"), None, None),
        P(None, ("chan", "bfly"), None, None),
        P(None, None, ("chan", "bfly"), None),
    )
    return jax.shard_map(local, mesh=mesh, in_specs=in_specs, out_specs=out_specs, check_vma=False)
```

```python
import functools

import jax
import jax.numpy as jnp
from jax import lax
from jax.experimental import pallas as pl
from jax.experimental.pallas import tpu as pltpu
from jax.sharding import PartitionSpec as P

BLOCK = 256
LAYERS = 2
ROW_AXES = ("chan", "bfly")
F32 = jnp.float32
BF16 = jnp.bfloat16


def to_columns(values):
    return lax.all_to_all(values, ROW_AXES, split_axis=1, concat_axis=0, tiled=True)


def to_rows(values):
    return lax.all_to_all(values, ROW_AXES, split_axis=0, concat_axis=1, tiled=True)


def stationary(features, cotangent, right_factor, left_factor, mixing):
    blocks = right_factor.shape[1]
    samples = features.shape[1]
    pairs = lax.axis_size("bfly")

    def flip(values):
        grouped = values.reshape((-1, pairs // 2, 2, blocks) + values.shape[1:])
        return grouped[:, :, ::-1].reshape(values.shape)

    left_bf = left_factor.astype(jnp.bfloat16)
    gains = lax.all_to_all(mixing, ROW_AXES, split_axis=3, concat_axis=2, tiled=True)
    height = features.reshape(blocks, BLOCK, samples)
    saved = []
    for layer in range(LAYERS):
        self_gain = gains[layer, 0][:, :, None]
        cross_gain = gains[layer, 1][:, :, None]
        mixed_u = to_columns(
            jnp.einsum(
                "bis,bij->bjs", height, right_factor[layer], preferred_element_type=jnp.float32
            ).astype(jnp.bfloat16)
        )
        mixed_v = (
            self_gain * mixed_u.astype(jnp.float32) + cross_gain * flip(mixed_u).astype(jnp.float32)
        ).astype(jnp.bfloat16)
        outer = jnp.einsum(
            "bjs,jbk->kjs", mixed_v, left_bf[layer], preferred_element_type=jnp.float32
        ).astype(jnp.bfloat16)
        activation = to_rows(outer)
        saved.append((height, mixed_u, mixed_v, activation))
        height = (height.astype(jnp.float32) + jax.nn.silu(activation.astype(jnp.float32))).astype(
            jnp.bfloat16
        )
    output = height.reshape(blocks * BLOCK, samples)
    grad = cotangent.reshape(blocks, BLOCK, samples)
    rights = [None] * LAYERS
    lefts = [None] * LAYERS
    mixes = [None] * LAYERS
    for layer in reversed(range(LAYERS)):
        height_in, mixed_u, mixed_v, activation = saved[layer]
        self_gain = gains[layer, 0][:, :, None]
        cross_gain = gains[layer, 1][:, :, None]
        before = activation.astype(jnp.float32)
        logistic = jax.nn.sigmoid(before)
        error = (grad.astype(jnp.float32) * logistic * (1.0 + before * (1.0 - logistic))).astype(
            jnp.bfloat16
        )
        error_cols = to_columns(error)
        grad_v = jnp.einsum(
            "jbk,kjs->bjs", left_bf[layer], error_cols, preferred_element_type=jnp.float32
        ).astype(jnp.bfloat16)
        grad_vf = grad_v.astype(jnp.float32)
        carried = (cross_gain * grad_vf).astype(jnp.bfloat16)
        grad_u = to_rows(
            (self_gain * grad_vf + flip(carried).astype(jnp.float32)).astype(jnp.bfloat16)
        )
        lefts[layer] = jnp.einsum(
            "bjs,kjs->jbk", mixed_v, error_cols, preferred_element_type=jnp.float32
        )
        mixes[layer] = jnp.stack(
            [
                jnp.sum(grad_vf * mixed_u.astype(jnp.float32), axis=2),
                jnp.sum(grad_vf * flip(mixed_u).astype(jnp.float32), axis=2),
            ]
        )
        rights[layer] = jnp.einsum(
            "bis,bjs->bij", height_in, grad_u, preferred_element_type=jnp.float32
        )
        back_term = jnp.einsum(
            "bij,bjs->bis", right_factor[layer], grad_u, preferred_element_type=jnp.float32
        )
        grad = (grad.astype(jnp.float32) + back_term).astype(jnp.bfloat16)
    all_mix = lax.psum(jnp.stack(mixes), "samp")
    all_mix = lax.all_to_all(all_mix, ROW_AXES, split_axis=2, concat_axis=3, tiled=True)
    all_right = jnp.stack(
        [lax.psum(part.astype(jnp.bfloat16), "samp").astype(jnp.float32) for part in rights]
    )
    all_left = jnp.stack(
        [lax.psum(part.astype(jnp.bfloat16), "samp").astype(jnp.float32) for part in lefts]
    )
    return (output, grad.reshape(blocks * BLOCK, samples), all_right, all_left, all_mix)


def shuffle_rows(where, source, target, half):
    own_x, own_core = where[0], where[1] ^ pl.program_id(0)
    for group in range(BLOCK // (4 * half)):
        for dx in range(2):
            for dc in range(2):
                start = 4 * half * group + 2 * half * (own_x ^ dx) + half * (own_core ^ dc)
                rows = pl.ds(pl.multiple_of(start, half), half)
                here = pl.ds(4 * half * group + 2 * half * dx + half * dc, half)
                yield rows, here


def split_kernel(where, array_ref, pieces_ref):
    half = array_ref.shape[0]
    for rows, here in shuffle_rows(where, array_ref, pieces_ref, half):
        pieces_ref[0, 0, :, here, :] = array_ref[:, rows, :]


def merge_kernel(where, pieces_ref, array_ref):
    half = array_ref.shape[0]
    for rows, here in shuffle_rows(where, array_ref, pieces_ref, half):
        array_ref[:, rows, :] = pieces_ref[0, 0, :, here, :]


def split(where, array, chans):
    blocks, units, samples = array.shape
    half, part = blocks // 2, samples // chans
    return pl.pallas_call(
        split_kernel,
        out_shape=jax.ShapeDtypeStruct((2, chans, half, units, part), array.dtype),
        grid_spec=pltpu.PrefetchScalarGridSpec(
            num_scalar_prefetch=1,
            grid=(2, chans),
            in_specs=[pl.BlockSpec((half, units, part), lambda e, d, w: (w[1] ^ e, 0, w[2] ^ d))],
            out_specs=pl.BlockSpec((1, 1, half, units, part), lambda e, d, w: (e, d, 0, 0, 0)),
        ),
        cost_estimate=pl.CostEstimate(flops=0, bytes_accessed=4 * array.size, transcendentals=0),
    )(where, array)


def merge(where, pieces):
    _, chans, half, units, part = pieces.shape
    return pl.pallas_call(
        merge_kernel,
        out_shape=jax.ShapeDtypeStruct((2 * half, units, chans * part), pieces.dtype),
        grid_spec=pltpu.PrefetchScalarGridSpec(
            num_scalar_prefetch=1,
            grid=(2, chans),
            in_specs=[pl.BlockSpec((1, 1, half, units, part), lambda e, d, w: (e, d, 0, 0, 0))],
            out_specs=pl.BlockSpec((half, units, part), lambda e, d, w: (w[1] ^ e, 0, w[2] ^ d)),
        ),
        cost_estimate=pl.CostEstimate(flops=0, bytes_accessed=4 * pieces.size, transcendentals=0),
    )(where, pieces)


HOPS = ((0, 0), (0, 1), (1, 0), (1, 1))
VMEM_LIMIT = 48 * 1024 * 1024


def cost(flops, *arrays):
    size = sum(a.size * a.dtype.itemsize for a in arrays)
    return pl.CostEstimate(flops=int(flops), bytes_accessed=int(size), transcendentals=0)


def join(pieces, index, half, swap=0):
    groups = pieces[0].shape[1] // half
    return jnp.concatenate(
        [
            pieces[2 * (dx ^ swap) + dc][index, half * g : half * g + half, :]
            for g in range(groups)
            for dx, dc in HOPS
        ],
        axis=0,
    )


def deal(pieces, index, half, value):
    groups = pieces[0].shape[1] // half
    for g in range(groups):
        for hop in range(4):
            start = half * (4 * g + hop)
            pieces[hop][index, half * g : half * g + half, :] = value[start : start + half, :]


def swap_dx(value, half):
    step = 2 * half
    return jnp.concatenate(
        [value[step * (i ^ 1) : step * (i ^ 1) + step, :] for i in range(value.shape[0] // step)],
        axis=0,
    )


def units_forward_kernel(half, *refs):
    u, (gain_ref, left_ref), v_ref, t = refs[:4], refs[4:6], refs[6], refs[7:]
    for i in range(left_ref.shape[0]):
        mine = join(u, i, half).astype(F32)
        partner = join(u, i, half, 1).astype(F32)
        v = (gain_ref[0, 0, :, i : i + 1] * mine + gain_ref[1, 0, :, i : i + 1] * partner).astype(BF16)
        v_ref[i] = v
        out = lax.dot_general(left_ref[i], v, (((0,), (0,)), ((), ())), preferred_element_type=F32)
        deal(t, i, half, out.astype(BF16))


def units_backward_kernel(half, *refs):
    e, u, (gain_ref, left_ref) = refs[:4], refs[4:8], refs[8:10]
    du, mix_ref = refs[10:14], refs[14]
    for i in range(left_ref.shape[0]):
        dv = jnp.dot(left_ref[i], join(e, i, half), preferred_element_type=F32)
        dv = dv.astype(BF16).astype(F32)
        mine = join(u, i, half).astype(F32)
        mix_ref[0, 0, :, i : i + 1] = jnp.sum(dv * mine, axis=1, keepdims=True)
        mix_ref[1, 0, :, i : i + 1] = jnp.sum(dv * swap_dx(mine, half), axis=1, keepdims=True)
        carried = (gain_ref[1, 0, :, i : i + 1] * dv).astype(BF16).astype(F32)
        value = gain_ref[0, 0, :, i : i + 1] * dv + swap_dx(carried, half)
        deal(du, i, half, value.astype(BF16))


TILE = 8


def units_forward(u, gain, left, half):
    own, part = u[0].shape[0], u[0].shape[2]
    piece = pl.BlockSpec((TILE, own, part), lambda i: (i, 0, 0))
    full = pl.BlockSpec((TILE, BLOCK, part), lambda i: (i, 0, 0))
    gains = pl.BlockSpec((2, 1, BLOCK, TILE), lambda i: (0, i, 0, 0))
    weight = pl.BlockSpec((TILE, BLOCK, BLOCK), lambda i: (i, 0, 0))
    shape = jax.ShapeDtypeStruct((own, own, part), BF16)
    v_shape = jax.ShapeDtypeStruct((own, BLOCK, part), BF16)
    out = pl.pallas_call(
        functools.partial(units_forward_kernel, half),
        grid=(own // TILE,),
        in_specs=[piece] * 4 + [gains, weight],
        out_specs=[full] + [piece] * 4,
        out_shape=[v_shape] + [shape] * 4,
        compiler_params=pltpu.CompilerParams(vmem_limit_bytes=VMEM_LIMIT),
        cost_estimate=cost(2 * own * BLOCK * BLOCK * part, left, v_shape, *u, *u),
        name="units_forward",
    )(*u, gain, left)
    return out[0], out[1:]


def units_backward(e, u, gain, left, half):
    own, part = u[0].shape[0], u[0].shape[2]
    piece = pl.BlockSpec((TILE, own, part), lambda i: (i, 0, 0))
    gains = pl.BlockSpec((2, 1, BLOCK, TILE), lambda i: (0, i, 0, 0))
    weight = pl.BlockSpec((TILE, BLOCK, BLOCK), lambda i: (i, 0, 0))
    shape = jax.ShapeDtypeStruct((own, own, part), BF16)
    out = pl.pallas_call(
        functools.partial(units_backward_kernel, half),
        grid=(own // TILE,),
        in_specs=[piece] * 8 + [gains, weight],
        out_specs=[piece] * 4 + [gains],
        out_shape=[shape] * 4 + [jax.ShapeDtypeStruct(gain.shape, F32)],
        compiler_params=pltpu.CompilerParams(vmem_limit_bytes=VMEM_LIMIT),
        cost_estimate=cost(2 * own * BLOCK * BLOCK * part, left, *u, *u, *u),
        name="units_backward",
    )(*e, *u, gain, left)
    return out[:4], out[4]


def gather_rows(pieces, scratch, half):
    for hop in range(4):
        turned = jnp.swapaxes(pieces[hop][...], 0, 1)
        for g in range(pieces[hop].shape[0] // half):
            start = half * (4 * g + hop)
            scratch[:, start : start + half, :] = turned[:, half * g : half * g + half, :]


def scatter_rows(scratch, pieces, half):
    for hop in range(4):
        for g in range(pieces[hop].shape[0] // half):
            start = half * (4 * g + hop)
            pieces[hop][half * g : half * g + half] = jnp.swapaxes(
                scratch[:, start : start + half, :], 0, 1
            )


def error_of(grad, before):
    logistic = jax.nn.sigmoid(before)
    return (grad * logistic * (1.0 + before * (1.0 - logistic))).astype(BF16)


def first_kernel(half, h_ref, right_ref, *refs):
    u, scratch = refs[:4], refs[4]
    for b in range(h_ref.shape[0]):
        out = lax.dot_general(
            right_ref[b], h_ref[b], (((0,), (0,)), ((), ())), preferred_element_type=F32
        )
        scratch[b] = out.astype(BF16)
    scatter_rows(scratch, u, half)


def middle_kernel(half, *refs):
    t, (h_ref, right_ref), (act_ref, next_ref), u = refs[:4], refs[4:6], refs[6:8], refs[8:12]
    scratch = refs[12]
    gather_rows(t, act_ref, half)
    for b in range(h_ref.shape[0]):
        height = (h_ref[b].astype(F32) + jax.nn.silu(act_ref[b].astype(F32))).astype(BF16)
        next_ref[b] = height
        out = lax.dot_general(
            right_ref[b], height, (((0,), (0,)), ((), ())), preferred_element_type=F32
        )
        scratch[b] = out.astype(BF16)
    scatter_rows(scratch, u, half)


def last_kernel(half, *refs):
    t, (h_ref, g_ref), next_ref, e = refs[:4], refs[4:6], refs[6], refs[7:11]
    act, scratch = refs[11:13]
    gather_rows(t, act, half)
    for b in range(h_ref.shape[0]):
        before = act[b].astype(F32)
        next_ref[b] = (h_ref[b].astype(F32) + jax.nn.silu(before)).astype(BF16)
        scratch[b] = error_of(g_ref[b].astype(F32), before)
    scatter_rows(scratch, e, half)


def back_kernel(half, *refs):
    du, (g_ref, right_ref, act_ref), (rows_ref, next_ref), e = refs[:4], refs[4:7], refs[7:9], refs[9:13]
    scratch = refs[13]
    gather_rows(du, rows_ref, half)
    for b in range(g_ref.shape[0]):
        term = jnp.dot(right_ref[b], rows_ref[b], preferred_element_type=F32)
        grad = (g_ref[b].astype(F32) + term).astype(BF16)
        next_ref[b] = grad
        scratch[b] = error_of(grad.astype(F32), act_ref[b].astype(F32))
    scatter_rows(scratch, e, half)


def final_kernel(half, *refs):
    du, (g_ref, right_ref), (rows_ref, next_ref) = refs[:4], refs[4:6], refs[6:8]
    gather_rows(du, rows_ref, half)
    for b in range(g_ref.shape[0]):
        term = jnp.dot(right_ref[b], rows_ref[b], preferred_element_type=F32)
        next_ref[b] = (g_ref[b].astype(F32) + term).astype(BF16)


def rows_call(kernel, half, ins, outs, scratches):
    own, part = 4 * half, 128
    rows = 16
    specs = {
        "p": pl.BlockSpec((own, rows, part), lambda i: (0, i, 0)),
        "r": pl.BlockSpec((rows, BLOCK, part), lambda i: (i, 0, 0)),
        "w": pl.BlockSpec((rows, BLOCK, BLOCK), lambda i: (i, 0, 0)),
    }
    shapes = {"p": (own, own, part), "r": (own, BLOCK, part)}
    out_shape = [jax.ShapeDtypeStruct(shapes[kind], BF16) for kind in outs]
    kinds = [kind for kind, _ in ins]
    arrays = [array for _, array in ins]
    flops = 2 * own * BLOCK * BLOCK * part if "w" in kinds else 0
    return pl.pallas_call(
        functools.partial(kernel, half),
        grid=(own // rows,),
        in_specs=[specs[kind] for kind in kinds],
        out_specs=[specs[kind] for kind in outs],
        out_shape=out_shape,
        scratch_shapes=[pltpu.VMEM((rows, BLOCK, part), BF16)] * scratches,
        compiler_params=pltpu.CompilerParams(vmem_limit_bytes=VMEM_LIMIT),
        cost_estimate=cost(flops, *arrays, *out_shape),
        name=kernel.__name__,
    )(*arrays)


def left_sum_kernel(half, where, *refs):
    v, e, out_ref = refs[:2], (refs[2:6], refs[6:10]), refs[10]
    for i in range(out_ref.shape[1]):
        total = 0.0
        for q in range(2):
            total += lax.dot_general(
                v[q][i], join(e[q], i, half), (((1,), (1,)), ((), ())), preferred_element_type=F32
            )
        out_ref[0, i] = total.astype(BF16)


def right_sum_kernel(half, where, *refs):
    h, du, out_ref = refs[:2], refs[2:4], refs[4]
    for i in range(out_ref.shape[1]):
        total = 0.0
        for q in range(2):
            total += lax.dot_general(
                h[q][i], du[q][i], (((1,), (1,)), ((), ())), preferred_element_type=F32
            )
        out_ref[0, i] = total.astype(BF16)


def sum_call(kernel, where, other, half, arrays):
    quarter = half // 2
    chans = arrays[0].shape[0] // half
    out_shape = jax.ShapeDtypeStruct((chans, quarter, BLOCK, BLOCK), BF16)

    def tile(g, w):
        return (2 * g + (w[3] ^ other), 0, 0)

    return pl.pallas_call(
        functools.partial(kernel, half),
        out_shape=out_shape,
        grid_spec=pltpu.PrefetchScalarGridSpec(
            num_scalar_prefetch=1,
            grid=(chans,),
            in_specs=[pl.BlockSpec((quarter,) + a.shape[1:], tile) for a in arrays],
            out_specs=pl.BlockSpec((1, quarter, BLOCK, BLOCK), lambda g, w: (g, 0, 0, 0)),
        ),
        compiler_params=pltpu.CompilerParams(vmem_limit_bytes=VMEM_LIMIT),
        cost_estimate=cost(4 * chans * quarter * BLOCK * BLOCK * 128, *arrays),
        name=kernel.__name__,
    )(where, *arrays)


def after(value, *others):
    return lax.optimization_barrier((value,) + others)[0]


def planes(features, cotangent, right_factor, left_factor, mixing):
    blocks = right_factor.shape[1]
    samples = features.shape[1]
    chans, samps = lax.axis_size("chan"), lax.axis_size("samp")
    half, quarter, part = blocks // 2, blocks // 4, samples // chans
    own = chans * half
    chan, own_x, samp = lax.axis_index("chan"), lax.axis_index("bfly"), lax.axis_index("samp")
    row, core = samp // 2, samp % 2
    where = jnp.stack([own_x, core, chan, row]).astype(jnp.int32)

    def over_chan(values, distance):
        return lax.ppermute(values, "chan", [(i, i ^ distance) for i in range(chans)])

    def over_samp(values, distance):
        return lax.ppermute(values, "samp", [(i, i ^ distance) for i in range(samps)])

    def in_plane(values, dx, dc):
        if dx == 0 and dc == 0:
            return values
        route = [(i, i ^ (dx * samps + dc)) for i in range(2 * samps)]
        return lax.ppermute(values, ("bfly", "samp"), route)

    def enter(array):
        pieces = split(where, array.reshape(blocks, BLOCK, samples), chans)
        mine, other = pieces[0], over_samp(pieces[1], 1)
        chunks = []
        for core_of in range(2):
            chunk = jnp.zeros((chans, half, BLOCK, part), BF16)
            for distance in range(chans):
                piece = jnp.where(core == core_of, mine[distance], other[distance])
                if distance:
                    piece = over_chan(piece, distance)
                chunk = lax.dynamic_update_index_in_dim(chunk, piece, chan ^ distance, 0)
            chunks.append(chunk.reshape(own, BLOCK, part))
        return chunks

    def leave_planes(chunks):
        arrived = []
        for chunk in chunks:
            chunk = chunk.reshape(chans, half, BLOCK, part)
            arrived.append([])
            for distance in range(chans):
                piece = lax.dynamic_index_in_dim(chunk, chan ^ distance, 0, keepdims=False)
                arrived[-1].append(over_chan(piece, distance) if distance else piece)
        return arrived

    def leave_chip(arrived):
        first, second = (jnp.stack(pieces) for pieces in arrived)
        keep = jnp.where(core == 0, first, second)
        got = over_samp(jnp.where(core == 0, second, first), 1)
        return merge(where, jnp.stack([keep, got])).reshape(blocks * BLOCK, samples)

    number = jnp.arange(BLOCK, dtype=jnp.int32)
    swap = (number[:, None] == (number ^ (2 * half * own_x + half * core))[None, :]).astype(BF16)

    def relabel(factor):
        turned = jnp.einsum("ai,bij->baj", swap, factor, preferred_element_type=F32).astype(BF16)
        return jnp.einsum("bij,jc->bic", turned, swap, preferred_element_type=F32).astype(BF16)

    def gather_factor(factor):
        mine = lax.dynamic_slice_in_dim(factor, half * core + quarter * row, quarter, 0)
        mine = relabel(mine.astype(BF16))
        mine = lax.all_gather(mine, "chan")
        other = over_samp(mine, 2)
        pair = [jnp.where(row == 0, mine, other), jnp.where(row == 0, other, mine)]
        return jnp.stack(pair, axis=1).reshape(own, BLOCK, BLOCK)

    def sum_factor(kernel, arrays):
        send = sum_call(kernel, where, 1, half, arrays)
        keep = sum_call(kernel, where, 0, half, arrays)
        return keep, over_samp(send, 2)

    def spread_factor(keep, got):
        total = (keep.astype(F32) + got.astype(F32)).astype(BF16)
        total = lax.psum_scatter(total, "chan", scatter_dimension=0, tiled=False)
        total = relabel(total)
        whole = lax.all_gather(total, "samp").reshape(2, 2, quarter, BLOCK, BLOCK)
        return jnp.swapaxes(whole, 0, 1).reshape(blocks, BLOCK, BLOCK).astype(F32)

    def swap_pieces(pieces):
        return [in_plane(piece, dx, dc) for piece, (dx, dc) in zip(pieces, HOPS)]

    both = range(2)
    rights_in, lefts_in = [None] * LAYERS, [None] * LAYERS
    rights_in[0] = gather_factor(right_factor[0])
    heights = [enter(features)]
    lefts_in[0] = gather_factor(after(left_factor[0], heights[0][0]))
    rights_in[1] = gather_factor(after(right_factor[1], heights[0][1], lefts_in[0]))
    lefts_in[1] = gather_factor(after(left_factor[1], rights_in[1]))
    gains = lax.all_gather(after(mixing, heights[0][0]), ROW_AXES, axis=2, tiled=True)
    gains = gains.reshape(LAYERS, 2, chans, 2, 2, half, BLOCK)
    gains = jnp.where(own_x == 1, gains[:, :, :, ::-1], gains)
    gains = jnp.where(core == 1, gains[:, :, :, :, ::-1], gains)
    gains = gains.reshape(LAYERS, 2, BLOCK, chans, 4, half)
    gains = lax.dynamic_index_in_dim(gains, 2 * own_x + core, 4, keepdims=False)
    gains = gains.reshape(LAYERS, 2, BLOCK, own // TILE, TILE).swapaxes(2, 3)

    mixed_u, mixed_v, act = [[None] * 2 for _ in range(LAYERS)], [[None] * 2 for _ in range(LAYERS)], [None] * 2
    outer = [None] * 2
    for q in both:
        ins = [("r", heights[0][q]), ("w", rights_in[0])]
        mixed_u[0][q] = swap_pieces(rows_call(first_kernel, half, ins, "pppp", 1))
    grad = enter(after(cotangent, mixed_u[0][0][3]))
    for q in both:
        mixed_v[0][q], t = units_forward(mixed_u[0][q], gains[0], lefts_in[0], half)
        outer[q] = swap_pieces(t)
    heights.append([None] * 2)
    for q in both:
        ins = [("p", p) for p in outer[q]] + [("r", heights[0][q]), ("w", rights_in[1])]
        out = rows_call(middle_kernel, half, ins, "rrpppp", 1)
        act[q], heights[1][q] = out[:2]
        mixed_u[1][q] = swap_pieces(out[2:])
    for q in both:
        mixed_v[1][q], t = units_forward(mixed_u[1][q], gains[1], lefts_in[1], half)
        outer[q] = swap_pieces(t)
    error, final = [None] * 2, [None] * 2
    for q in both:
        ins = [("p", p) for p in outer[q]] + [("r", heights[1][q]), ("r", grad[q])]
        out = rows_call(last_kernel, half, ins, "rpppp", 2)
        final[q] = out[0]
        error[q] = swap_pieces(out[1:])
    out_parts = leave_planes(final)
    mix = [None] * LAYERS
    grad_u = [None] * 2
    for q in both:
        du, mix_q = units_backward(error[q], mixed_u[1][q], gains[1], lefts_in[1], half)
        mix[1] = mix_q if q == 0 else mix[1] + mix_q
        grad_u[q] = swap_pieces(du)
    left_1 = sum_factor(left_sum_kernel, mixed_v[1] + error[0] + error[1])
    rows = [None] * 2
    old_error, error = error, [None] * 2
    for q in both:
        ins = [("p", p) for p in grad_u[q]] + [("r", grad[q]), ("w", rights_in[1]), ("r", act[q])]
        out = rows_call(back_kernel, half, ins, "rrpppp", 1)
        rows[q], grad[q] = out[:2]
        error[q] = swap_pieces(out[2:])
    right_1 = sum_factor(right_sum_kernel, heights[1] + rows)
    for q in both:
        du, mix_q = units_backward(error[q], mixed_u[0][q], gains[0], lefts_in[0], half)
        mix[0] = mix_q if q == 0 else mix[0] + mix_q
        grad_u[q] = swap_pieces(du)
    grad_left_1 = spread_factor(*left_1)
    left_0 = sum_factor(left_sum_kernel, mixed_v[0] + error[0] + error[1])
    rows = [None] * 2
    for q in both:
        ins = [("p", p) for p in grad_u[q]] + [("r", grad[q]), ("w", rights_in[0])]
        rows[q], grad[q] = rows_call(final_kernel, half, ins, "rr", 0)
    right_0 = sum_factor(right_sum_kernel, heights[0] + rows)
    in_parts = leave_planes(grad)
    grad_right_1 = spread_factor(*right_1)
    grad_left_0 = spread_factor(*left_0)
    grad_right_0 = spread_factor(*right_0)
    output = leave_chip(out_parts)
    feature_grad = leave_chip(in_parts)
    mix = jnp.stack(mix).swapaxes(2, 3).reshape(LAYERS, 2, chans, 2, 2, half, own)
    mix = jnp.where(own_x == 1, mix[:, :, :, ::-1], mix)
    mix = jnp.where(core == 1, mix[:, :, :, :, ::-1], mix)
    mix = mix.reshape(LAYERS, 2, BLOCK, chans, 1, half)
    mix = jnp.where(jnp.arange(4)[:, None] == 2 * own_x + core, mix, 0.0)
    mix = lax.psum(mix.reshape(LAYERS, 2, BLOCK, BLOCK), ("chan", "bfly", "samp"))
    mix = lax.dynamic_slice_in_dim(mix, blocks * (2 * chan + own_x), blocks, 2)
    rights = jnp.stack([grad_right_0, grad_right_1])
    return (output, feature_grad, rights, jnp.stack([grad_left_0, grad_left_1]), mix)


def solution(mesh):
    sizes = dict(mesh.shape)
    fits = sizes["chan"] == 4 and sizes["bfly"] == 2 and sizes["samp"] == 4
    local = planes if fits else stationary
    rows = P(ROW_AXES, "samp")
    factors = P(None, ROW_AXES, None, None)
    gains = P(None, None, ROW_AXES, None)
    return jax.shard_map(
        local,
        mesh=mesh,
        in_specs=(rows, rows, factors, factors, gains),
        out_specs=(rows, rows, factors, factors, gains),
        check_vma=False,
    )
```

```python
import functools

import jax
import jax.numpy as jnp
from jax import lax
from jax.experimental import pallas as pl
from jax.experimental.pallas import tpu as pltpu
from jax.sharding import PartitionSpec as P

BLOCK = 256
LAYERS = 2
ROW_AXES = ("chan", "bfly")
F32 = jnp.float32
BF16 = jnp.bfloat16


def to_columns(values):
    return lax.all_to_all(values, ROW_AXES, split_axis=1, concat_axis=0, tiled=True)


def to_rows(values):
    return lax.all_to_all(values, ROW_AXES, split_axis=0, concat_axis=1, tiled=True)


def stationary(features, cotangent, right_factor, left_factor, mixing):
    blocks = right_factor.shape[1]
    samples = features.shape[1]
    pairs = lax.axis_size("bfly")

    def flip(values):
        grouped = values.reshape((-1, pairs // 2, 2, blocks) + values.shape[1:])
        return grouped[:, :, ::-1].reshape(values.shape)

    left_bf = left_factor.astype(jnp.bfloat16)
    gains = lax.all_to_all(mixing, ROW_AXES, split_axis=3, concat_axis=2, tiled=True)
    height = features.reshape(blocks, BLOCK, samples)
    saved = []
    for layer in range(LAYERS):
        self_gain = gains[layer, 0][:, :, None]
        cross_gain = gains[layer, 1][:, :, None]
        mixed_u = to_columns(
            jnp.einsum(
                "bis,bij->bjs", height, right_factor[layer], preferred_element_type=jnp.float32
            ).astype(jnp.bfloat16)
        )
        mixed_v = (
            self_gain * mixed_u.astype(jnp.float32) + cross_gain * flip(mixed_u).astype(jnp.float32)
        ).astype(jnp.bfloat16)
        outer = jnp.einsum(
            "bjs,jbk->kjs", mixed_v, left_bf[layer], preferred_element_type=jnp.float32
        ).astype(jnp.bfloat16)
        activation = to_rows(outer)
        saved.append((height, mixed_u, mixed_v, activation))
        height = (height.astype(jnp.float32) + jax.nn.silu(activation.astype(jnp.float32))).astype(
            jnp.bfloat16
        )
    output = height.reshape(blocks * BLOCK, samples)
    grad = cotangent.reshape(blocks, BLOCK, samples)
    rights = [None] * LAYERS
    lefts = [None] * LAYERS
    mixes = [None] * LAYERS
    for layer in reversed(range(LAYERS)):
        height_in, mixed_u, mixed_v, activation = saved[layer]
        self_gain = gains[layer, 0][:, :, None]
        cross_gain = gains[layer, 1][:, :, None]
        before = activation.astype(jnp.float32)
        logistic = jax.nn.sigmoid(before)
        error = (grad.astype(jnp.float32) * logistic * (1.0 + before * (1.0 - logistic))).astype(
            jnp.bfloat16
        )
        error_cols = to_columns(error)
        grad_v = jnp.einsum(
            "jbk,kjs->bjs", left_bf[layer], error_cols, preferred_element_type=jnp.float32
        ).astype(jnp.bfloat16)
        grad_vf = grad_v.astype(jnp.float32)
        carried = (cross_gain * grad_vf).astype(jnp.bfloat16)
        grad_u = to_rows(
            (self_gain * grad_vf + flip(carried).astype(jnp.float32)).astype(jnp.bfloat16)
        )
        lefts[layer] = jnp.einsum(
            "bjs,kjs->jbk", mixed_v, error_cols, preferred_element_type=jnp.float32
        )
        mixes[layer] = jnp.stack(
            [
                jnp.sum(grad_vf * mixed_u.astype(jnp.float32), axis=2),
                jnp.sum(grad_vf * flip(mixed_u).astype(jnp.float32), axis=2),
            ]
        )
        rights[layer] = jnp.einsum(
            "bis,bjs->bij", height_in, grad_u, preferred_element_type=jnp.float32
        )
        back_term = jnp.einsum(
            "bij,bjs->bis", right_factor[layer], grad_u, preferred_element_type=jnp.float32
        )
        grad = (grad.astype(jnp.float32) + back_term).astype(jnp.bfloat16)
    all_mix = lax.psum(jnp.stack(mixes), "samp")
    all_mix = lax.all_to_all(all_mix, ROW_AXES, split_axis=2, concat_axis=3, tiled=True)
    all_right = jnp.stack(
        [lax.psum(part.astype(jnp.bfloat16), "samp").astype(jnp.float32) for part in rights]
    )
    all_left = jnp.stack(
        [lax.psum(part.astype(jnp.bfloat16), "samp").astype(jnp.float32) for part in lefts]
    )
    return (output, grad.reshape(blocks * BLOCK, samples), all_right, all_left, all_mix)


def shuffle_rows(where, source, target, half):
    own_x, own_core = where[0], where[1] ^ pl.program_id(0)
    for group in range(BLOCK // (4 * half)):
        for dx in range(2):
            for dc in range(2):
                start = 4 * half * group + 2 * half * (own_x ^ dx) + half * (own_core ^ dc)
                rows = pl.ds(pl.multiple_of(start, half), half)
                here = pl.ds(4 * half * group + 2 * half * dx + half * dc, half)
                yield rows, here


def split_kernel(where, array_ref, pieces_ref):
    half = array_ref.shape[0]
    for rows, here in shuffle_rows(where, array_ref, pieces_ref, half):
        pieces_ref[0, 0, :, here, :] = array_ref[:, rows, :]


def merge_kernel(where, pieces_ref, array_ref):
    half = array_ref.shape[0]
    for rows, here in shuffle_rows(where, array_ref, pieces_ref, half):
        array_ref[:, rows, :] = pieces_ref[0, 0, :, here, :]


def split(where, array, chans):
    blocks, units, samples = array.shape
    half, part = blocks // 2, samples // chans
    return pl.pallas_call(
        split_kernel,
        out_shape=jax.ShapeDtypeStruct((2, chans, half, units, part), array.dtype),
        grid_spec=pltpu.PrefetchScalarGridSpec(
            num_scalar_prefetch=1,
            grid=(2, chans),
            in_specs=[pl.BlockSpec((half, units, part), lambda e, d, w: (w[1] ^ e, 0, w[2] ^ d))],
            out_specs=pl.BlockSpec((1, 1, half, units, part), lambda e, d, w: (e, d, 0, 0, 0)),
        ),
        cost_estimate=pl.CostEstimate(flops=0, bytes_accessed=4 * array.size, transcendentals=0),
    )(where, array)


def merge(where, pieces):
    _, chans, half, units, part = pieces.shape
    return pl.pallas_call(
        merge_kernel,
        out_shape=jax.ShapeDtypeStruct((2 * half, units, chans * part), pieces.dtype),
        grid_spec=pltpu.PrefetchScalarGridSpec(
            num_scalar_prefetch=1,
            grid=(2, chans),
            in_specs=[pl.BlockSpec((1, 1, half, units, part), lambda e, d, w: (e, d, 0, 0, 0))],
            out_specs=pl.BlockSpec((half, units, part), lambda e, d, w: (w[1] ^ e, 0, w[2] ^ d)),
        ),
        cost_estimate=pl.CostEstimate(flops=0, bytes_accessed=4 * pieces.size, transcendentals=0),
    )(where, pieces)


HOPS = ((0, 0), (0, 1), (1, 0), (1, 1))
VMEM_LIMIT = 48 * 1024 * 1024


def cost(flops, *arrays):
    size = sum(a.size * a.dtype.itemsize for a in arrays)
    return pl.CostEstimate(flops=int(flops), bytes_accessed=int(size), transcendentals=0)


def join(pieces, index, half, swap=0):
    groups = pieces[0].shape[1] // half
    return jnp.concatenate(
        [
            pieces[2 * (dx ^ swap) + dc][index, half * g : half * g + half, :]
            for g in range(groups)
            for dx, dc in HOPS
        ],
        axis=0,
    )


def deal(pieces, index, half, value):
    groups = pieces[0].shape[1] // half
    for g in range(groups):
        for hop in range(4):
            start = half * (4 * g + hop)
            pieces[hop][index, half * g : half * g + half, :] = value[start : start + half, :]


def swap_dx(value, half):
    step = 2 * half
    return jnp.concatenate(
        [value[step * (i ^ 1) : step * (i ^ 1) + step, :] for i in range(value.shape[0] // step)],
        axis=0,
    )


def units_forward_kernel(half, *refs):
    u, (gain_ref, left_ref), v_ref, t = refs[:4], refs[4:6], refs[6], refs[7:]
    for i in range(left_ref.shape[0]):
        mine = join(u, i, half).astype(F32)
        partner = join(u, i, half, 1).astype(F32)
        v = (gain_ref[0, 0, :, i : i + 1] * mine + gain_ref[1, 0, :, i : i + 1] * partner).astype(BF16)
        v_ref[i] = v
        out = lax.dot_general(left_ref[i], v, (((0,), (0,)), ((), ())), preferred_element_type=F32)
        deal(t, i, half, out.astype(BF16))


def units_backward_kernel(half, *refs):
    e, u, (gain_ref, left_ref) = refs[:4], refs[4:8], refs[8:10]
    du, mix_ref = refs[10:14], refs[14]
    for i in range(left_ref.shape[0]):
        dv = jnp.dot(left_ref[i], join(e, i, half), preferred_element_type=F32)
        dv = dv.astype(BF16).astype(F32)
        mine = join(u, i, half).astype(F32)
        mix_ref[0, 0, :, i : i + 1] = jnp.sum(dv * mine, axis=1, keepdims=True)
        mix_ref[1, 0, :, i : i + 1] = jnp.sum(dv * swap_dx(mine, half), axis=1, keepdims=True)
        carried = (gain_ref[1, 0, :, i : i + 1] * dv).astype(BF16).astype(F32)
        value = gain_ref[0, 0, :, i : i + 1] * dv + swap_dx(carried, half)
        deal(du, i, half, value.astype(BF16))


TILE = 8


def units_forward(u, gain, left, half):
    own, part = u[0].shape[0], u[0].shape[2]
    piece = pl.BlockSpec((TILE, own, part), lambda i: (i, 0, 0))
    full = pl.BlockSpec((TILE, BLOCK, part), lambda i: (i, 0, 0))
    gains = pl.BlockSpec((2, 1, BLOCK, TILE), lambda i: (0, i, 0, 0))
    weight = pl.BlockSpec((TILE, BLOCK, BLOCK), lambda i: (i, 0, 0))
    shape = jax.ShapeDtypeStruct((own, own, part), BF16)
    v_shape = jax.ShapeDtypeStruct((own, BLOCK, part), BF16)
    out = pl.pallas_call(
        functools.partial(units_forward_kernel, half),
        grid=(own // TILE,),
        in_specs=[piece] * 4 + [gains, weight],
        out_specs=[full] + [piece] * 4,
        out_shape=[v_shape] + [shape] * 4,
        compiler_params=pltpu.CompilerParams(vmem_limit_bytes=VMEM_LIMIT),
        cost_estimate=cost(2 * own * BLOCK * BLOCK * part, left, v_shape, *u, *u),
        name="units_forward",
    )(*u, gain, left)
    return out[0], out[1:]


def units_backward(e, u, gain, left, half):
    own, part = u[0].shape[0], u[0].shape[2]
    piece = pl.BlockSpec((TILE, own, part), lambda i: (i, 0, 0))
    gains = pl.BlockSpec((2, 1, BLOCK, TILE), lambda i: (0, i, 0, 0))
    weight = pl.BlockSpec((TILE, BLOCK, BLOCK), lambda i: (i, 0, 0))
    shape = jax.ShapeDtypeStruct((own, own, part), BF16)
    out = pl.pallas_call(
        functools.partial(units_backward_kernel, half),
        grid=(own // TILE,),
        in_specs=[piece] * 8 + [gains, weight],
        out_specs=[piece] * 4 + [gains],
        out_shape=[shape] * 4 + [jax.ShapeDtypeStruct(gain.shape, F32)],
        compiler_params=pltpu.CompilerParams(vmem_limit_bytes=VMEM_LIMIT),
        cost_estimate=cost(2 * own * BLOCK * BLOCK * part, left, *u, *u, *u),
        name="units_backward",
    )(*e, *u, gain, left)
    return out[:4], out[4]


def gather_rows(pieces, scratch, half):
    for hop in range(4):
        turned = jnp.swapaxes(pieces[hop][...], 0, 1)
        for g in range(pieces[hop].shape[0] // half):
            start = half * (4 * g + hop)
            scratch[:, start : start + half, :] = turned[:, half * g : half * g + half, :]


def scatter_rows(scratch, pieces, half):
    for hop in range(4):
        for g in range(pieces[hop].shape[0] // half):
            start = half * (4 * g + hop)
            pieces[hop][half * g : half * g + half] = jnp.swapaxes(
                scratch[:, start : start + half, :], 0, 1
            )


def error_of(grad, before):
    logistic = jax.nn.sigmoid(before)
    return (grad * logistic * (1.0 + before * (1.0 - logistic))).astype(BF16)


def first_kernel(half, h_ref, right_ref, *refs):
    u, scratch = refs[:4], refs[4]
    for b in range(h_ref.shape[0]):
        out = lax.dot_general(
            right_ref[b], h_ref[b], (((0,), (0,)), ((), ())), preferred_element_type=F32
        )
        scratch[b] = out.astype(BF16)
    scatter_rows(scratch, u, half)


def middle_kernel(half, *refs):
    t, (h_ref, right_ref), (act_ref, next_ref), u = refs[:4], refs[4:6], refs[6:8], refs[8:12]
    scratch = refs[12]
    gather_rows(t, act_ref, half)
    for b in range(h_ref.shape[0]):
        height = (h_ref[b].astype(F32) + jax.nn.silu(act_ref[b].astype(F32))).astype(BF16)
        next_ref[b] = height
        out = lax.dot_general(
            right_ref[b], height, (((0,), (0,)), ((), ())), preferred_element_type=F32
        )
        scratch[b] = out.astype(BF16)
    scatter_rows(scratch, u, half)


def last_kernel(half, *refs):
    t, (h_ref, g_ref), next_ref, e = refs[:4], refs[4:6], refs[6], refs[7:11]
    act, scratch = refs[11:13]
    gather_rows(t, act, half)
    for b in range(h_ref.shape[0]):
        before = act[b].astype(F32)
        next_ref[b] = (h_ref[b].astype(F32) + jax.nn.silu(before)).astype(BF16)
        scratch[b] = error_of(g_ref[b].astype(F32), before)
    scatter_rows(scratch, e, half)


def back_kernel(half, *refs):
    du, (g_ref, right_ref, act_ref), (rows_ref, next_ref), e = refs[:4], refs[4:7], refs[7:9], refs[9:13]
    scratch = refs[13]
    gather_rows(du, rows_ref, half)
    for b in range(g_ref.shape[0]):
        term = jnp.dot(right_ref[b], rows_ref[b], preferred_element_type=F32)
        grad = (g_ref[b].astype(F32) + term).astype(BF16)
        next_ref[b] = grad
        scratch[b] = error_of(grad.astype(F32), act_ref[b].astype(F32))
    scatter_rows(scratch, e, half)


def final_kernel(half, *refs):
    du, (g_ref, right_ref), (rows_ref, next_ref) = refs[:4], refs[4:6], refs[6:8]
    gather_rows(du, rows_ref, half)
    for b in range(g_ref.shape[0]):
        term = jnp.dot(right_ref[b], rows_ref[b], preferred_element_type=F32)
        next_ref[b] = (g_ref[b].astype(F32) + term).astype(BF16)


def rows_call(kernel, half, ins, outs, scratches):
    own, part = 4 * half, 128
    rows = 16
    specs = {
        "p": pl.BlockSpec((own, rows, part), lambda i: (0, i, 0)),
        "r": pl.BlockSpec((rows, BLOCK, part), lambda i: (i, 0, 0)),
        "w": pl.BlockSpec((rows, BLOCK, BLOCK), lambda i: (i, 0, 0)),
    }
    shapes = {"p": (own, own, part), "r": (own, BLOCK, part)}
    out_shape = [jax.ShapeDtypeStruct(shapes[kind], BF16) for kind in outs]
    kinds = [kind for kind, _ in ins]
    arrays = [array for _, array in ins]
    flops = 2 * own * BLOCK * BLOCK * part if "w" in kinds else 0
    return pl.pallas_call(
        functools.partial(kernel, half),
        grid=(own // rows,),
        in_specs=[specs[kind] for kind in kinds],
        out_specs=[specs[kind] for kind in outs],
        out_shape=out_shape,
        scratch_shapes=[pltpu.VMEM((rows, BLOCK, part), BF16)] * scratches,
        compiler_params=pltpu.CompilerParams(vmem_limit_bytes=VMEM_LIMIT),
        cost_estimate=cost(flops, *arrays, *out_shape),
        name=kernel.__name__,
    )(*arrays)


def left_sum_kernel(half, where, *refs):
    v, e, out_ref = refs[:2], (refs[2:6], refs[6:10]), refs[10]
    for i in range(out_ref.shape[1]):
        total = 0.0
        for q in range(2):
            total += lax.dot_general(
                v[q][i], join(e[q], i, half), (((1,), (1,)), ((), ())), preferred_element_type=F32
            )
        out_ref[0, i] = total.astype(BF16)


def right_sum_kernel(half, where, *refs):
    h, du, out_ref = refs[:2], refs[2:4], refs[4]
    for i in range(out_ref.shape[1]):
        total = 0.0
        for q in range(2):
            total += lax.dot_general(
                h[q][i], du[q][i], (((1,), (1,)), ((), ())), preferred_element_type=F32
            )
        out_ref[0, i] = total.astype(BF16)


def sum_call(kernel, where, other, half, arrays):
    quarter = half // 2
    chans = arrays[0].shape[0] // half
    out_shape = jax.ShapeDtypeStruct((chans, quarter, BLOCK, BLOCK), BF16)

    def tile(g, w):
        return (2 * g + (w[3] ^ other), 0, 0)

    return pl.pallas_call(
        functools.partial(kernel, half),
        out_shape=out_shape,
        grid_spec=pltpu.PrefetchScalarGridSpec(
            num_scalar_prefetch=1,
            grid=(chans,),
            in_specs=[pl.BlockSpec((quarter,) + a.shape[1:], tile) for a in arrays],
            out_specs=pl.BlockSpec((1, quarter, BLOCK, BLOCK), lambda g, w: (g, 0, 0, 0)),
        ),
        compiler_params=pltpu.CompilerParams(vmem_limit_bytes=VMEM_LIMIT),
        cost_estimate=cost(4 * chans * quarter * BLOCK * BLOCK * 128, *arrays),
        name=kernel.__name__,
    )(where, *arrays)


def weave_kernel(where, mine_ref, other_ref, out_ref):
    @pl.when(pl.program_id(1) == where[3])
    def _():
        out_ref[0, 0] = mine_ref[0]

    @pl.when(pl.program_id(1) != where[3])
    def _():
        out_ref[0, 0] = other_ref[0]


def weave(where, mine, other):
    block = (1,) + mine.shape[1:]
    spec = pl.BlockSpec(block, lambda g, y, w: (g, 0, 0, 0))
    return pl.pallas_call(
        weave_kernel,
        out_shape=jax.ShapeDtypeStruct(mine.shape[:1] + (2,) + mine.shape[1:], mine.dtype),
        grid_spec=pltpu.PrefetchScalarGridSpec(
            num_scalar_prefetch=1,
            grid=(mine.shape[0], 2),
            in_specs=[spec, spec],
            out_specs=pl.BlockSpec((1,) + block, lambda g, y, w: (g, y, 0, 0, 0)),
        ),
        cost_estimate=pl.CostEstimate(flops=0, bytes_accessed=8 * mine.size, transcendentals=0),
    )(where, mine, other)


def after(value, *others):
    return lax.optimization_barrier((value,) + others)[0]


def planes(features, cotangent, right_factor, left_factor, mixing):
    blocks = right_factor.shape[1]
    samples = features.shape[1]
    chans, samps = lax.axis_size("chan"), lax.axis_size("samp")
    half, quarter, part = blocks // 2, blocks // 4, samples // chans
    own = chans * half
    chan, own_x, samp = lax.axis_index("chan"), lax.axis_index("bfly"), lax.axis_index("samp")
    row, core = samp // 2, samp % 2
    where = jnp.stack([own_x, core, chan, row]).astype(jnp.int32)

    def over_chan(values, distance):
        return lax.ppermute(values, "chan", [(i, i ^ distance) for i in range(chans)])

    def over_samp(values, distance):
        return lax.ppermute(values, "samp", [(i, i ^ distance) for i in range(samps)])

    def in_plane(values, dx, dc):
        if dx == 0 and dc == 0:
            return values
        route = [(i, i ^ (dx * samps + dc)) for i in range(2 * samps)]
        return lax.ppermute(values, ("bfly", "samp"), route)

    def enter(array):
        pieces = split(where, array.reshape(blocks, BLOCK, samples), chans)
        mine, other = pieces[0], over_samp(pieces[1], 1)
        chunks = []
        for core_of in range(2):
            chunk = jnp.zeros((chans, half, BLOCK, part), BF16)
            for distance in range(chans):
                piece = jnp.where(core == core_of, mine[distance], other[distance])
                if distance:
                    piece = over_chan(piece, distance)
                chunk = lax.dynamic_update_index_in_dim(chunk, piece, chan ^ distance, 0)
            chunks.append(chunk.reshape(own, BLOCK, part))
        return chunks

    def leave_planes(chunks):
        arrived = []
        for chunk in chunks:
            chunk = chunk.reshape(chans, half, BLOCK, part)
            arrived.append([])
            for distance in range(chans):
                piece = lax.dynamic_index_in_dim(chunk, chan ^ distance, 0, keepdims=False)
                arrived[-1].append(over_chan(piece, distance) if distance else piece)
        return arrived

    def leave_chip(arrived):
        first, second = (jnp.stack(pieces) for pieces in arrived)
        keep = jnp.where(core == 0, first, second)
        got = over_samp(jnp.where(core == 0, second, first), 1)
        return merge(where, jnp.stack([keep, got])).reshape(blocks * BLOCK, samples)

    number = jnp.arange(BLOCK, dtype=jnp.int32)
    swap = (number[:, None] == (number ^ (2 * half * own_x + half * core))[None, :]).astype(BF16)

    def relabel(factor):
        turned = jnp.einsum("ai,bij->baj", swap, factor, preferred_element_type=F32).astype(BF16)
        return jnp.einsum("bij,jc->bic", turned, swap, preferred_element_type=F32).astype(BF16)

    def gather_chan(factor):
        mine = lax.dynamic_slice_in_dim(factor, half * core + quarter * row, quarter, 0)
        return lax.all_gather(relabel(mine.astype(BF16)), "chan")

    def gather_row(mine, *gate):
        other = after(over_samp(mine, 2), *gate) if gate else over_samp(mine, 2)
        return weave(where, mine, other).reshape(own, BLOCK, BLOCK)

    def hold(pieces, *gate):
        return [after(pieces[0], *gate)] + list(pieces[1:])

    def sum_factor(kernel, arrays):
        send = sum_call(kernel, where, 1, half, arrays)
        keep = sum_call(kernel, where, 0, half, arrays)
        return keep, over_samp(send, 2)

    def spread_factor(keep, got):
        total = (keep.astype(F32) + got.astype(F32)).astype(BF16)
        return lax.psum_scatter(total, "chan", scatter_dimension=0, tiled=False)

    def finish_factor(total):
        total = relabel(total)
        whole = lax.all_gather(total, "samp").reshape(2, 2, quarter, BLOCK, BLOCK)
        return jnp.swapaxes(whole, 0, 1).reshape(blocks, BLOCK, BLOCK).astype(F32)

    def swap_pieces(pieces):
        return [in_plane(piece, dx, dc) for piece, (dx, dc) in zip(pieces, HOPS)]

    both = range(2)
    right_mine = gather_chan(right_factor[0])
    heights = [enter(features)]
    rights_in = [gather_row(right_mine), None]
    left_mine = gather_chan(after(left_factor[0], right_mine))
    gains = lax.all_gather(after(mixing, right_mine), ROW_AXES, axis=2, tiled=True)
    gains = gains.reshape(LAYERS, 2, chans, 2, 2, half, BLOCK)
    gains = jnp.where(own_x == 1, gains[:, :, :, ::-1], gains)
    gains = jnp.where(core == 1, gains[:, :, :, :, ::-1], gains)
    gains = gains.reshape(LAYERS, 2, BLOCK, chans, 4, half)
    gains = lax.dynamic_index_in_dim(gains, 2 * own_x + core, 4, keepdims=False)
    gains = gains.reshape(LAYERS, 2, BLOCK, own // TILE, TILE).swapaxes(2, 3)

    mixed_u, mixed_v, act = [[None] * 2 for _ in range(LAYERS)], [[None] * 2 for _ in range(LAYERS)], [None] * 2
    outer, sent = [None] * 2, [None] * 2
    for q in both:
        ins = [("r", heights[0][q]), ("w", rights_in[0])]
        sent[q] = rows_call(first_kernel, half, ins, "pppp", 1)
        mixed_u[0][q] = swap_pieces(sent[q])
    lefts_in = [gather_row(after(left_mine, heights[0][1]), sent[1][0]), None]
    right_mine = gather_chan(after(right_factor[1], sent[1][0], left_mine))
    mixed_u[0][0] = hold(mixed_u[0][0], sent[1][0])
    for q in both:
        mixed_v[0][q], sent[q] = units_forward(mixed_u[0][q], gains[0], lefts_in[0], half)
        outer[q] = swap_pieces(sent[q])
    rights_in[1] = gather_row(after(right_mine, sent[0][0]), sent[1][0])
    outer[0] = hold(outer[0], sent[1][0])
    left_mine = gather_chan(after(left_factor[1], right_mine, sent[1][0]))
    grad = enter(after(cotangent, sent[1][0]))
    heights.append([None] * 2)
    for q in both:
        ins = [("p", p) for p in outer[q]] + [("r", heights[0][q]), ("w", rights_in[1])]
        out = rows_call(middle_kernel, half, ins, "rrpppp", 1)
        act[q], heights[1][q] = out[:2]
        sent[q] = out[2:]
        mixed_u[1][q] = swap_pieces(out[2:])
    lefts_in[1] = gather_row(after(left_mine, sent[0][0]), sent[1][0])
    mixed_u[1][0] = hold(mixed_u[1][0], sent[1][0])
    for q in both:
        mixed_v[1][q], sent[q] = units_forward(mixed_u[1][q], gains[1], lefts_in[1], half)
        outer[q] = swap_pieces(sent[q])
    outer[0] = hold(outer[0], sent[1][0])
    error, final = [None] * 2, [None] * 2
    for q in both:
        ins = [("p", p) for p in outer[q]] + [("r", heights[1][q]), ("r", grad[q])]
        out = rows_call(last_kernel, half, ins, "rpppp", 2)
        final[q] = out[0]
        error[q] = swap_pieces(out[1:])
    error[0] = hold(error[0], final[1])
    out_parts = leave_planes(final)
    mix = [None] * LAYERS
    grad_u = [None] * 2
    for q in both:
        du, mix_q = units_backward(error[q], mixed_u[1][q], gains[1], lefts_in[1], half)
        mix[1] = mix_q if q == 0 else mix[1] + mix_q
        grad_u[q] = swap_pieces(du)
    grad_u[0] = hold(grad_u[0], mix[1])
    left_1 = sum_factor(left_sum_kernel, mixed_v[1] + error[0] + error[1])
    rows = [None] * 2
    error = [None] * 2
    for q in both:
        ins = [("p", p) for p in hold(grad_u[q], *out_parts[q])]
        ins += [("r", grad[q]), ("w", rights_in[1]), ("r", act[q])]
        out = rows_call(back_kernel, half, ins, "rrpppp", 1)
        rows[q], grad[q] = out[:2]
        sent[q] = out[2:]
        error[q] = swap_pieces(out[2:])
    output = leave_chip(out_parts)
    left_1 = spread_factor(left_1[0], after(left_1[1], sent[1][0]))
    right_1 = sum_factor(right_sum_kernel, heights[1] + rows)
    for q in both:
        error[q] = hold(error[q], rows[1] if q == 0 else output)
        du, mix_q = units_backward(error[q], mixed_u[0][q], gains[0], lefts_in[0], half)
        mix[0] = mix_q if q == 0 else mix[0] + mix_q
        sent[q] = du
        grad_u[q] = swap_pieces(du)
    right_1 = spread_factor(right_1[0], after(right_1[1], sent[1][0], left_1))
    left_0 = sum_factor(left_sum_kernel, mixed_v[0] + error[0] + error[1])
    grad_left_1 = finish_factor(after(left_1, sent[1][0]))
    rows = [None] * 2
    for q in both:
        ins = [("p", p) for p in hold(grad_u[q], sent[1][0] if q == 0 else grad_left_1)]
        ins += [("r", grad[q]), ("w", rights_in[0])]
        rows[q], grad[q] = rows_call(final_kernel, half, ins, "rr", 0)
    right_0 = sum_factor(right_sum_kernel, heights[0] + rows)
    in_parts = leave_planes(grad)
    left_0 = spread_factor(left_0[0], after(left_0[1], rows[0], right_1))
    grad_right_1 = finish_factor(after(right_1, rows[1]))
    grad_left_0 = finish_factor(left_0)
    feature_grad = leave_chip(in_parts)
    grad_right_0 = finish_factor(spread_factor(right_0[0], after(right_0[1], left_0, *in_parts[0])))
    mix = jnp.stack(mix).swapaxes(2, 3).reshape(LAYERS, 2, chans, 2, 2, half, own)
    mix = jnp.where(own_x == 1, mix[:, :, :, ::-1], mix)
    mix = jnp.where(core == 1, mix[:, :, :, :, ::-1], mix)
    mix = mix.reshape(LAYERS, 2, BLOCK, chans, 1, half)
    mix = jnp.where(jnp.arange(4)[:, None] == 2 * own_x + core, mix, 0.0)
    mix = lax.psum(mix.reshape(LAYERS, 2, BLOCK, BLOCK), ("chan", "bfly", "samp"))
    mix = lax.dynamic_slice_in_dim(mix, blocks * (2 * chan + own_x), blocks, 2)
    rights = jnp.stack([grad_right_0, grad_right_1])
    return (output, feature_grad, rights, jnp.stack([grad_left_0, grad_left_1]), mix)


def solution(mesh):
    sizes = dict(mesh.shape)
    fits = sizes["chan"] == 4 and sizes["bfly"] == 2 and sizes["samp"] == 4
    local = planes if fits else stationary
    rows = P(ROW_AXES, "samp")
    factors = P(None, ROW_AXES, None, None)
    gains = P(None, None, ROW_AXES, None)
    return jax.shard_map(
        local,
        mesh=mesh,
        in_specs=(rows, rows, factors, factors, gains),
        out_specs=(rows, rows, factors, factors, gains),
        check_vma=False,
    )
```

```python
import functools

import jax
import jax.numpy as jnp
from jax import lax
from jax.experimental import pallas as pl
from jax.experimental.pallas import tpu as pltpu
from jax.sharding import PartitionSpec as P

BLOCK = 256
LAYERS = 2
ROW_AXES = ("chan", "bfly")
F32 = jnp.float32
BF16 = jnp.bfloat16


def to_columns(values):
    return lax.all_to_all(values, ROW_AXES, split_axis=1, concat_axis=0, tiled=True)


def to_rows(values):
    return lax.all_to_all(values, ROW_AXES, split_axis=0, concat_axis=1, tiled=True)


def stationary(features, cotangent, right_factor, left_factor, mixing):
    blocks = right_factor.shape[1]
    samples = features.shape[1]
    pairs = lax.axis_size("bfly")

    def flip(values):
        grouped = values.reshape((-1, pairs // 2, 2, blocks) + values.shape[1:])
        return grouped[:, :, ::-1].reshape(values.shape)

    left_bf = left_factor.astype(jnp.bfloat16)
    gains = lax.all_to_all(mixing, ROW_AXES, split_axis=3, concat_axis=2, tiled=True)
    height = features.reshape(blocks, BLOCK, samples)
    saved = []
    for layer in range(LAYERS):
        self_gain = gains[layer, 0][:, :, None]
        cross_gain = gains[layer, 1][:, :, None]
        mixed_u = to_columns(
            jnp.einsum(
                "bis,bij->bjs", height, right_factor[layer], preferred_element_type=jnp.float32
            ).astype(jnp.bfloat16)
        )
        mixed_v = (
            self_gain * mixed_u.astype(jnp.float32) + cross_gain * flip(mixed_u).astype(jnp.float32)
        ).astype(jnp.bfloat16)
        outer = jnp.einsum(
            "bjs,jbk->kjs", mixed_v, left_bf[layer], preferred_element_type=jnp.float32
        ).astype(jnp.bfloat16)
        activation = to_rows(outer)
        saved.append((height, mixed_u, mixed_v, activation))
        height = (height.astype(jnp.float32) + jax.nn.silu(activation.astype(jnp.float32))).astype(
            jnp.bfloat16
        )
    output = height.reshape(blocks * BLOCK, samples)
    grad = cotangent.reshape(blocks, BLOCK, samples)
    rights = [None] * LAYERS
    lefts = [None] * LAYERS
    mixes = [None] * LAYERS
    for layer in reversed(range(LAYERS)):
        height_in, mixed_u, mixed_v, activation = saved[layer]
        self_gain = gains[layer, 0][:, :, None]
        cross_gain = gains[layer, 1][:, :, None]
        before = activation.astype(jnp.float32)
        logistic = jax.nn.sigmoid(before)
        error = (grad.astype(jnp.float32) * logistic * (1.0 + before * (1.0 - logistic))).astype(
            jnp.bfloat16
        )
        error_cols = to_columns(error)
        grad_v = jnp.einsum(
            "jbk,kjs->bjs", left_bf[layer], error_cols, preferred_element_type=jnp.float32
        ).astype(jnp.bfloat16)
        grad_vf = grad_v.astype(jnp.float32)
        carried = (cross_gain * grad_vf).astype(jnp.bfloat16)
        grad_u = to_rows(
            (self_gain * grad_vf + flip(carried).astype(jnp.float32)).astype(jnp.bfloat16)
        )
        lefts[layer] = jnp.einsum(
            "bjs,kjs->jbk", mixed_v, error_cols, preferred_element_type=jnp.float32
        )
        mixes[layer] = jnp.stack(
            [
                jnp.sum(grad_vf * mixed_u.astype(jnp.float32), axis=2),
                jnp.sum(grad_vf * flip(mixed_u).astype(jnp.float32), axis=2),
            ]
        )
        rights[layer] = jnp.einsum(
            "bis,bjs->bij", height_in, grad_u, preferred_element_type=jnp.float32
        )
        back_term = jnp.einsum(
            "bij,bjs->bis", right_factor[layer], grad_u, preferred_element_type=jnp.float32
        )
        grad = (grad.astype(jnp.float32) + back_term).astype(jnp.bfloat16)
    all_mix = lax.psum(jnp.stack(mixes), "samp")
    all_mix = lax.all_to_all(all_mix, ROW_AXES, split_axis=2, concat_axis=3, tiled=True)
    all_right = jnp.stack(
        [lax.psum(part.astype(jnp.bfloat16), "samp").astype(jnp.float32) for part in rights]
    )
    all_left = jnp.stack(
        [lax.psum(part.astype(jnp.bfloat16), "samp").astype(jnp.float32) for part in lefts]
    )
    return (output, grad.reshape(blocks * BLOCK, samples), all_right, all_left, all_mix)


def gated(kernel, count, gates):
    def run(*refs):
        kernel(*refs[:count], *refs[count + len(gates) :])

    return run, [pl.BlockSpec(memory_space=pl.ANY)] * len(gates)


def shuffle_rows(where, source, target, half):
    own_x, own_core = where[0], where[1] ^ pl.program_id(0)
    for group in range(BLOCK // (4 * half)):
        for dx in range(2):
            for dc in range(2):
                start = 4 * half * group + 2 * half * (own_x ^ dx) + half * (own_core ^ dc)
                rows = pl.ds(pl.multiple_of(start, half), half)
                here = pl.ds(4 * half * group + 2 * half * dx + half * dc, half)
                yield rows, here


def split_kernel(where, array_ref, pieces_ref):
    half = array_ref.shape[0]
    for rows, here in shuffle_rows(where, array_ref, pieces_ref, half):
        pieces_ref[0, 0, :, here, :] = array_ref[:, rows, :]


def merge_kernel(where, pieces_ref, array_ref):
    half = array_ref.shape[0]
    for rows, here in shuffle_rows(where, array_ref, pieces_ref, half):
        array_ref[:, rows, :] = pieces_ref[0, 0, :, here, :]


def split(where, array, chans, *gates):
    blocks, units, samples = array.shape
    half, part = blocks // 2, samples // chans
    kernel, extra = gated(split_kernel, 2, gates)
    return pl.pallas_call(
        kernel,
        out_shape=jax.ShapeDtypeStruct((2, chans, half, units, part), array.dtype),
        grid_spec=pltpu.PrefetchScalarGridSpec(
            num_scalar_prefetch=1,
            grid=(2, chans),
            in_specs=[pl.BlockSpec((half, units, part), lambda e, d, w: (w[1] ^ e, 0, w[2] ^ d))]
            + extra,
            out_specs=pl.BlockSpec((1, 1, half, units, part), lambda e, d, w: (e, d, 0, 0, 0)),
        ),
        cost_estimate=pl.CostEstimate(flops=0, bytes_accessed=4 * array.size, transcendentals=0),
        name="split",
    )(where, array, *gates)


def merge(where, pieces, *gates):
    _, chans, half, units, part = pieces.shape
    kernel, extra = gated(merge_kernel, 2, gates)
    return pl.pallas_call(
        kernel,
        out_shape=jax.ShapeDtypeStruct((2 * half, units, chans * part), pieces.dtype),
        grid_spec=pltpu.PrefetchScalarGridSpec(
            num_scalar_prefetch=1,
            grid=(2, chans),
            in_specs=[pl.BlockSpec((1, 1, half, units, part), lambda e, d, w: (e, d, 0, 0, 0))]
            + extra,
            out_specs=pl.BlockSpec((half, units, part), lambda e, d, w: (w[1] ^ e, 0, w[2] ^ d)),
        ),
        cost_estimate=pl.CostEstimate(flops=0, bytes_accessed=4 * pieces.size, transcendentals=0),
        name="merge",
    )(where, pieces, *gates)


HOPS = ((0, 0), (0, 1), (1, 0), (1, 1))
VMEM_LIMIT = 48 * 1024 * 1024


def cost(flops, *arrays):
    size = sum(a.size * a.dtype.itemsize for a in arrays)
    return pl.CostEstimate(flops=int(flops), bytes_accessed=int(size), transcendentals=0)


def join(pieces, index, half, swap=0):
    groups = pieces[0].shape[1] // half
    return jnp.concatenate(
        [
            pieces[2 * (dx ^ swap) + dc][index, half * g : half * g + half, :]
            for g in range(groups)
            for dx, dc in HOPS
        ],
        axis=0,
    )


def deal(pieces, index, half, value):
    groups = pieces[0].shape[1] // half
    for g in range(groups):
        for hop in range(4):
            start = half * (4 * g + hop)
            pieces[hop][index, half * g : half * g + half, :] = value[start : start + half, :]


def swap_dx(value, half):
    step = 2 * half
    return jnp.concatenate(
        [value[step * (i ^ 1) : step * (i ^ 1) + step, :] for i in range(value.shape[0] // step)],
        axis=0,
    )


def units_forward_kernel(half, *refs):
    u, (gain_ref, left_ref), v_ref, t = refs[:4], refs[4:6], refs[6], refs[7:]
    for i in range(left_ref.shape[0]):
        mine = join(u, i, half).astype(F32)
        partner = join(u, i, half, 1).astype(F32)
        v = (gain_ref[0, 0, :, i : i + 1] * mine + gain_ref[1, 0, :, i : i + 1] * partner).astype(BF16)
        v_ref[i] = v
        out = lax.dot_general(left_ref[i], v, (((0,), (0,)), ((), ())), preferred_element_type=F32)
        deal(t, i, half, out.astype(BF16))


def units_backward_kernel(half, *refs):
    e, u, (gain_ref, left_ref) = refs[:4], refs[4:8], refs[8:10]
    du, mix_ref = refs[10:14], refs[14]
    for i in range(left_ref.shape[0]):
        dv = jnp.dot(left_ref[i], join(e, i, half), preferred_element_type=F32)
        dv = dv.astype(BF16).astype(F32)
        mine = join(u, i, half).astype(F32)
        mix_ref[0, 0, :, i : i + 1] = jnp.sum(dv * mine, axis=1, keepdims=True)
        mix_ref[1, 0, :, i : i + 1] = jnp.sum(dv * swap_dx(mine, half), axis=1, keepdims=True)
        carried = (gain_ref[1, 0, :, i : i + 1] * dv).astype(BF16).astype(F32)
        value = gain_ref[0, 0, :, i : i + 1] * dv + swap_dx(carried, half)
        deal(du, i, half, value.astype(BF16))


TILE = 8


def units_forward(u, gain, left, half, *gates):
    own, part = u[0].shape[0], u[0].shape[2]
    piece = pl.BlockSpec((TILE, own, part), lambda i: (i, 0, 0))
    full = pl.BlockSpec((TILE, BLOCK, part), lambda i: (i, 0, 0))
    gains = pl.BlockSpec((2, 1, BLOCK, TILE), lambda i: (0, i, 0, 0))
    weight = pl.BlockSpec((TILE, BLOCK, BLOCK), lambda i: (i, 0, 0))
    shape = jax.ShapeDtypeStruct((own, own, part), BF16)
    v_shape = jax.ShapeDtypeStruct((own, BLOCK, part), BF16)
    kernel, extra = gated(functools.partial(units_forward_kernel, half), 6, gates)
    out = pl.pallas_call(
        kernel,
        grid=(own // TILE,),
        in_specs=[piece] * 4 + [gains, weight] + extra,
        out_specs=[full] + [piece] * 4,
        out_shape=[v_shape] + [shape] * 4,
        compiler_params=pltpu.CompilerParams(vmem_limit_bytes=VMEM_LIMIT),
        cost_estimate=cost(2 * own * BLOCK * BLOCK * part, left, v_shape, *u, *u),
        name="units_forward",
    )(*u, gain, left, *gates)
    return out[0], out[1:]


def units_backward(e, u, gain, left, half, *gates):
    own, part = u[0].shape[0], u[0].shape[2]
    piece = pl.BlockSpec((TILE, own, part), lambda i: (i, 0, 0))
    gains = pl.BlockSpec((2, 1, BLOCK, TILE), lambda i: (0, i, 0, 0))
    weight = pl.BlockSpec((TILE, BLOCK, BLOCK), lambda i: (i, 0, 0))
    shape = jax.ShapeDtypeStruct((own, own, part), BF16)
    kernel, extra = gated(functools.partial(units_backward_kernel, half), 10, gates)
    out = pl.pallas_call(
        kernel,
        grid=(own // TILE,),
        in_specs=[piece] * 8 + [gains, weight] + extra,
        out_specs=[piece] * 4 + [gains],
        out_shape=[shape] * 4 + [jax.ShapeDtypeStruct(gain.shape, F32)],
        compiler_params=pltpu.CompilerParams(vmem_limit_bytes=VMEM_LIMIT),
        cost_estimate=cost(2 * own * BLOCK * BLOCK * part, left, *u, *u, *u),
        name="units_backward",
    )(*e, *u, gain, left, *gates)
    return out[:4], out[4]


def gather_rows(pieces, scratch, half):
    for hop in range(4):
        turned = jnp.swapaxes(pieces[hop][...], 0, 1)
        for g in range(pieces[hop].shape[0] // half):
            start = half * (4 * g + hop)
            scratch[:, start : start + half, :] = turned[:, half * g : half * g + half, :]


def scatter_rows(scratch, pieces, half):
    for hop in range(4):
        for g in range(pieces[hop].shape[0] // half):
            start = half * (4 * g + hop)
            pieces[hop][half * g : half * g + half] = jnp.swapaxes(
                scratch[:, start : start + half, :], 0, 1
            )


def error_of(grad, before):
    logistic = jax.nn.sigmoid(before)
    return (grad * logistic * (1.0 + before * (1.0 - logistic))).astype(BF16)


def first_kernel(half, h_ref, right_ref, *refs):
    u, scratch = refs[:4], refs[4]
    for b in range(h_ref.shape[0]):
        out = lax.dot_general(
            right_ref[b], h_ref[b], (((0,), (0,)), ((), ())), preferred_element_type=F32
        )
        scratch[b] = out.astype(BF16)
    scatter_rows(scratch, u, half)


def middle_kernel(half, *refs):
    t, (h_ref, right_ref), (act_ref, next_ref), u = refs[:4], refs[4:6], refs[6:8], refs[8:12]
    scratch = refs[12]
    gather_rows(t, act_ref, half)
    for b in range(h_ref.shape[0]):
        height = (h_ref[b].astype(F32) + jax.nn.silu(act_ref[b].astype(F32))).astype(BF16)
        next_ref[b] = height
        out = lax.dot_general(
            right_ref[b], height, (((0,), (0,)), ((), ())), preferred_element_type=F32
        )
        scratch[b] = out.astype(BF16)
    scatter_rows(scratch, u, half)


def last_kernel(half, *refs):
    t, (h_ref, g_ref), next_ref, e = refs[:4], refs[4:6], refs[6], refs[7:11]
    act, scratch = refs[11:13]
    gather_rows(t, act, half)
    for b in range(h_ref.shape[0]):
        before = act[b].astype(F32)
        next_ref[b] = (h_ref[b].astype(F32) + jax.nn.silu(before)).astype(BF16)
        scratch[b] = error_of(g_ref[b].astype(F32), before)
    scatter_rows(scratch, e, half)


def back_kernel(half, *refs):
    du, (g_ref, right_ref, act_ref), (rows_ref, next_ref), e = refs[:4], refs[4:7], refs[7:9], refs[9:13]
    scratch = refs[13]
    gather_rows(du, rows_ref, half)
    for b in range(g_ref.shape[0]):
        term = jnp.dot(right_ref[b], rows_ref[b], preferred_element_type=F32)
        grad = (g_ref[b].astype(F32) + term).astype(BF16)
        next_ref[b] = grad
        scratch[b] = error_of(grad.astype(F32), act_ref[b].astype(F32))
    scatter_rows(scratch, e, half)


def final_kernel(half, *refs):
    du, (g_ref, right_ref), (rows_ref, next_ref) = refs[:4], refs[4:6], refs[6:8]
    gather_rows(du, rows_ref, half)
    for b in range(g_ref.shape[0]):
        term = jnp.dot(right_ref[b], rows_ref[b], preferred_element_type=F32)
        next_ref[b] = (g_ref[b].astype(F32) + term).astype(BF16)


def rows_call(kernel, half, ins, outs, scratches, *gates):
    own, part = 4 * half, 128
    rows = 16
    specs = {
        "p": pl.BlockSpec((own, rows, part), lambda i: (0, i, 0)),
        "r": pl.BlockSpec((rows, BLOCK, part), lambda i: (i, 0, 0)),
        "w": pl.BlockSpec((rows, BLOCK, BLOCK), lambda i: (i, 0, 0)),
    }
    shapes = {"p": (own, own, part), "r": (own, BLOCK, part)}
    out_shape = [jax.ShapeDtypeStruct(shapes[kind], BF16) for kind in outs]
    kinds = [kind for kind, _ in ins]
    arrays = [array for _, array in ins]
    flops = 2 * own * BLOCK * BLOCK * part if "w" in kinds else 0
    run, extra = gated(functools.partial(kernel, half), len(ins), gates)
    return pl.pallas_call(
        run,
        grid=(own // rows,),
        in_specs=[specs[kind] for kind in kinds] + extra,
        out_specs=[specs[kind] for kind in outs],
        out_shape=out_shape,
        scratch_shapes=[pltpu.VMEM((rows, BLOCK, part), BF16)] * scratches,
        compiler_params=pltpu.CompilerParams(vmem_limit_bytes=VMEM_LIMIT),
        cost_estimate=cost(flops, *arrays, *out_shape),
        name=kernel.__name__,
    )(*arrays, *gates)


def left_sum_kernel(half, where, *refs):
    v, e, out_ref = refs[:2], (refs[2:6], refs[6:10]), refs[10]
    for i in range(out_ref.shape[1]):
        total = 0.0
        for q in range(2):
            total += lax.dot_general(
                v[q][i], join(e[q], i, half), (((1,), (1,)), ((), ())), preferred_element_type=F32
            )
        out_ref[0, i] = total.astype(BF16)


def right_sum_kernel(half, where, *refs):
    h, du, out_ref = refs[:2], refs[2:4], refs[4]
    for i in range(out_ref.shape[1]):
        total = 0.0
        for q in range(2):
            total += lax.dot_general(
                h[q][i], du[q][i], (((1,), (1,)), ((), ())), preferred_element_type=F32
            )
        out_ref[0, i] = total.astype(BF16)


def sum_call(kernel, where, other, half, arrays):
    quarter = half // 2
    chans = arrays[0].shape[0] // half
    out_shape = jax.ShapeDtypeStruct((chans, quarter, BLOCK, BLOCK), BF16)

    def tile(g, w):
        return (2 * g + (w[3] ^ other), 0, 0)

    return pl.pallas_call(
        functools.partial(kernel, half),
        out_shape=out_shape,
        grid_spec=pltpu.PrefetchScalarGridSpec(
            num_scalar_prefetch=1,
            grid=(chans,),
            in_specs=[pl.BlockSpec((quarter,) + a.shape[1:], tile) for a in arrays],
            out_specs=pl.BlockSpec((1, quarter, BLOCK, BLOCK), lambda g, w: (g, 0, 0, 0)),
        ),
        compiler_params=pltpu.CompilerParams(vmem_limit_bytes=VMEM_LIMIT),
        cost_estimate=cost(4 * chans * quarter * BLOCK * BLOCK * 128, *arrays),
        name=kernel.__name__,
    )(where, *arrays)


def weave_kernel(where, mine_ref, other_ref, out_ref):
    @pl.when(pl.program_id(1) == where[3])
    def _():
        out_ref[0, 0] = mine_ref[0]

    @pl.when(pl.program_id(1) != where[3])
    def _():
        out_ref[0, 0] = other_ref[0]


def weave(where, mine, other, *gates):
    block = (1,) + mine.shape[1:]
    spec = pl.BlockSpec(block, lambda g, y, w: (g, 0, 0, 0))
    kernel, extra = gated(weave_kernel, 3, gates)
    return pl.pallas_call(
        kernel,
        out_shape=jax.ShapeDtypeStruct(mine.shape[:1] + (2,) + mine.shape[1:], mine.dtype),
        grid_spec=pltpu.PrefetchScalarGridSpec(
            num_scalar_prefetch=1,
            grid=(mine.shape[0], 2),
            in_specs=[spec, spec] + extra,
            out_specs=pl.BlockSpec((1,) + block, lambda g, y, w: (g, y, 0, 0, 0)),
        ),
        cost_estimate=pl.CostEstimate(flops=0, bytes_accessed=8 * mine.size, transcendentals=0),
        name="weave",
    )(where, mine, other, *gates)


def prepare_kernel(half, where, factor_ref, out_ref):
    mask = 2 * half * where[0] + half * where[1]
    rows = lax.broadcasted_iota(jnp.int32, (BLOCK, BLOCK), 0)
    columns = lax.broadcasted_iota(jnp.int32, (BLOCK, BLOCK), 1)
    swap = jnp.where(rows == (columns ^ mask), 1.0, 0.0).astype(BF16)
    for i in range(out_ref.shape[0]):
        turned = jnp.dot(swap, factor_ref[0, i].astype(BF16), preferred_element_type=F32)
        out_ref[i] = jnp.dot(
            turned.astype(BF16), swap, preferred_element_type=F32
        ).astype(BF16)


def prepare(where, factor, layer, half, *gates):
    kernel, extra = gated(functools.partial(prepare_kernel, half), 2, gates)
    block = (1, half // 2) + factor.shape[2:]
    whole = factor.shape[1] == block[1]
    spec = pl.BlockSpec(block, lambda i, w: (layer, 0 if whole else 2 * w[1] + w[3], 0, 0))
    return pl.pallas_call(
        kernel,
        out_shape=jax.ShapeDtypeStruct(block[1:], BF16),
        grid_spec=pltpu.PrefetchScalarGridSpec(
            num_scalar_prefetch=1,
            grid=(1,),
            in_specs=[spec] + extra,
            out_specs=pl.BlockSpec(block[1:], lambda i, w: (0, 0, 0)),
        ),
        cost_estimate=pl.CostEstimate(flops=2**29, bytes_accessed=2**22, transcendentals=0),
        name="prepare",
    )(where, factor, *gates)


def total_kernel(keep_ref, got_ref, out_ref):
    out_ref[...] = (keep_ref[...].astype(F32) + got_ref[...].astype(F32)).astype(BF16)


def total_of(keep, got, *gates):
    kernel, extra = gated(total_kernel, 2, gates)
    spec = pl.BlockSpec((1,) + keep.shape[1:], lambda g: (g, 0, 0, 0))
    return pl.pallas_call(
        kernel,
        out_shape=jax.ShapeDtypeStruct(keep.shape, BF16),
        grid=keep.shape[:1],
        in_specs=[spec, spec] + extra,
        out_specs=spec,
        cost_estimate=pl.CostEstimate(flops=0, bytes_accessed=6 * keep.size, transcendentals=0),
        name="total_of",
    )(keep, got, *gates)


def after(value, *others):
    return lax.optimization_barrier((value,) + others)[0]


def planes(features, cotangent, right_factor, left_factor, mixing):
    blocks = right_factor.shape[1]
    samples = features.shape[1]
    chans, samps = lax.axis_size("chan"), lax.axis_size("samp")
    half, quarter, part = blocks // 2, blocks // 4, samples // chans
    own = chans * half
    chan, own_x, samp = lax.axis_index("chan"), lax.axis_index("bfly"), lax.axis_index("samp")
    row, core = samp // 2, samp % 2
    where = jnp.stack([own_x, core, chan, row]).astype(jnp.int32)

    def over_chan(values, distance):
        return lax.ppermute(values, "chan", [(i, i ^ distance) for i in range(chans)])

    def over_samp(values, distance):
        return lax.ppermute(values, "samp", [(i, i ^ distance) for i in range(samps)])

    def in_plane(values, dx, dc):
        if dx == 0 and dc == 0:
            return values
        route = [(i, i ^ (dx * samps + dc)) for i in range(2 * samps)]
        return lax.ppermute(values, ("bfly", "samp"), route)

    def enter(array, *gates):
        pieces = split(where, array.reshape(blocks, BLOCK, samples), chans, *gates)
        mine, other = pieces[0], over_samp(pieces[1], 1)
        chunks = []
        for core_of in range(2):
            chunk = jnp.zeros((chans, half, BLOCK, part), BF16)
            for distance in range(chans):
                piece = jnp.where(core == core_of, mine[distance], other[distance])
                if distance:
                    piece = over_chan(piece, distance)
                chunk = lax.dynamic_update_index_in_dim(chunk, piece, chan ^ distance, 0)
            chunks.append(chunk.reshape(own, BLOCK, part))
        return pieces, chunks

    def leave_planes(chunks):
        arrived = []
        for chunk in chunks:
            chunk = chunk.reshape(chans, half, BLOCK, part)
            arrived.append([])
            for distance in range(chans):
                piece = lax.dynamic_index_in_dim(chunk, chan ^ distance, 0, keepdims=False)
                arrived[-1].append(over_chan(piece, distance) if distance else piece)
        return arrived

    def leave_chip(arrived, *gates):
        first, second = (jnp.stack(pieces) for pieces in arrived)
        keep = jnp.where(core == 0, first, second)
        got = over_samp(jnp.where(core == 0, second, first), 1)
        return merge(where, jnp.stack([keep, got]), *gates).reshape(blocks * BLOCK, samples)

    def gather_row(mine, *gates):
        return weave(where, mine, over_samp(mine, 2), *gates).reshape(own, BLOCK, BLOCK)

    def sum_factor(kernel, arrays):
        send = sum_call(kernel, where, 1, half, arrays)
        keep = sum_call(kernel, where, 0, half, arrays)
        return keep, send, over_samp(send, 2)

    def spread_factor(parts, *gates):
        total = total_of(parts[0], parts[2], *gates)
        return lax.psum_scatter(total, "chan", scatter_dimension=0, tiled=False)

    def finish_factor(total, *gates):
        total = prepare(where, total[None], 0, half, *gates)
        whole = lax.all_gather(total, "samp").reshape(2, 2, quarter, BLOCK, BLOCK)
        return total, jnp.swapaxes(whole, 0, 1).reshape(blocks, BLOCK, BLOCK).astype(F32)

    def swap_pieces(pieces):
        return [in_plane(piece, dx, dc) for piece, (dx, dc) in zip(pieces, HOPS)]

    both = range(2)
    ready = prepare(where, right_factor, 0, half)
    right_mine = lax.all_gather(ready, "chan")
    entered, features_in = enter(features, ready)
    heights = [features_in]
    ready = prepare(where, left_factor, 0, half, entered)
    left_mine = lax.all_gather(ready, "chan")
    rights_in = [gather_row(right_mine), None]
    gains = lax.all_gather(after(mixing, ready), ROW_AXES, axis=2, tiled=True)
    gains = gains.reshape(LAYERS, 2, chans, 2, 2, half, BLOCK)
    gains = jnp.where(own_x == 1, gains[:, :, :, ::-1], gains)
    gains = jnp.where(core == 1, gains[:, :, :, :, ::-1], gains)
    gains = gains.reshape(LAYERS, 2, BLOCK, chans, 4, half)
    gains = lax.dynamic_index_in_dim(gains, 2 * own_x + core, 4, keepdims=False)
    gains = gains.reshape(LAYERS, 2, BLOCK, own // TILE, TILE).swapaxes(2, 3)

    mixed_u, mixed_v, act = [[None] * 2 for _ in range(LAYERS)], [[None] * 2 for _ in range(LAYERS)], [None] * 2
    outer, sent = [None] * 2, [None] * 2
    for q in both:
        ins = [("r", heights[0][q]), ("w", rights_in[0])]
        sent[q] = rows_call(first_kernel, half, ins, "pppp", 1)
        mixed_u[0][q] = swap_pieces(sent[q])
    first = sent[:]
    lefts_in = [gather_row(left_mine, first[0][0]), None]
    right_mine = lax.all_gather(prepare(where, right_factor, 1, half, first[0][0]), "chan")
    left_mine = lax.all_gather(prepare(where, left_factor, 1, half, first[1][0]), "chan")
    for q in both:
        gates = [first[1][0]] if q == 0 else []
        mixed_v[0][q], sent[q] = units_forward(mixed_u[0][q], gains[0], lefts_in[0], half, *gates)
        outer[q] = swap_pieces(sent[q])
    rights_in[1] = gather_row(right_mine, sent[0][0])
    _, grad = enter(cotangent, sent[0][0])
    heights.append([None] * 2)
    last = sent[1][0]
    for q in both:
        ins = [("p", p) for p in outer[q]] + [("r", heights[0][q]), ("w", rights_in[1])]
        gates = [last] if q == 0 else []
        out = rows_call(middle_kernel, half, ins, "rrpppp", 1, *gates)
        act[q], heights[1][q] = out[:2]
        sent[q] = out[2:]
        mixed_u[1][q] = swap_pieces(out[2:])
    lefts_in[1] = gather_row(left_mine, sent[0][0])
    last = sent[1][0]
    for q in both:
        gates = [last] if q == 0 else []
        mixed_v[1][q], sent[q] = units_forward(mixed_u[1][q], gains[1], lefts_in[1], half, *gates)
        outer[q] = swap_pieces(sent[q])
    error, final = [None] * 2, [None] * 2
    last = sent[1][0]
    for q in both:
        ins = [("p", p) for p in outer[q]] + [("r", heights[1][q]), ("r", grad[q])]
        gates = [last] if q == 0 else []
        out = rows_call(last_kernel, half, ins, "rpppp", 2, *gates)
        final[q] = out[0]
        error[q] = swap_pieces(out[1:])
    out_parts = leave_planes(final)
    mix = [None] * LAYERS
    grad_u = [None] * 2
    for q in both:
        gates = [final[1]] if q == 0 else []
        sent[q], mix_q = units_backward(error[q], mixed_u[1][q], gains[1], lefts_in[1], half, *gates)
        mix[1] = mix_q if q == 0 else mix[1] + mix_q
        grad_u[q] = swap_pieces(sent[q])
    left_1 = sum_factor(left_sum_kernel, mixed_v[1] + error[0] + error[1])
    rows = [None] * 2
    error = [None] * 2
    last = sent[1][0]
    for q in both:
        ins = [("p", p) for p in grad_u[q]]
        ins += [("r", grad[q]), ("w", rights_in[1]), ("r", act[q])]
        gates = [last, left_1[1]] if q == 0 else out_parts[0][1:]
        out = rows_call(back_kernel, half, ins, "rrpppp", 1, *gates)
        rows[q], grad[q] = out[:2]
        sent[q] = out[2:]
        error[q] = swap_pieces(out[2:])
    left_1 = spread_factor(left_1, sent[1][0])
    right_1 = sum_factor(right_sum_kernel, heights[1] + rows)
    for q in both:
        gates = [right_1[1]] if q == 0 else out_parts[1][1:]
        sent[q], mix_q = units_backward(error[q], mixed_u[0][q], gains[0], lefts_in[0], half, *gates)
        mix[0] = mix_q if q == 0 else mix[0] + mix_q
        grad_u[q] = swap_pieces(sent[q])
    right_1 = spread_factor(right_1, sent[1][0])
    output = leave_chip(out_parts, sent[1][0])
    left_0 = sum_factor(left_sum_kernel, mixed_v[0] + error[0] + error[1])
    left_1 = finish_factor(left_1, sent[1][0])
    rows = [None] * 2
    for q in both:
        ins = [("p", p) for p in grad_u[q]] + [("r", grad[q]), ("w", rights_in[0])]
        gates = [left_0[1], sent[1][0]] if q == 0 else [output, left_1[0]]
        rows[q], grad[q] = rows_call(final_kernel, half, ins, "rr", 0, *gates)
    in_parts = leave_planes(grad)
    left_0 = spread_factor(left_0, rows[0])
    right_0 = sum_factor(right_sum_kernel, heights[0] + rows)
    right_1 = finish_factor(right_1, rows[0])
    left_0 = finish_factor(left_0, right_0[1])
    right_0 = finish_factor(spread_factor(right_0, right_1[0], *in_parts[0][1:]))
    feature_grad = leave_chip(in_parts)
    mix = jnp.stack(mix).swapaxes(2, 3).reshape(LAYERS, 2, chans, 2, 2, half, own)
    mix = jnp.where(own_x == 1, mix[:, :, :, ::-1], mix)
    mix = jnp.where(core == 1, mix[:, :, :, :, ::-1], mix)
    mix = lax.psum_scatter(mix, "chan", scatter_dimension=2, tiled=False)
    mix = lax.all_gather(mix, ("bfly", "samp")).reshape((2, 2, 2) + mix.shape)
    mix = mix[:, 0] + mix[:, 1]
    mix = lax.dynamic_index_in_dim(mix, own_x, 4, keepdims=False)
    mix = mix.reshape(2, 2, LAYERS, 2, blocks, chans, half)
    mix = mix.transpose(2, 3, 4, 5, 0, 1, 6).reshape(LAYERS, 2, blocks, BLOCK)
    grad_right_0, grad_right_1 = right_0[1], right_1[1]
    grad_left_0, grad_left_1 = left_0[1], left_1[1]
    rights = jnp.stack([grad_right_0, grad_right_1])
    return (output, feature_grad, rights, jnp.stack([grad_left_0, grad_left_1]), mix)


def solution(mesh):
    sizes = dict(mesh.shape)
    fits = sizes["chan"] == 4 and sizes["bfly"] == 2 and sizes["samp"] == 4
    local = planes if fits else stationary
    rows = P(ROW_AXES, "samp")
    factors = P(None, ROW_AXES, None, None)
    gains = P(None, None, ROW_AXES, None)
    return jax.shard_map(
        local,
        mesh=mesh,
        in_specs=(rows, rows, factors, factors, gains),
        out_specs=(rows, rows, factors, factors, gains),
        check_vma=False,
    )
```

```python
import functools

import jax
import jax.numpy as jnp
from jax import lax
from jax.experimental import pallas as pl
from jax.experimental.pallas import tpu as pltpu
from jax.sharding import PartitionSpec as P

BLOCK = 256
LAYERS = 2
ROW_AXES = ("chan", "bfly")
F32 = jnp.float32
BF16 = jnp.bfloat16


def to_columns(values):
    return lax.all_to_all(values, ROW_AXES, split_axis=1, concat_axis=0, tiled=True)


def to_rows(values):
    return lax.all_to_all(values, ROW_AXES, split_axis=0, concat_axis=1, tiled=True)


def stationary(features, cotangent, right_factor, left_factor, mixing):
    blocks = right_factor.shape[1]
    samples = features.shape[1]
    pairs = lax.axis_size("bfly")

    def flip(values):
        grouped = values.reshape((-1, pairs // 2, 2, blocks) + values.shape[1:])
        return grouped[:, :, ::-1].reshape(values.shape)

    left_bf = left_factor.astype(jnp.bfloat16)
    gains = lax.all_to_all(mixing, ROW_AXES, split_axis=3, concat_axis=2, tiled=True)
    height = features.reshape(blocks, BLOCK, samples)
    saved = []
    for layer in range(LAYERS):
        self_gain = gains[layer, 0][:, :, None]
        cross_gain = gains[layer, 1][:, :, None]
        mixed_u = to_columns(
            jnp.einsum(
                "bis,bij->bjs", height, right_factor[layer], preferred_element_type=jnp.float32
            ).astype(jnp.bfloat16)
        )
        mixed_v = (
            self_gain * mixed_u.astype(jnp.float32) + cross_gain * flip(mixed_u).astype(jnp.float32)
        ).astype(jnp.bfloat16)
        outer = jnp.einsum(
            "bjs,jbk->kjs", mixed_v, left_bf[layer], preferred_element_type=jnp.float32
        ).astype(jnp.bfloat16)
        activation = to_rows(outer)
        saved.append((height, mixed_u, mixed_v, activation))
        height = (height.astype(jnp.float32) + jax.nn.silu(activation.astype(jnp.float32))).astype(
            jnp.bfloat16
        )
    output = height.reshape(blocks * BLOCK, samples)
    grad = cotangent.reshape(blocks, BLOCK, samples)
    rights = [None] * LAYERS
    lefts = [None] * LAYERS
    mixes = [None] * LAYERS
    for layer in reversed(range(LAYERS)):
        height_in, mixed_u, mixed_v, activation = saved[layer]
        self_gain = gains[layer, 0][:, :, None]
        cross_gain = gains[layer, 1][:, :, None]
        before = activation.astype(jnp.float32)
        logistic = jax.nn.sigmoid(before)
        error = (grad.astype(jnp.float32) * logistic * (1.0 + before * (1.0 - logistic))).astype(
            jnp.bfloat16
        )
        error_cols = to_columns(error)
        grad_v = jnp.einsum(
            "jbk,kjs->bjs", left_bf[layer], error_cols, preferred_element_type=jnp.float32
        ).astype(jnp.bfloat16)
        grad_vf = grad_v.astype(jnp.float32)
        carried = (cross_gain * grad_vf).astype(jnp.bfloat16)
        grad_u = to_rows(
            (self_gain * grad_vf + flip(carried).astype(jnp.float32)).astype(jnp.bfloat16)
        )
        lefts[layer] = jnp.einsum(
            "bjs,kjs->jbk", mixed_v, error_cols, preferred_element_type=jnp.float32
        )
        mixes[layer] = jnp.stack(
            [
                jnp.sum(grad_vf * mixed_u.astype(jnp.float32), axis=2),
                jnp.sum(grad_vf * flip(mixed_u).astype(jnp.float32), axis=2),
            ]
        )
        rights[layer] = jnp.einsum(
            "bis,bjs->bij", height_in, grad_u, preferred_element_type=jnp.float32
        )
        back_term = jnp.einsum(
            "bij,bjs->bis", right_factor[layer], grad_u, preferred_element_type=jnp.float32
        )
        grad = (grad.astype(jnp.float32) + back_term).astype(jnp.bfloat16)
    all_mix = lax.psum(jnp.stack(mixes), "samp")
    all_mix = lax.all_to_all(all_mix, ROW_AXES, split_axis=2, concat_axis=3, tiled=True)
    all_right = jnp.stack(
        [lax.psum(part.astype(jnp.bfloat16), "samp").astype(jnp.float32) for part in rights]
    )
    all_left = jnp.stack(
        [lax.psum(part.astype(jnp.bfloat16), "samp").astype(jnp.float32) for part in lefts]
    )
    return (output, grad.reshape(blocks * BLOCK, samples), all_right, all_left, all_mix)


def gated(kernel, count, gates):
    def run(*refs):
        kernel(*refs[:count], *refs[count + len(gates) :])

    return run, [pl.BlockSpec(memory_space=pl.ANY)] * len(gates)


def shuffle_rows(where, source, target, half):
    own_x, own_core = where[0], where[1] ^ pl.program_id(0)
    for group in range(BLOCK // (4 * half)):
        for dx in range(2):
            for dc in range(2):
                start = 4 * half * group + 2 * half * (own_x ^ dx) + half * (own_core ^ dc)
                rows = pl.ds(pl.multiple_of(start, half), half)
                here = pl.ds(4 * half * group + 2 * half * dx + half * dc, half)
                yield rows, here


def split_kernel(where, array_ref, pieces_ref):
    half = array_ref.shape[0]
    for rows, here in shuffle_rows(where, array_ref, pieces_ref, half):
        pieces_ref[0, 0, :, here, :] = array_ref[:, rows, :]


def merge_kernel(where, pieces_ref, array_ref):
    half = array_ref.shape[0]
    for rows, here in shuffle_rows(where, array_ref, pieces_ref, half):
        array_ref[:, rows, :] = pieces_ref[0, 0, :, here, :]


def split(where, array, chans, *gates):
    blocks, units, samples = array.shape
    half, part = blocks // 2, samples // chans
    kernel, extra = gated(split_kernel, 2, gates)
    return pl.pallas_call(
        kernel,
        out_shape=jax.ShapeDtypeStruct((2, chans, half, units, part), array.dtype),
        grid_spec=pltpu.PrefetchScalarGridSpec(
            num_scalar_prefetch=1,
            grid=(2, chans),
            in_specs=[pl.BlockSpec((half, units, part), lambda e, d, w: (w[1] ^ e, 0, w[2] ^ d))]
            + extra,
            out_specs=pl.BlockSpec((1, 1, half, units, part), lambda e, d, w: (e, d, 0, 0, 0)),
        ),
        cost_estimate=pl.CostEstimate(flops=0, bytes_accessed=4 * array.size, transcendentals=0),
        name="split",
    )(where, array, *gates)


def merge(where, pieces, *gates):
    _, chans, half, units, part = pieces.shape
    kernel, extra = gated(merge_kernel, 2, gates)
    return pl.pallas_call(
        kernel,
        out_shape=jax.ShapeDtypeStruct((2 * half, units, chans * part), pieces.dtype),
        grid_spec=pltpu.PrefetchScalarGridSpec(
            num_scalar_prefetch=1,
            grid=(2, chans),
            in_specs=[pl.BlockSpec((1, 1, half, units, part), lambda e, d, w: (e, d, 0, 0, 0))]
            + extra,
            out_specs=pl.BlockSpec((half, units, part), lambda e, d, w: (w[1] ^ e, 0, w[2] ^ d)),
        ),
        cost_estimate=pl.CostEstimate(flops=0, bytes_accessed=4 * pieces.size, transcendentals=0),
        name="merge",
    )(where, pieces, *gates)


HOPS = ((0, 0), (0, 1), (1, 0), (1, 1))
VMEM_LIMIT = 48 * 1024 * 1024


def cost(flops, *arrays):
    size = sum(a.size * a.dtype.itemsize for a in arrays)
    return pl.CostEstimate(flops=int(flops), bytes_accessed=int(size), transcendentals=0)


def join(pieces, index, half, swap=0):
    groups = pieces[0].shape[1] // half
    return jnp.concatenate(
        [
            pieces[2 * (dx ^ swap) + dc][index, half * g : half * g + half, :]
            for g in range(groups)
            for dx, dc in HOPS
        ],
        axis=0,
    )


def deal(pieces, index, half, value):
    groups = pieces[0].shape[1] // half
    for g in range(groups):
        for hop in range(4):
            start = half * (4 * g + hop)
            pieces[hop][index, half * g : half * g + half, :] = value[start : start + half, :]


def swap_dx(value, half):
    step = 2 * half
    return jnp.concatenate(
        [value[step * (i ^ 1) : step * (i ^ 1) + step, :] for i in range(value.shape[0] // step)],
        axis=0,
    )


def units_forward_kernel(half, *refs):
    u, (gain_ref, left_ref), v_ref, t = refs[:4], refs[4:6], refs[6], refs[7:]
    for i in range(left_ref.shape[0]):
        mine = join(u, i, half).astype(F32)
        partner = join(u, i, half, 1).astype(F32)
        v = (gain_ref[0, 0, :, i : i + 1] * mine + gain_ref[1, 0, :, i : i + 1] * partner).astype(BF16)
        v_ref[i] = v
        out = lax.dot_general(left_ref[i], v, (((0,), (0,)), ((), ())), preferred_element_type=F32)
        deal(t, i, half, out.astype(BF16))


def units_backward_kernel(half, *refs):
    e, u, (gain_ref, left_ref) = refs[:4], refs[4:8], refs[8:10]
    du, mix_ref = refs[10:14], refs[14]
    for i in range(left_ref.shape[0]):
        dv = jnp.dot(left_ref[i], join(e, i, half), preferred_element_type=F32)
        dv = dv.astype(BF16).astype(F32)
        mine = join(u, i, half).astype(F32)
        mix_ref[0, 0, :, i : i + 1] = jnp.sum(dv * mine, axis=1, keepdims=True)
        mix_ref[1, 0, :, i : i + 1] = jnp.sum(dv * swap_dx(mine, half), axis=1, keepdims=True)
        carried = (gain_ref[1, 0, :, i : i + 1] * dv).astype(BF16).astype(F32)
        value = gain_ref[0, 0, :, i : i + 1] * dv + swap_dx(carried, half)
        deal(du, i, half, value.astype(BF16))


TILE = 8


def units_forward(u, gain, left, half, *gates):
    own, part = u[0].shape[0], u[0].shape[2]
    piece = pl.BlockSpec((TILE, own, part), lambda i: (i, 0, 0))
    full = pl.BlockSpec((TILE, BLOCK, part), lambda i: (i, 0, 0))
    gains = pl.BlockSpec((2, 1, BLOCK, TILE), lambda i: (0, i, 0, 0))
    weight = pl.BlockSpec((TILE, BLOCK, BLOCK), lambda i: (i, 0, 0))
    shape = jax.ShapeDtypeStruct((own, own, part), BF16)
    v_shape = jax.ShapeDtypeStruct((own, BLOCK, part), BF16)
    kernel, extra = gated(functools.partial(units_forward_kernel, half), 6, gates)
    out = pl.pallas_call(
        kernel,
        grid=(own // TILE,),
        in_specs=[piece] * 4 + [gains, weight] + extra,
        out_specs=[full] + [piece] * 4,
        out_shape=[v_shape] + [shape] * 4,
        compiler_params=pltpu.CompilerParams(vmem_limit_bytes=VMEM_LIMIT),
        cost_estimate=cost(2 * own * BLOCK * BLOCK * part, left, v_shape, *u, *u),
        name="units_forward",
    )(*u, gain, left, *gates)
    return out[0], out[1:]


def units_backward(e, u, gain, left, half, *gates):
    own, part = u[0].shape[0], u[0].shape[2]
    piece = pl.BlockSpec((TILE, own, part), lambda i: (i, 0, 0))
    gains = pl.BlockSpec((2, 1, BLOCK, TILE), lambda i: (0, i, 0, 0))
    weight = pl.BlockSpec((TILE, BLOCK, BLOCK), lambda i: (i, 0, 0))
    shape = jax.ShapeDtypeStruct((own, own, part), BF16)
    kernel, extra = gated(functools.partial(units_backward_kernel, half), 10, gates)
    out = pl.pallas_call(
        kernel,
        grid=(own // TILE,),
        in_specs=[piece] * 8 + [gains, weight] + extra,
        out_specs=[piece] * 4 + [gains],
        out_shape=[shape] * 4 + [jax.ShapeDtypeStruct(gain.shape, F32)],
        compiler_params=pltpu.CompilerParams(vmem_limit_bytes=VMEM_LIMIT),
        cost_estimate=cost(2 * own * BLOCK * BLOCK * part, left, *u, *u, *u),
        name="units_backward",
    )(*e, *u, gain, left, *gates)
    return out[:4], out[4]


def gather_rows(pieces, scratch, half):
    for hop in range(4):
        turned = jnp.swapaxes(pieces[hop][...], 0, 1)
        for g in range(pieces[hop].shape[0] // half):
            start = half * (4 * g + hop)
            scratch[:, start : start + half, :] = turned[:, half * g : half * g + half, :]


def scatter_rows(scratch, pieces, half):
    for hop in range(4):
        for g in range(pieces[hop].shape[0] // half):
            start = half * (4 * g + hop)
            pieces[hop][half * g : half * g + half] = jnp.swapaxes(
                scratch[:, start : start + half, :], 0, 1
            )


def error_of(grad, before):
    logistic = jax.nn.sigmoid(before)
    return (grad * logistic * (1.0 + before * (1.0 - logistic))).astype(BF16)


def first_kernel(half, h_ref, right_ref, *refs):
    u, scratch = refs[:4], refs[4]
    for b in range(h_ref.shape[0]):
        out = lax.dot_general(
            right_ref[b], h_ref[b], (((0,), (0,)), ((), ())), preferred_element_type=F32
        )
        scratch[b] = out.astype(BF16)
    scatter_rows(scratch, u, half)


def middle_kernel(half, *refs):
    t, (h_ref, right_ref), (act_ref, next_ref), u = refs[:4], refs[4:6], refs[6:8], refs[8:12]
    scratch = refs[12]
    gather_rows(t, act_ref, half)
    for b in range(h_ref.shape[0]):
        height = (h_ref[b].astype(F32) + jax.nn.silu(act_ref[b].astype(F32))).astype(BF16)
        next_ref[b] = height
        out = lax.dot_general(
            right_ref[b], height, (((0,), (0,)), ((), ())), preferred_element_type=F32
        )
        scratch[b] = out.astype(BF16)
    scatter_rows(scratch, u, half)


def last_kernel(half, *refs):
    t, (h_ref, g_ref), next_ref, e = refs[:4], refs[4:6], refs[6], refs[7:11]
    act, scratch = refs[11:13]
    gather_rows(t, act, half)
    for b in range(h_ref.shape[0]):
        before = act[b].astype(F32)
        next_ref[b] = (h_ref[b].astype(F32) + jax.nn.silu(before)).astype(BF16)
        scratch[b] = error_of(g_ref[b].astype(F32), before)
    scatter_rows(scratch, e, half)


def back_kernel(half, *refs):
    du, (g_ref, right_ref, act_ref), (rows_ref, next_ref), e = refs[:4], refs[4:7], refs[7:9], refs[9:13]
    scratch = refs[13]
    gather_rows(du, rows_ref, half)
    for b in range(g_ref.shape[0]):
        term = jnp.dot(right_ref[b], rows_ref[b], preferred_element_type=F32)
        grad = (g_ref[b].astype(F32) + term).astype(BF16)
        next_ref[b] = grad
        scratch[b] = error_of(grad.astype(F32), act_ref[b].astype(F32))
    scatter_rows(scratch, e, half)


def final_kernel(half, *refs):
    du, (g_ref, right_ref), (rows_ref, next_ref) = refs[:4], refs[4:6], refs[6:8]
    gather_rows(du, rows_ref, half)
    for b in range(g_ref.shape[0]):
        term = jnp.dot(right_ref[b], rows_ref[b], preferred_element_type=F32)
        next_ref[b] = (g_ref[b].astype(F32) + term).astype(BF16)


def rows_call(kernel, half, ins, outs, scratches, *gates):
    own, part = 4 * half, 128
    rows = 16
    specs = {
        "p": pl.BlockSpec((own, rows, part), lambda i: (0, i, 0)),
        "r": pl.BlockSpec((rows, BLOCK, part), lambda i: (i, 0, 0)),
        "w": pl.BlockSpec((rows, BLOCK, BLOCK), lambda i: (i, 0, 0)),
    }
    shapes = {"p": (own, own, part), "r": (own, BLOCK, part)}
    out_shape = [jax.ShapeDtypeStruct(shapes[kind], BF16) for kind in outs]
    kinds = [kind for kind, _ in ins]
    arrays = [array for _, array in ins]
    flops = 2 * own * BLOCK * BLOCK * part if "w" in kinds else 0
    run, extra = gated(functools.partial(kernel, half), len(ins), gates)
    return pl.pallas_call(
        run,
        grid=(own // rows,),
        in_specs=[specs[kind] for kind in kinds] + extra,
        out_specs=[specs[kind] for kind in outs],
        out_shape=out_shape,
        scratch_shapes=[pltpu.VMEM((rows, BLOCK, part), BF16)] * scratches,
        compiler_params=pltpu.CompilerParams(vmem_limit_bytes=VMEM_LIMIT),
        cost_estimate=cost(flops, *arrays, *out_shape),
        name=kernel.__name__,
    )(*arrays, *gates)


def left_sum_kernel(half, where, *refs):
    v, e, out_ref = refs[:2], (refs[2:6], refs[6:10]), refs[10]
    for i in range(out_ref.shape[1]):
        total = 0.0
        for q in range(2):
            total += lax.dot_general(
                v[q][i], join(e[q], i, half), (((1,), (1,)), ((), ())), preferred_element_type=F32
            )
        out_ref[0, i] = total.astype(BF16)


def right_sum_kernel(half, where, *refs):
    h, du, out_ref = refs[:2], refs[2:4], refs[4]
    for i in range(out_ref.shape[1]):
        total = 0.0
        for q in range(2):
            total += lax.dot_general(
                h[q][i], du[q][i], (((1,), (1,)), ((), ())), preferred_element_type=F32
            )
        out_ref[0, i] = total.astype(BF16)


def sum_call(kernel, where, other, half, arrays, *gates):
    quarter = half // 2
    chans = arrays[0].shape[0] // half
    out_shape = jax.ShapeDtypeStruct((chans, quarter, BLOCK, BLOCK), BF16)

    def tile(g, w):
        return (2 * g + (w[3] ^ other), 0, 0)

    run, extra = gated(functools.partial(kernel, half), 1 + len(arrays), gates)
    return pl.pallas_call(
        run,
        out_shape=out_shape,
        grid_spec=pltpu.PrefetchScalarGridSpec(
            num_scalar_prefetch=1,
            grid=(chans,),
            in_specs=[pl.BlockSpec((quarter,) + a.shape[1:], tile) for a in arrays] + extra,
            out_specs=pl.BlockSpec((1, quarter, BLOCK, BLOCK), lambda g, w: (g, 0, 0, 0)),
        ),
        compiler_params=pltpu.CompilerParams(vmem_limit_bytes=VMEM_LIMIT),
        cost_estimate=cost(4 * chans * quarter * BLOCK * BLOCK * 128, *arrays),
        name=kernel.__name__,
    )(where, *arrays, *gates)


def prepare_kernel(half, where, factor_ref, out_ref):
    mask = 2 * half * where[0] + half * where[1]
    rows = lax.broadcasted_iota(jnp.int32, (BLOCK, BLOCK), 0)
    columns = lax.broadcasted_iota(jnp.int32, (BLOCK, BLOCK), 1)
    swap = jnp.where(rows == (columns ^ mask), 1.0, 0.0).astype(BF16)
    for i in range(out_ref.shape[0]):
        turned = jnp.dot(swap, factor_ref[0, i].astype(BF16), preferred_element_type=F32)
        out_ref[i] = jnp.dot(
            turned.astype(BF16), swap, preferred_element_type=F32
        ).astype(BF16)


def prepare(where, factor, layer, half, *gates):
    kernel, extra = gated(functools.partial(prepare_kernel, half), 2, gates)
    whole = factor.shape[1] <= half
    block = (1, factor.shape[1] if whole else half) + factor.shape[2:]
    spec = pl.BlockSpec(block, lambda i, w: (layer, 0 if whole else w[1], 0, 0))
    return pl.pallas_call(
        kernel,
        out_shape=jax.ShapeDtypeStruct(block[1:], BF16),
        grid_spec=pltpu.PrefetchScalarGridSpec(
            num_scalar_prefetch=1,
            grid=(1,),
            in_specs=[spec] + extra,
            out_specs=pl.BlockSpec(block[1:], lambda i, w: (0, 0, 0)),
        ),
        compiler_params=pltpu.CompilerParams(vmem_limit_bytes=VMEM_LIMIT),
        cost_estimate=pl.CostEstimate(flops=2**30, bytes_accessed=2**23, transcendentals=0),
        name="prepare",
    )(where, factor, *gates)


def total_kernel(keep_ref, got_ref, out_ref):
    out_ref[...] = (keep_ref[...].astype(F32) + got_ref[...].astype(F32)).astype(BF16)


def total_of(keep, got, *gates):
    kernel, extra = gated(total_kernel, 2, gates)
    spec = pl.BlockSpec((1,) + keep.shape[1:], lambda g: (g, 0, 0, 0))
    return pl.pallas_call(
        kernel,
        out_shape=jax.ShapeDtypeStruct(keep.shape, BF16),
        grid=keep.shape[:1],
        in_specs=[spec, spec] + extra,
        out_specs=spec,
        cost_estimate=pl.CostEstimate(flops=0, bytes_accessed=6 * keep.size, transcendentals=0),
        name="total_of",
    )(keep, got, *gates)


def after(value, *others):
    return lax.optimization_barrier((value,) + others)[0]


def planes(features, cotangent, right_factor, left_factor, mixing):
    blocks = right_factor.shape[1]
    samples = features.shape[1]
    chans, samps = lax.axis_size("chan"), lax.axis_size("samp")
    half, quarter, part = blocks // 2, blocks // 4, samples // chans
    own = chans * half
    chan, own_x, samp = lax.axis_index("chan"), lax.axis_index("bfly"), lax.axis_index("samp")
    row, core = samp // 2, samp % 2
    where = jnp.stack([own_x, core, chan, row]).astype(jnp.int32)

    def over_chan(values, distance):
        return lax.ppermute(values, "chan", [(i, i ^ distance) for i in range(chans)])

    def over_samp(values, distance):
        return lax.ppermute(values, "samp", [(i, i ^ distance) for i in range(samps)])

    def in_plane(values, dx, dc):
        if dx == 0 and dc == 0:
            return values
        route = [(i, i ^ (dx * samps + dc)) for i in range(2 * samps)]
        return lax.ppermute(values, ("bfly", "samp"), route)

    def enter(array, *gates):
        pieces = split(where, array.reshape(blocks, BLOCK, samples), chans, *gates)
        mine, other = pieces[0], over_samp(pieces[1], 1)
        chunks = []
        for core_of in range(2):
            chunk = jnp.zeros((chans, half, BLOCK, part), BF16)
            for distance in range(chans):
                piece = jnp.where(core == core_of, mine[distance], other[distance])
                if distance:
                    piece = over_chan(piece, distance)
                chunk = lax.dynamic_update_index_in_dim(chunk, piece, chan ^ distance, 0)
            chunks.append(chunk.reshape(own, BLOCK, part))
        return pieces, chunks

    def leave_planes(chunks):
        arrived = []
        for chunk in chunks:
            chunk = chunk.reshape(chans, half, BLOCK, part)
            arrived.append([])
            for distance in range(chans):
                piece = lax.dynamic_index_in_dim(chunk, chan ^ distance, 0, keepdims=False)
                arrived[-1].append(over_chan(piece, distance) if distance else piece)
        return arrived

    def leave_chip(arrived, *gates):
        first, second = (jnp.stack(pieces) for pieces in arrived)
        keep = jnp.where(core == 0, first, second)
        got = over_samp(jnp.where(core == 0, second, first), 1)
        return merge(where, jnp.stack([keep, got]), *gates).reshape(blocks * BLOCK, samples)

    def gather_factor(ready):
        return lax.all_gather(ready, "chan", tiled=True)

    def sum_factor(kernel, arrays, *gates):
        send = sum_call(kernel, where, 1, half, arrays, *gates)
        keep = sum_call(kernel, where, 0, half, arrays, send)
        return keep, send, over_samp(send, 2)

    def spread_factor(parts, *gates):
        total = total_of(parts[0], parts[2], *gates)
        return lax.psum_scatter(total, "chan", scatter_dimension=0, tiled=False)

    def finish_factor(total, *gates):
        total = prepare(where, total[None], 0, half, *gates)
        total = lax.all_gather(total, "samp")
        whole = total.reshape(2, 2, quarter, BLOCK, BLOCK)
        return total, jnp.swapaxes(whole, 0, 1).reshape(blocks, BLOCK, BLOCK).astype(F32)

    def swap_pieces(pieces):
        return [in_plane(piece, dx, dc) for piece, (dx, dc) in zip(pieces, HOPS)]

    both = range(2)
    ready = prepare(where, right_factor, 0, half)
    rights_in = [gather_factor(ready), None]
    entered, features_in = enter(features, ready)
    heights = [features_in]
    ready = prepare(where, left_factor, 0, half, entered)
    lefts_in = [gather_factor(ready), None]
    gains = lax.all_gather(after(mixing, ready), ROW_AXES, axis=2, tiled=True)
    gains = gains.reshape(LAYERS, 2, chans, 2, 2, half, BLOCK)
    gains = jnp.where(own_x == 1, gains[:, :, :, ::-1], gains)
    gains = jnp.where(core == 1, gains[:, :, :, :, ::-1], gains)
    gains = gains.reshape(LAYERS, 2, BLOCK, chans, 4, half)
    gains = lax.dynamic_index_in_dim(gains, 2 * own_x + core, 4, keepdims=False)
    gains = gains.reshape(LAYERS, 2, BLOCK, own // TILE, TILE).swapaxes(2, 3)

    mixed_u, mixed_v, act = [[None] * 2 for _ in range(LAYERS)], [[None] * 2 for _ in range(LAYERS)], [None] * 2
    outer, sent = [None] * 2, [None] * 2
    for q in both:
        ins = [("r", heights[0][q]), ("w", rights_in[0])]
        gates = [] if q == 0 else [sent[0][0]]
        sent[q] = rows_call(first_kernel, half, ins, "pppp", 1, *gates)
        mixed_u[0][q] = swap_pieces(sent[q])
    first = sent[:]
    rights_in[1] = gather_factor(prepare(where, right_factor, 1, half, first[0][0]))
    for q in both:
        gates = [first[1][0]] if q == 0 else [sent[0][0]]
        mixed_v[0][q], sent[q] = units_forward(mixed_u[0][q], gains[0], lefts_in[0], half, *gates)
        outer[q] = swap_pieces(sent[q])
    lefts_in[1] = gather_factor(prepare(where, left_factor, 1, half, sent[0][0]))
    _, grad = enter(cotangent, sent[0][0])
    heights.append([None] * 2)
    last = sent[1][0]
    for q in both:
        ins = [("p", p) for p in outer[q]] + [("r", heights[0][q]), ("w", rights_in[1])]
        gates = [last] if q == 0 else [sent[0][0]]
        out = rows_call(middle_kernel, half, ins, "rrpppp", 1, *gates)
        act[q], heights[1][q] = out[:2]
        sent[q] = out[2:]
        mixed_u[1][q] = swap_pieces(out[2:])
    last = sent[1][0]
    for q in both:
        gates = [last] if q == 0 else [sent[0][0]]
        mixed_v[1][q], sent[q] = units_forward(mixed_u[1][q], gains[1], lefts_in[1], half, *gates)
        outer[q] = swap_pieces(sent[q])
    error, final = [None] * 2, [None] * 2
    last = sent[1][0]
    for q in both:
        ins = [("p", p) for p in outer[q]] + [("r", heights[1][q]), ("r", grad[q])]
        gates = [last] if q == 0 else [final[0]]
        out = rows_call(last_kernel, half, ins, "rpppp", 2, *gates)
        final[q] = out[0]
        error[q] = swap_pieces(out[1:])
    out_parts = leave_planes(final)
    mix = [None] * LAYERS
    grad_u = [None] * 2
    for q in both:
        gates = [final[1]] if q == 0 else [sent[0][0]]
        sent[q], mix_q = units_backward(error[q], mixed_u[1][q], gains[1], lefts_in[1], half, *gates)
        mix[1] = mix_q if q == 0 else mix[1] + mix_q
        grad_u[q] = swap_pieces(sent[q])
    left_1 = sum_factor(left_sum_kernel, mixed_v[1] + error[0] + error[1], sent[1][0])
    rows = [None] * 2
    error = [None] * 2
    last = sent[1][0]
    for q in both:
        ins = [("p", p) for p in grad_u[q]]
        ins += [("r", grad[q]), ("w", rights_in[1]), ("r", act[q])]
        gates = [last, left_1[1]] if q == 0 else [sent[0][0]]
        out = rows_call(back_kernel, half, ins, "rrpppp", 1, *gates)
        rows[q], grad[q] = out[:2]
        sent[q] = out[2:]
        error[q] = swap_pieces(out[2:])
    left_1 = spread_factor(left_1, sent[1][0])
    right_1 = sum_factor(right_sum_kernel, heights[1] + rows)
    for q in both:
        gates = [right_1[1], *out_parts[0][1:]] if q == 0 else [sent[0][0]]
        sent[q], mix_q = units_backward(error[q], mixed_u[0][q], gains[0], lefts_in[0], half, *gates)
        mix[0] = mix_q if q == 0 else mix[0] + mix_q
        grad_u[q] = swap_pieces(sent[q])
    right_1 = spread_factor(right_1, sent[1][0])
    left_0 = sum_factor(left_sum_kernel, mixed_v[0] + error[0] + error[1], sent[1][0])
    left_1 = finish_factor(left_1, sent[1][0])
    rows = [None] * 2
    for q in both:
        ins = [("p", p) for p in grad_u[q]] + [("r", grad[q]), ("w", rights_in[0])]
        gates = [left_0[1], sent[1][0], *out_parts[1][1:]] if q == 0 else [grad[0], left_1[0]]
        rows[q], grad[q] = rows_call(final_kernel, half, ins, "rr", 0, *gates)
    in_parts = leave_planes(grad)
    output = leave_chip(out_parts, rows[0])
    left_0 = spread_factor(left_0, rows[0])
    right_0 = sum_factor(right_sum_kernel, heights[0] + rows)
    right_1 = finish_factor(right_1, rows[0])
    left_0 = finish_factor(left_0, right_0[1])
    right_0 = finish_factor(spread_factor(right_0, right_1[0], *in_parts[0][1:]), left_0[0], output)
    feature_grad = leave_chip(in_parts)
    mix = jnp.stack(mix).swapaxes(2, 3).reshape(LAYERS, 2, chans, 2, 2, half, own)
    mix = jnp.where(own_x == 1, mix[:, :, :, ::-1], mix)
    mix = jnp.where(core == 1, mix[:, :, :, :, ::-1], mix)
    mix = lax.psum_scatter(mix, "chan", scatter_dimension=2, tiled=False)
    mix = lax.all_gather(mix, ("bfly", "samp")).reshape((2, 2, 2) + mix.shape)
    mix = mix[:, 0] + mix[:, 1]
    mix = lax.dynamic_index_in_dim(mix, own_x, 4, keepdims=False)
    mix = mix.reshape(2, 2, LAYERS, 2, blocks, chans, half)
    mix = mix.transpose(2, 3, 4, 5, 0, 1, 6).reshape(LAYERS, 2, blocks, BLOCK)
    grad_right_0, grad_right_1 = right_0[1], right_1[1]
    grad_left_0, grad_left_1 = left_0[1], left_1[1]
    rights = jnp.stack([grad_right_0, grad_right_1])
    return (output, feature_grad, rights, jnp.stack([grad_left_0, grad_left_1]), mix)


def solution(mesh):
    sizes = dict(mesh.shape)
    fits = sizes["chan"] == 4 and sizes["bfly"] == 2 and sizes["samp"] == 4
    local = planes if fits else stationary
    rows = P(ROW_AXES, "samp")
    factors = P(None, ROW_AXES, None, None)
    gains = P(None, None, ROW_AXES, None)
    return jax.shard_map(
        local,
        mesh=mesh,
        in_specs=(rows, rows, factors, factors, gains),
        out_specs=(rows, rows, factors, factors, gains),
        check_vma=False,
    )
```

```python
import functools

import jax
import jax.numpy as jnp
from jax import lax
from jax.experimental import pallas as pl
from jax.experimental.pallas import tpu as pltpu
from jax.sharding import PartitionSpec as P

BLOCK = 256
LAYERS = 2
ROW_AXES = ("chan", "bfly")
F32 = jnp.float32
BF16 = jnp.bfloat16


def to_columns(values):
    return lax.all_to_all(values, ROW_AXES, split_axis=1, concat_axis=0, tiled=True)


def to_rows(values):
    return lax.all_to_all(values, ROW_AXES, split_axis=0, concat_axis=1, tiled=True)


def stationary(features, cotangent, right_factor, left_factor, mixing):
    blocks = right_factor.shape[1]
    samples = features.shape[1]
    pairs = lax.axis_size("bfly")

    def flip(values):
        grouped = values.reshape((-1, pairs // 2, 2, blocks) + values.shape[1:])
        return grouped[:, :, ::-1].reshape(values.shape)

    left_bf = left_factor.astype(jnp.bfloat16)
    gains = lax.all_to_all(mixing, ROW_AXES, split_axis=3, concat_axis=2, tiled=True)
    height = features.reshape(blocks, BLOCK, samples)
    saved = []
    for layer in range(LAYERS):
        self_gain = gains[layer, 0][:, :, None]
        cross_gain = gains[layer, 1][:, :, None]
        mixed_u = to_columns(
            jnp.einsum(
                "bis,bij->bjs", height, right_factor[layer], preferred_element_type=jnp.float32
            ).astype(jnp.bfloat16)
        )
        mixed_v = (
            self_gain * mixed_u.astype(jnp.float32) + cross_gain * flip(mixed_u).astype(jnp.float32)
        ).astype(jnp.bfloat16)
        outer = jnp.einsum(
            "bjs,jbk->kjs", mixed_v, left_bf[layer], preferred_element_type=jnp.float32
        ).astype(jnp.bfloat16)
        activation = to_rows(outer)
        saved.append((height, mixed_u, mixed_v, activation))
        height = (height.astype(jnp.float32) + jax.nn.silu(activation.astype(jnp.float32))).astype(
            jnp.bfloat16
        )
    output = height.reshape(blocks * BLOCK, samples)
    grad = cotangent.reshape(blocks, BLOCK, samples)
    rights = [None] * LAYERS
    lefts = [None] * LAYERS
    mixes = [None] * LAYERS
    for layer in reversed(range(LAYERS)):
        height_in, mixed_u, mixed_v, activation = saved[layer]
        self_gain = gains[layer, 0][:, :, None]
        cross_gain = gains[layer, 1][:, :, None]
        before = activation.astype(jnp.float32)
        logistic = jax.nn.sigmoid(before)
        error = (grad.astype(jnp.float32) * logistic * (1.0 + before * (1.0 - logistic))).astype(
            jnp.bfloat16
        )
        error_cols = to_columns(error)
        grad_v = jnp.einsum(
            "jbk,kjs->bjs", left_bf[layer], error_cols, preferred_element_type=jnp.float32
        ).astype(jnp.bfloat16)
        grad_vf = grad_v.astype(jnp.float32)
        carried = (cross_gain * grad_vf).astype(jnp.bfloat16)
        grad_u = to_rows(
            (self_gain * grad_vf + flip(carried).astype(jnp.float32)).astype(jnp.bfloat16)
        )
        lefts[layer] = jnp.einsum(
            "bjs,kjs->jbk", mixed_v, error_cols, preferred_element_type=jnp.float32
        )
        mixes[layer] = jnp.stack(
            [
                jnp.sum(grad_vf * mixed_u.astype(jnp.float32), axis=2),
                jnp.sum(grad_vf * flip(mixed_u).astype(jnp.float32), axis=2),
            ]
        )
        rights[layer] = jnp.einsum(
            "bis,bjs->bij", height_in, grad_u, preferred_element_type=jnp.float32
        )
        back_term = jnp.einsum(
            "bij,bjs->bis", right_factor[layer], grad_u, preferred_element_type=jnp.float32
        )
        grad = (grad.astype(jnp.float32) + back_term).astype(jnp.bfloat16)
    all_mix = lax.psum(jnp.stack(mixes), "samp")
    all_mix = lax.all_to_all(all_mix, ROW_AXES, split_axis=2, concat_axis=3, tiled=True)
    all_right = jnp.stack(
        [lax.psum(part.astype(jnp.bfloat16), "samp").astype(jnp.float32) for part in rights]
    )
    all_left = jnp.stack(
        [lax.psum(part.astype(jnp.bfloat16), "samp").astype(jnp.float32) for part in lefts]
    )
    return (output, grad.reshape(blocks * BLOCK, samples), all_right, all_left, all_mix)


def gated(kernel, count, gates):
    def run(*refs):
        kernel(*refs[:count], *refs[count + len(gates) :])

    return run, [pl.BlockSpec(memory_space=pl.ANY)] * len(gates)


def shuffle_rows(where, source, target, half):
    own_x, own_core = where[0], where[1] ^ pl.program_id(0)
    for group in range(BLOCK // (4 * half)):
        for dx in range(2):
            for dc in range(2):
                start = 4 * half * group + 2 * half * (own_x ^ dx) + half * (own_core ^ dc)
                rows = pl.ds(pl.multiple_of(start, half), half)
                here = pl.ds(4 * half * group + 2 * half * dx + half * dc, half)
                yield rows, here


def split_kernel(where, array_ref, pieces_ref):
    half = array_ref.shape[0]
    for rows, here in shuffle_rows(where, array_ref, pieces_ref, half):
        pieces_ref[0, 0, :, here, :] = array_ref[:, rows, :]


def merge_kernel(where, pieces_ref, array_ref):
    half = array_ref.shape[0]
    for rows, here in shuffle_rows(where, array_ref, pieces_ref, half):
        array_ref[:, rows, :] = pieces_ref[0, 0, :, here, :]


def split(where, array, chans, *gates):
    blocks, units, samples = array.shape
    half, part = blocks // 2, samples // chans
    kernel, extra = gated(split_kernel, 2, gates)
    return pl.pallas_call(
        kernel,
        out_shape=jax.ShapeDtypeStruct((2, chans, half, units, part), array.dtype),
        grid_spec=pltpu.PrefetchScalarGridSpec(
            num_scalar_prefetch=1,
            grid=(2, chans),
            in_specs=[pl.BlockSpec((half, units, part), lambda e, d, w: (w[1] ^ e, 0, w[2] ^ d))]
            + extra,
            out_specs=pl.BlockSpec((1, 1, half, units, part), lambda e, d, w: (e, d, 0, 0, 0)),
        ),
        cost_estimate=pl.CostEstimate(flops=0, bytes_accessed=4 * array.size, transcendentals=0),
        name="split",
    )(where, array, *gates)


def merge(where, pieces, *gates):
    _, chans, half, units, part = pieces.shape
    kernel, extra = gated(merge_kernel, 2, gates)
    return pl.pallas_call(
        kernel,
        out_shape=jax.ShapeDtypeStruct((2 * half, units, chans * part), pieces.dtype),
        grid_spec=pltpu.PrefetchScalarGridSpec(
            num_scalar_prefetch=1,
            grid=(2, chans),
            in_specs=[pl.BlockSpec((1, 1, half, units, part), lambda e, d, w: (e, d, 0, 0, 0))]
            + extra,
            out_specs=pl.BlockSpec((half, units, part), lambda e, d, w: (w[1] ^ e, 0, w[2] ^ d)),
        ),
        cost_estimate=pl.CostEstimate(flops=0, bytes_accessed=4 * pieces.size, transcendentals=0),
        name="merge",
    )(where, pieces, *gates)


HOPS = ((0, 0), (0, 1), (1, 0), (1, 1))
VMEM_LIMIT = 48 * 1024 * 1024


def cost(flops, *arrays):
    size = sum(a.size * a.dtype.itemsize for a in arrays)
    return pl.CostEstimate(flops=int(flops), bytes_accessed=int(size), transcendentals=0)


def join(pieces, index, half, swap=0):
    groups = pieces[0].shape[1] // half
    return jnp.concatenate(
        [
            pieces[2 * (dx ^ swap) + dc][index, half * g : half * g + half, :]
            for g in range(groups)
            for dx, dc in HOPS
        ],
        axis=0,
    )


def deal(pieces, index, half, value):
    groups = pieces[0].shape[1] // half
    for g in range(groups):
        for hop in range(4):
            start = half * (4 * g + hop)
            pieces[hop][index, half * g : half * g + half, :] = value[start : start + half, :]


def swap_dx(value, half):
    step = 2 * half
    return jnp.concatenate(
        [value[step * (i ^ 1) : step * (i ^ 1) + step, :] for i in range(value.shape[0] // step)],
        axis=0,
    )


def units_forward_kernel(half, *refs):
    u, (gain_ref, left_ref), v_ref, t = refs[:4], refs[4:6], refs[6], refs[7:]
    for i in range(left_ref.shape[0]):
        mine = join(u, i, half).astype(F32)
        partner = join(u, i, half, 1).astype(F32)
        v = (gain_ref[0, 0, :, i : i + 1] * mine + gain_ref[1, 0, :, i : i + 1] * partner).astype(BF16)
        v_ref[i] = v
        out = lax.dot_general(left_ref[i], v, (((0,), (0,)), ((), ())), preferred_element_type=F32)
        deal(t, i, half, out.astype(BF16))


def units_backward_kernel(half, *refs):
    e, u, (gain_ref, left_ref) = refs[:4], refs[4:8], refs[8:10]
    du, mix_ref = refs[10:14], refs[14]
    for i in range(left_ref.shape[0]):
        dv = jnp.dot(left_ref[i], join(e, i, half), preferred_element_type=F32)
        dv = dv.astype(BF16).astype(F32)
        mine = join(u, i, half).astype(F32)
        mix_ref[0, 0, :, i : i + 1] = jnp.sum(dv * mine, axis=1, keepdims=True)
        mix_ref[1, 0, :, i : i + 1] = jnp.sum(dv * swap_dx(mine, half), axis=1, keepdims=True)
        carried = (gain_ref[1, 0, :, i : i + 1] * dv).astype(BF16).astype(F32)
        value = gain_ref[0, 0, :, i : i + 1] * dv + swap_dx(carried, half)
        deal(du, i, half, value.astype(BF16))


TILE = 8


def units_forward(u, gain, left, half, *gates):
    own, part = u[0].shape[0], u[0].shape[2]
    piece = pl.BlockSpec((TILE, own, part), lambda i: (i, 0, 0))
    full = pl.BlockSpec((TILE, BLOCK, part), lambda i: (i, 0, 0))
    gains = pl.BlockSpec((2, 1, BLOCK, TILE), lambda i: (0, i, 0, 0))
    weight = pl.BlockSpec((TILE, BLOCK, BLOCK), lambda i: (i, 0, 0))
    shape = jax.ShapeDtypeStruct((own, own, part), BF16)
    v_shape = jax.ShapeDtypeStruct((own, BLOCK, part), BF16)
    kernel, extra = gated(functools.partial(units_forward_kernel, half), 6, gates)
    out = pl.pallas_call(
        kernel,
        grid=(own // TILE,),
        in_specs=[piece] * 4 + [gains, weight] + extra,
        out_specs=[full] + [piece] * 4,
        out_shape=[v_shape] + [shape] * 4,
        compiler_params=pltpu.CompilerParams(vmem_limit_bytes=VMEM_LIMIT),
        cost_estimate=cost(2 * own * BLOCK * BLOCK * part, left, v_shape, *u, *u),
        name="units_forward",
    )(*u, gain, left, *gates)
    return out[0], out[1:]


def units_backward(e, u, gain, left, half, *gates):
    own, part = u[0].shape[0], u[0].shape[2]
    piece = pl.BlockSpec((TILE, own, part), lambda i: (i, 0, 0))
    gains = pl.BlockSpec((2, 1, BLOCK, TILE), lambda i: (0, i, 0, 0))
    weight = pl.BlockSpec((TILE, BLOCK, BLOCK), lambda i: (i, 0, 0))
    shape = jax.ShapeDtypeStruct((own, own, part), BF16)
    kernel, extra = gated(functools.partial(units_backward_kernel, half), 10, gates)
    out = pl.pallas_call(
        kernel,
        grid=(own // TILE,),
        in_specs=[piece] * 8 + [gains, weight] + extra,
        out_specs=[piece] * 4 + [gains],
        out_shape=[shape] * 4 + [jax.ShapeDtypeStruct(gain.shape, F32)],
        compiler_params=pltpu.CompilerParams(vmem_limit_bytes=VMEM_LIMIT),
        cost_estimate=cost(2 * own * BLOCK * BLOCK * part, left, *u, *u, *u),
        name="units_backward",
    )(*e, *u, gain, left, *gates)
    return out[:4], out[4]


def gather_rows(pieces, scratch, half):
    for hop in range(4):
        turned = jnp.swapaxes(pieces[hop][...], 0, 1)
        for g in range(pieces[hop].shape[0] // half):
            start = half * (4 * g + hop)
            scratch[:, start : start + half, :] = turned[:, half * g : half * g + half, :]


def scatter_rows(scratch, pieces, half):
    for hop in range(4):
        for g in range(pieces[hop].shape[0] // half):
            start = half * (4 * g + hop)
            pieces[hop][half * g : half * g + half] = jnp.swapaxes(
                scratch[:, start : start + half, :], 0, 1
            )


def error_of(grad, before):
    logistic = jax.nn.sigmoid(before)
    return (grad * logistic * (1.0 + before * (1.0 - logistic))).astype(BF16)


def first_kernel(half, h_ref, right_ref, *refs):
    u, scratch = refs[:4], refs[4]
    for b in range(h_ref.shape[0]):
        out = lax.dot_general(
            right_ref[b], h_ref[b], (((0,), (0,)), ((), ())), preferred_element_type=F32
        )
        scratch[b] = out.astype(BF16)
    scatter_rows(scratch, u, half)


def middle_kernel(half, *refs):
    t, (h_ref, right_ref), (act_ref, next_ref), u = refs[:4], refs[4:6], refs[6:8], refs[8:12]
    scratch = refs[12]
    gather_rows(t, act_ref, half)
    for b in range(h_ref.shape[0]):
        height = (h_ref[b].astype(F32) + jax.nn.silu(act_ref[b].astype(F32))).astype(BF16)
        next_ref[b] = height
        out = lax.dot_general(
            right_ref[b], height, (((0,), (0,)), ((), ())), preferred_element_type=F32
        )
        scratch[b] = out.astype(BF16)
    scatter_rows(scratch, u, half)


def last_kernel(half, *refs):
    t, (h_ref, g_ref), next_ref, e = refs[:4], refs[4:6], refs[6], refs[7:11]
    act, scratch = refs[11:13]
    gather_rows(t, act, half)
    for b in range(h_ref.shape[0]):
        before = act[b].astype(F32)
        next_ref[b] = (h_ref[b].astype(F32) + jax.nn.silu(before)).astype(BF16)
        scratch[b] = error_of(g_ref[b].astype(F32), before)
    scatter_rows(scratch, e, half)


def back_kernel(half, *refs):
    du, (g_ref, right_ref, act_ref), (rows_ref, next_ref), e = refs[:4], refs[4:7], refs[7:9], refs[9:13]
    scratch = refs[13]
    gather_rows(du, rows_ref, half)
    for b in range(g_ref.shape[0]):
        term = jnp.dot(right_ref[b], rows_ref[b], preferred_element_type=F32)
        grad = (g_ref[b].astype(F32) + term).astype(BF16)
        next_ref[b] = grad
        scratch[b] = error_of(grad.astype(F32), act_ref[b].astype(F32))
    scatter_rows(scratch, e, half)


def final_kernel(half, *refs):
    du, (g_ref, right_ref), (rows_ref, next_ref) = refs[:4], refs[4:6], refs[6:8]
    gather_rows(du, rows_ref, half)
    for b in range(g_ref.shape[0]):
        term = jnp.dot(right_ref[b], rows_ref[b], preferred_element_type=F32)
        next_ref[b] = (g_ref[b].astype(F32) + term).astype(BF16)


def rows_call(kernel, half, ins, outs, scratches, *gates):
    own, part = 4 * half, 128
    rows = 16
    specs = {
        "p": pl.BlockSpec((own, rows, part), lambda i: (0, i, 0)),
        "r": pl.BlockSpec((rows, BLOCK, part), lambda i: (i, 0, 0)),
        "w": pl.BlockSpec((rows, BLOCK, BLOCK), lambda i: (i, 0, 0)),
    }
    shapes = {"p": (own, own, part), "r": (own, BLOCK, part)}
    out_shape = [jax.ShapeDtypeStruct(shapes[kind], BF16) for kind in outs]
    kinds = [kind for kind, _ in ins]
    arrays = [array for _, array in ins]
    flops = 2 * own * BLOCK * BLOCK * part if "w" in kinds else 0
    run, extra = gated(functools.partial(kernel, half), len(ins), gates)
    return pl.pallas_call(
        run,
        grid=(own // rows,),
        in_specs=[specs[kind] for kind in kinds] + extra,
        out_specs=[specs[kind] for kind in outs],
        out_shape=out_shape,
        scratch_shapes=[pltpu.VMEM((rows, BLOCK, part), BF16)] * scratches,
        compiler_params=pltpu.CompilerParams(vmem_limit_bytes=VMEM_LIMIT),
        cost_estimate=cost(flops, *arrays, *out_shape),
        name=kernel.__name__,
    )(*arrays, *gates)


def left_sum_kernel(half, where, *refs):
    v, e, out_ref = refs[:2], (refs[2:6], refs[6:10]), refs[10]
    for i in range(out_ref.shape[1]):
        total = 0.0
        for q in range(2):
            total += lax.dot_general(
                v[q][i], join(e[q], i, half), (((1,), (1,)), ((), ())), preferred_element_type=F32
            )
        out_ref[0, i] = total.astype(BF16)


def right_sum_kernel(half, where, *refs):
    h, du, out_ref = refs[:2], refs[2:4], refs[4]
    for i in range(out_ref.shape[1]):
        total = 0.0
        for q in range(2):
            total += lax.dot_general(
                h[q][i], du[q][i], (((1,), (1,)), ((), ())), preferred_element_type=F32
            )
        out_ref[0, i] = total.astype(BF16)


def sum_call(kernel, where, other, half, arrays, *gates):
    quarter = half // 2
    chans = arrays[0].shape[0] // half
    out_shape = jax.ShapeDtypeStruct((chans, quarter, BLOCK, BLOCK), BF16)

    def tile(g, w):
        return (2 * g + (w[3] ^ other), 0, 0)

    run, extra = gated(functools.partial(kernel, half), 1 + len(arrays), gates)
    return pl.pallas_call(
        run,
        out_shape=out_shape,
        grid_spec=pltpu.PrefetchScalarGridSpec(
            num_scalar_prefetch=1,
            grid=(chans,),
            in_specs=[pl.BlockSpec((quarter,) + a.shape[1:], tile) for a in arrays] + extra,
            out_specs=pl.BlockSpec((1, quarter, BLOCK, BLOCK), lambda g, w: (g, 0, 0, 0)),
        ),
        compiler_params=pltpu.CompilerParams(vmem_limit_bytes=VMEM_LIMIT),
        cost_estimate=cost(4 * chans * quarter * BLOCK * BLOCK * 128, *arrays),
        name=kernel.__name__,
    )(where, *arrays, *gates)


def weave_kernel(where, mine_ref, other_ref, out_ref):
    @pl.when(pl.program_id(1) == where[3])
    def _():
        out_ref[0, 0] = mine_ref[0]

    @pl.when(pl.program_id(1) != where[3])
    def _():
        out_ref[0, 0] = other_ref[0]


def weave(where, mine, other, *gates):
    block = (1,) + mine.shape[1:]
    spec = pl.BlockSpec(block, lambda g, y, w: (g, 0, 0, 0))
    kernel, extra = gated(weave_kernel, 3, gates)
    return pl.pallas_call(
        kernel,
        out_shape=jax.ShapeDtypeStruct(mine.shape[:1] + (2,) + mine.shape[1:], mine.dtype),
        grid_spec=pltpu.PrefetchScalarGridSpec(
            num_scalar_prefetch=1,
            grid=(mine.shape[0], 2),
            in_specs=[spec, spec] + extra,
            out_specs=pl.BlockSpec((1,) + block, lambda g, y, w: (g, y, 0, 0, 0)),
        ),
        cost_estimate=pl.CostEstimate(flops=0, bytes_accessed=8 * mine.size, transcendentals=0),
        name="weave",
    )(where, mine, other, *gates)


def prepare_kernel(half, where, factor_ref, out_ref):
    mask = 2 * half * where[0] + half * where[1]
    rows = lax.broadcasted_iota(jnp.int32, (BLOCK, BLOCK), 0)
    columns = lax.broadcasted_iota(jnp.int32, (BLOCK, BLOCK), 1)
    swap = jnp.where(rows == (columns ^ mask), 1.0, 0.0).astype(BF16)
    for i in range(out_ref.shape[0]):
        turned = jnp.dot(swap, factor_ref[0, i].astype(BF16), preferred_element_type=F32)
        out_ref[i] = jnp.dot(
            turned.astype(BF16), swap, preferred_element_type=F32
        ).astype(BF16)


def prepare(where, factor, layer, half, *gates):
    kernel, extra = gated(functools.partial(prepare_kernel, half), 2, gates)
    block = (1, half // 2) + factor.shape[2:]
    whole = factor.shape[1] == block[1]
    spec = pl.BlockSpec(block, lambda i, w: (layer, 0 if whole else 2 * w[1] + w[3], 0, 0))
    return pl.pallas_call(
        kernel,
        out_shape=jax.ShapeDtypeStruct(block[1:], BF16),
        grid_spec=pltpu.PrefetchScalarGridSpec(
            num_scalar_prefetch=1,
            grid=(1,),
            in_specs=[spec] + extra,
            out_specs=pl.BlockSpec(block[1:], lambda i, w: (0, 0, 0)),
        ),
        cost_estimate=pl.CostEstimate(flops=2**29, bytes_accessed=2**22, transcendentals=0),
        name="prepare",
    )(where, factor, *gates)


def copy_kernel(array_ref, out_ref):
    out_ref[...] = array_ref[...]


def copy_after(array, *gates):
    kernel, extra = gated(copy_kernel, 1, gates)
    spec = pl.BlockSpec((1,) + array.shape[1:], lambda g: (g, 0, 0, 0))
    return pl.pallas_call(
        kernel,
        out_shape=jax.ShapeDtypeStruct(array.shape, BF16),
        grid=array.shape[:1],
        in_specs=[spec] + extra,
        out_specs=spec,
        cost_estimate=pl.CostEstimate(flops=0, bytes_accessed=4 * array.size, transcendentals=0),
        name="copy_after",
    )(array, *gates)


def total_kernel(keep_ref, got_ref, out_ref):
    out_ref[...] = (keep_ref[...].astype(F32) + got_ref[...].astype(F32)).astype(BF16)


def total_of(keep, got, *gates):
    kernel, extra = gated(total_kernel, 2, gates)
    spec = pl.BlockSpec((1,) + keep.shape[1:], lambda g: (g, 0, 0, 0))
    return pl.pallas_call(
        kernel,
        out_shape=jax.ShapeDtypeStruct(keep.shape, BF16),
        grid=keep.shape[:1],
        in_specs=[spec, spec] + extra,
        out_specs=spec,
        cost_estimate=pl.CostEstimate(flops=0, bytes_accessed=6 * keep.size, transcendentals=0),
        name="total_of",
    )(keep, got, *gates)


def after(value, *others):
    return lax.optimization_barrier((value,) + others)[0]


def planes(features, cotangent, right_factor, left_factor, mixing):
    blocks = right_factor.shape[1]
    samples = features.shape[1]
    chans, samps = lax.axis_size("chan"), lax.axis_size("samp")
    half, quarter, part = blocks // 2, blocks // 4, samples // chans
    own = chans * half
    chan, own_x, samp = lax.axis_index("chan"), lax.axis_index("bfly"), lax.axis_index("samp")
    row, core = samp // 2, samp % 2
    where = jnp.stack([own_x, core, chan, row]).astype(jnp.int32)

    def over_chan(values, distance):
        return lax.ppermute(values, "chan", [(i, i ^ distance) for i in range(chans)])

    def over_samp(values, distance):
        return lax.ppermute(values, "samp", [(i, i ^ distance) for i in range(samps)])

    def in_plane(values, dx, dc):
        if dx == 0 and dc == 0:
            return values
        route = [(i, i ^ (dx * samps + dc)) for i in range(2 * samps)]
        return lax.ppermute(values, ("bfly", "samp"), route)

    def enter(array, *gates):
        pieces = split(where, array.reshape(blocks, BLOCK, samples), chans, *gates)
        mine, other = pieces[0], over_samp(pieces[1], 1)
        chunks, arrived = [], []
        for core_of in range(2):
            chunk = jnp.zeros((chans, half, BLOCK, part), BF16)
            for distance in range(chans):
                piece = jnp.where(core == core_of, mine[distance], other[distance])
                if distance:
                    piece = over_chan(piece, distance)
                    arrived.append(piece)
                chunk = lax.dynamic_update_index_in_dim(chunk, piece, chan ^ distance, 0)
            chunks.append(chunk.reshape(own, BLOCK, part))
        return pieces, chunks, arrived[0]

    def leave_planes(chunks):
        arrived = []
        for chunk in chunks:
            chunk = chunk.reshape(chans, half, BLOCK, part)
            arrived.append([])
            for distance in range(chans):
                piece = lax.dynamic_index_in_dim(chunk, chan ^ distance, 0, keepdims=False)
                arrived[-1].append(over_chan(piece, distance) if distance else piece)
        return arrived

    def leave_chip(arrived, *gates):
        first, second = (jnp.stack(pieces) for pieces in arrived)
        keep = jnp.where(core == 0, first, second)
        got = over_samp(jnp.where(core == 0, second, first), 1)
        return merge(where, jnp.stack([keep, got]), *gates).reshape(blocks * BLOCK, samples)

    def gather_row(mine, *gates):
        return weave(where, mine, over_samp(mine, 2), *gates).reshape(own, BLOCK, BLOCK)

    def sum_factor(kernel, arrays, *gates):
        send = sum_call(kernel, where, 1, half, arrays, *gates)
        keep = sum_call(kernel, where, 0, half, arrays, send)
        return keep, send, over_samp(send, 2)

    def spread_factor(parts, *gates):
        total = total_of(parts[0], parts[2], *gates)
        return lax.psum_scatter(total, "chan", scatter_dimension=0, tiled=False)

    def finish_factor(total, *gates):
        total = prepare(where, total[None], 0, half, *gates)
        total = lax.all_gather(total, "samp")
        whole = total.reshape(2, 2, quarter, BLOCK, BLOCK)
        return total, jnp.swapaxes(whole, 0, 1).reshape(blocks, BLOCK, BLOCK).astype(F32)

    def swap_pieces(pieces):
        return [in_plane(piece, dx, dc) for piece, (dx, dc) in zip(pieces, HOPS)]

    both = range(2)
    ready = prepare(where, right_factor, 0, half)
    right_mine = lax.all_gather(ready, "chan")
    entered, features_in, arrival = enter(features, ready)
    heights = [features_in]
    ready = prepare(where, left_factor, 0, half, entered)
    left_mine = lax.all_gather(ready, "chan")
    rights_in = [gather_row(copy_after(right_mine, arrival)), None]
    gains = lax.all_gather(after(mixing, ready), ROW_AXES, axis=2, tiled=True)
    gains = gains.reshape(LAYERS, 2, chans, 2, 2, half, BLOCK)
    gains = jnp.where(own_x == 1, gains[:, :, :, ::-1], gains)
    gains = jnp.where(core == 1, gains[:, :, :, :, ::-1], gains)
    gains = gains.reshape(LAYERS, 2, BLOCK, chans, 4, half)
    gains = lax.dynamic_index_in_dim(gains, 2 * own_x + core, 4, keepdims=False)
    gains = gains.reshape(LAYERS, 2, BLOCK, own // TILE, TILE).swapaxes(2, 3)

    mixed_u, mixed_v, act = [[None] * 2 for _ in range(LAYERS)], [[None] * 2 for _ in range(LAYERS)], [None] * 2
    outer, sent = [None] * 2, [None] * 2
    for q in both:
        ins = [("r", heights[0][q]), ("w", rights_in[0])]
        gates = [] if q == 0 else [sent[0][0], *mixed_u[0][0][1:]]
        sent[q] = rows_call(first_kernel, half, ins, "pppp", 1, *gates)
        mixed_u[0][q] = swap_pieces(sent[q])
    first = sent[:]
    lefts_in = [gather_row(left_mine, first[0][0]), None]
    right_mine = lax.all_gather(prepare(where, right_factor, 1, half, first[0][0]), "chan")
    left_mine = lax.all_gather(prepare(where, left_factor, 1, half, first[1][0]), "chan")
    for q in both:
        gates = [first[1][0]] if q == 0 else [sent[0][0]]
        mixed_v[0][q], sent[q] = units_forward(mixed_u[0][q], gains[0], lefts_in[0], half, *gates)
        outer[q] = swap_pieces(sent[q])
    rights_in[1] = gather_row(right_mine, sent[0][0])
    _, grad, _ = enter(cotangent, sent[0][0])
    heights.append([None] * 2)
    last = sent[1][0]
    for q in both:
        ins = [("p", p) for p in outer[q]] + [("r", heights[0][q]), ("w", rights_in[1])]
        gates = [last] if q == 0 else [sent[0][0]]
        out = rows_call(middle_kernel, half, ins, "rrpppp", 1, *gates)
        act[q], heights[1][q] = out[:2]
        sent[q] = out[2:]
        mixed_u[1][q] = swap_pieces(out[2:])
    lefts_in[1] = gather_row(left_mine, sent[0][0])
    last = sent[1][0]
    for q in both:
        gates = [last] if q == 0 else [sent[0][0]]
        mixed_v[1][q], sent[q] = units_forward(mixed_u[1][q], gains[1], lefts_in[1], half, *gates)
        outer[q] = swap_pieces(sent[q])
    error, final = [None] * 2, [None] * 2
    last = sent[1][0]
    for q in both:
        ins = [("p", p) for p in outer[q]] + [("r", heights[1][q]), ("r", grad[q])]
        gates = [last] if q == 0 else [final[0]]
        out = rows_call(last_kernel, half, ins, "rpppp", 2, *gates)
        final[q] = out[0]
        error[q] = swap_pieces(out[1:])
    out_parts = leave_planes(final)
    mix = [None] * LAYERS
    grad_u = [None] * 2
    for q in both:
        gates = [final[1]] if q == 0 else [sent[0][0], out_parts[0][1]]
        sent[q], mix_q = units_backward(error[q], mixed_u[1][q], gains[1], lefts_in[1], half, *gates)
        mix[1] = mix_q if q == 0 else mix[1] + mix_q
        grad_u[q] = swap_pieces(sent[q])
    left_1 = sum_factor(left_sum_kernel, mixed_v[1] + error[0] + error[1], sent[1][0])
    rows = [None] * 2
    error = [None] * 2
    last = sent[1][0]
    for q in both:
        ins = [("p", p) for p in grad_u[q]]
        ins += [("r", grad[q]), ("w", rights_in[1]), ("r", act[q])]
        gates = [last, left_1[1], out_parts[0][2]] if q == 0 else [sent[0][0], out_parts[0][3]]
        out = rows_call(back_kernel, half, ins, "rrpppp", 1, *gates)
        rows[q], grad[q] = out[:2]
        sent[q] = out[2:]
        error[q] = swap_pieces(out[2:])
    left_1 = spread_factor(left_1, sent[1][0])
    right_1 = sum_factor(right_sum_kernel, heights[1] + rows)
    for q in both:
        gates = [right_1[1], out_parts[1][1]] if q == 0 else [sent[0][0], out_parts[1][2]]
        sent[q], mix_q = units_backward(error[q], mixed_u[0][q], gains[0], lefts_in[0], half, *gates)
        mix[0] = mix_q if q == 0 else mix[0] + mix_q
        grad_u[q] = swap_pieces(sent[q])
    right_1 = spread_factor(right_1, sent[1][0])
    left_0 = sum_factor(left_sum_kernel, mixed_v[0] + error[0] + error[1], sent[1][0])
    left_1 = finish_factor(left_1, sent[1][0])
    rows = [None] * 2
    for q in both:
        ins = [("p", p) for p in grad_u[q]] + [("r", grad[q]), ("w", rights_in[0])]
        gates = [left_0[1], sent[1][0], out_parts[1][3]] if q == 0 else [grad[0], left_1[0]]
        rows[q], grad[q] = rows_call(final_kernel, half, ins, "rr", 0, *gates)
    in_parts = leave_planes(grad)
    output = leave_chip(out_parts, rows[0])
    left_0 = spread_factor(left_0, rows[0])
    right_0 = sum_factor(right_sum_kernel, heights[0] + rows)
    right_1 = finish_factor(right_1, rows[0])
    left_0 = finish_factor(left_0, right_0[1])
    right_0 = spread_factor(right_0, right_1[0], *in_parts[0][1:], *in_parts[1][1:])
    right_0 = finish_factor(right_0, left_0[0], output)
    feature_grad = leave_chip(in_parts)
    mix = jnp.stack(mix).swapaxes(2, 3).reshape(LAYERS, 2, chans, 2, 2, half, own)
    mix = jnp.where(own_x == 1, mix[:, :, :, ::-1], mix)
    mix = jnp.where(core == 1, mix[:, :, :, :, ::-1], mix)
    mix = lax.psum_scatter(mix, "chan", scatter_dimension=2, tiled=False)
    mix = lax.all_gather(mix, ("bfly", "samp")).reshape((2, 2, 2) + mix.shape)
    mix = mix[:, 0] + mix[:, 1]
    mix = lax.dynamic_index_in_dim(mix, own_x, 4, keepdims=False)
    mix = mix.reshape(2, 2, LAYERS, 2, blocks, chans, half)
    mix = mix.transpose(2, 3, 4, 5, 0, 1, 6).reshape(LAYERS, 2, blocks, BLOCK)
    grad_right_0, grad_right_1 = right_0[1], right_1[1]
    grad_left_0, grad_left_1 = left_0[1], left_1[1]
    rights = jnp.stack([grad_right_0, grad_right_1])
    return (output, feature_grad, rights, jnp.stack([grad_left_0, grad_left_1]), mix)


def solution(mesh):
    sizes = dict(mesh.shape)
    fits = sizes["chan"] == 4 and sizes["bfly"] == 2 and sizes["samp"] == 4
    local = planes if fits else stationary
    rows = P(ROW_AXES, "samp")
    factors = P(None, ROW_AXES, None, None)
    gains = P(None, None, ROW_AXES, None)
    return jax.shard_map(
        local,
        mesh=mesh,
        in_specs=(rows, rows, factors, factors, gains),
        out_specs=(rows, rows, factors, factors, gains),
        check_vma=False,
    )
```

```python
import functools

import jax
import jax.numpy as jnp
from jax import lax
from jax.experimental import pallas as pl
from jax.experimental.pallas import tpu as pltpu
from jax.sharding import PartitionSpec as P

BLOCK = 256
LAYERS = 2
ROW_AXES = ("chan", "bfly")
F32 = jnp.float32
BF16 = jnp.bfloat16


def to_columns(values):
    return lax.all_to_all(values, ROW_AXES, split_axis=1, concat_axis=0, tiled=True)


def to_rows(values):
    return lax.all_to_all(values, ROW_AXES, split_axis=0, concat_axis=1, tiled=True)


def stationary(features, cotangent, right_factor, left_factor, mixing):
    blocks = right_factor.shape[1]
    samples = features.shape[1]
    pairs = lax.axis_size("bfly")

    def flip(values):
        grouped = values.reshape((-1, pairs // 2, 2, blocks) + values.shape[1:])
        return grouped[:, :, ::-1].reshape(values.shape)

    left_bf = left_factor.astype(jnp.bfloat16)
    gains = lax.all_to_all(mixing, ROW_AXES, split_axis=3, concat_axis=2, tiled=True)
    height = features.reshape(blocks, BLOCK, samples)
    saved = []
    for layer in range(LAYERS):
        self_gain = gains[layer, 0][:, :, None]
        cross_gain = gains[layer, 1][:, :, None]
        mixed_u = to_columns(
            jnp.einsum(
                "bis,bij->bjs", height, right_factor[layer], preferred_element_type=jnp.float32
            ).astype(jnp.bfloat16)
        )
        mixed_v = (
            self_gain * mixed_u.astype(jnp.float32) + cross_gain * flip(mixed_u).astype(jnp.float32)
        ).astype(jnp.bfloat16)
        outer = jnp.einsum(
            "bjs,jbk->kjs", mixed_v, left_bf[layer], preferred_element_type=jnp.float32
        ).astype(jnp.bfloat16)
        activation = to_rows(outer)
        saved.append((height, mixed_u, mixed_v, activation))
        height = (height.astype(jnp.float32) + jax.nn.silu(activation.astype(jnp.float32))).astype(
            jnp.bfloat16
        )
    output = height.reshape(blocks * BLOCK, samples)
    grad = cotangent.reshape(blocks, BLOCK, samples)
    rights = [None] * LAYERS
    lefts = [None] * LAYERS
    mixes = [None] * LAYERS
    for layer in reversed(range(LAYERS)):
        height_in, mixed_u, mixed_v, activation = saved[layer]
        self_gain = gains[layer, 0][:, :, None]
        cross_gain = gains[layer, 1][:, :, None]
        before = activation.astype(jnp.float32)
        logistic = jax.nn.sigmoid(before)
        error = (grad.astype(jnp.float32) * logistic * (1.0 + before * (1.0 - logistic))).astype(
            jnp.bfloat16
        )
        error_cols = to_columns(error)
        grad_v = jnp.einsum(
            "jbk,kjs->bjs", left_bf[layer], error_cols, preferred_element_type=jnp.float32
        ).astype(jnp.bfloat16)
        grad_vf = grad_v.astype(jnp.float32)
        carried = (cross_gain * grad_vf).astype(jnp.bfloat16)
        grad_u = to_rows(
            (self_gain * grad_vf + flip(carried).astype(jnp.float32)).astype(jnp.bfloat16)
        )
        lefts[layer] = jnp.einsum(
            "bjs,kjs->jbk", mixed_v, error_cols, preferred_element_type=jnp.float32
        )
        mixes[layer] = jnp.stack(
            [
                jnp.sum(grad_vf * mixed_u.astype(jnp.float32), axis=2),
                jnp.sum(grad_vf * flip(mixed_u).astype(jnp.float32), axis=2),
            ]
        )
        rights[layer] = jnp.einsum(
            "bis,bjs->bij", height_in, grad_u, preferred_element_type=jnp.float32
        )
        back_term = jnp.einsum(
            "bij,bjs->bis", right_factor[layer], grad_u, preferred_element_type=jnp.float32
        )
        grad = (grad.astype(jnp.float32) + back_term).astype(jnp.bfloat16)
    all_mix = lax.psum(jnp.stack(mixes), "samp")
    all_mix = lax.all_to_all(all_mix, ROW_AXES, split_axis=2, concat_axis=3, tiled=True)
    all_right = jnp.stack(
        [lax.psum(part.astype(jnp.bfloat16), "samp").astype(jnp.float32) for part in rights]
    )
    all_left = jnp.stack(
        [lax.psum(part.astype(jnp.bfloat16), "samp").astype(jnp.float32) for part in lefts]
    )
    return (output, grad.reshape(blocks * BLOCK, samples), all_right, all_left, all_mix)


def gated(kernel, count, gates):
    def run(*refs):
        kernel(*refs[:count], *refs[count + len(gates) :])

    return run, [pl.BlockSpec(memory_space=pl.ANY)] * len(gates)


def shuffle_rows(where, source, target, half):
    own_x, own_core = where[0], where[1] ^ pl.program_id(0)
    for group in range(BLOCK // (4 * half)):
        for dx in range(2):
            for dc in range(2):
                start = 4 * half * group + 2 * half * (own_x ^ dx) + half * (own_core ^ dc)
                rows = pl.ds(pl.multiple_of(start, half), half)
                here = pl.ds(4 * half * group + 2 * half * dx + half * dc, half)
                yield rows, here


def split_kernel(where, array_ref, pieces_ref):
    half = array_ref.shape[0]
    for rows, here in shuffle_rows(where, array_ref, pieces_ref, half):
        pieces_ref[0, 0, :, here, :] = array_ref[:, rows, :]


def merge_kernel(where, pieces_ref, array_ref):
    half = array_ref.shape[0]
    for rows, here in shuffle_rows(where, array_ref, pieces_ref, half):
        array_ref[:, rows, :] = pieces_ref[0, 0, :, here, :]


def split(where, array, chans, *gates):
    blocks, units, samples = array.shape
    half, part = blocks // 2, samples // chans
    kernel, extra = gated(split_kernel, 2, gates)
    return pl.pallas_call(
        kernel,
        out_shape=jax.ShapeDtypeStruct((2, chans, half, units, part), array.dtype),
        grid_spec=pltpu.PrefetchScalarGridSpec(
            num_scalar_prefetch=1,
            grid=(2, chans),
            in_specs=[pl.BlockSpec((half, units, part), lambda e, d, w: (w[1] ^ e, 0, w[2] ^ d))]
            + extra,
            out_specs=pl.BlockSpec((1, 1, half, units, part), lambda e, d, w: (e, d, 0, 0, 0)),
        ),
        cost_estimate=pl.CostEstimate(flops=0, bytes_accessed=4 * array.size, transcendentals=0),
        name="split",
    )(where, array, *gates)


def merge(where, pieces, *gates):
    _, chans, half, units, part = pieces.shape
    kernel, extra = gated(merge_kernel, 2, gates)
    return pl.pallas_call(
        kernel,
        out_shape=jax.ShapeDtypeStruct((2 * half, units, chans * part), pieces.dtype),
        grid_spec=pltpu.PrefetchScalarGridSpec(
            num_scalar_prefetch=1,
            grid=(2, chans),
            in_specs=[pl.BlockSpec((1, 1, half, units, part), lambda e, d, w: (e, d, 0, 0, 0))]
            + extra,
            out_specs=pl.BlockSpec((half, units, part), lambda e, d, w: (w[1] ^ e, 0, w[2] ^ d)),
        ),
        cost_estimate=pl.CostEstimate(flops=0, bytes_accessed=4 * pieces.size, transcendentals=0),
        name="merge",
    )(where, pieces, *gates)


HOPS = ((0, 0), (0, 1), (1, 0), (1, 1))
VMEM_LIMIT = 48 * 1024 * 1024


def cost(flops, *arrays):
    size = sum(a.size * a.dtype.itemsize for a in arrays)
    return pl.CostEstimate(flops=int(flops), bytes_accessed=int(size), transcendentals=0)


def join(pieces, index, half, swap=0):
    groups = pieces[0].shape[1] // half
    return jnp.concatenate(
        [
            pieces[2 * (dx ^ swap) + dc][index, half * g : half * g + half, :]
            for g in range(groups)
            for dx, dc in HOPS
        ],
        axis=0,
    )


def deal(pieces, index, half, value):
    groups = pieces[0].shape[1] // half
    for g in range(groups):
        for hop in range(4):
            start = half * (4 * g + hop)
            pieces[hop][index, half * g : half * g + half, :] = value[start : start + half, :]


def swap_dx(value, half):
    step = 2 * half
    return jnp.concatenate(
        [value[step * (i ^ 1) : step * (i ^ 1) + step, :] for i in range(value.shape[0] // step)],
        axis=0,
    )


def units_forward_kernel(half, *refs):
    u, (gain_ref, left_ref), v_ref, t = refs[:4], refs[4:6], refs[6], refs[7:]
    for i in range(left_ref.shape[0]):
        mine = join(u, i, half).astype(F32)
        partner = join(u, i, half, 1).astype(F32)
        v = (gain_ref[0, 0, :, i : i + 1] * mine + gain_ref[1, 0, :, i : i + 1] * partner).astype(BF16)
        v_ref[i] = v
        out = lax.dot_general(left_ref[i], v, (((0,), (0,)), ((), ())), preferred_element_type=F32)
        deal(t, i, half, out.astype(BF16))


def units_backward_kernel(half, *refs):
    e, u, (gain_ref, left_ref) = refs[:4], refs[4:8], refs[8:10]
    du, mix_ref = refs[10:14], refs[14]
    for i in range(left_ref.shape[0]):
        dv = jnp.dot(left_ref[i], join(e, i, half), preferred_element_type=F32)
        dv = dv.astype(BF16).astype(F32)
        mine = join(u, i, half).astype(F32)
        mix_ref[0, 0, :, i : i + 1] = jnp.sum(dv * mine, axis=1, keepdims=True)
        mix_ref[1, 0, :, i : i + 1] = jnp.sum(dv * swap_dx(mine, half), axis=1, keepdims=True)
        carried = (gain_ref[1, 0, :, i : i + 1] * dv).astype(BF16).astype(F32)
        value = gain_ref[0, 0, :, i : i + 1] * dv + swap_dx(carried, half)
        deal(du, i, half, value.astype(BF16))


TILE = 8


def units_forward(u, gain, left, half, *gates):
    own, part = u[0].shape[0], u[0].shape[2]
    piece = pl.BlockSpec((TILE, own, part), lambda i: (i, 0, 0))
    full = pl.BlockSpec((TILE, BLOCK, part), lambda i: (i, 0, 0))
    gains = pl.BlockSpec((2, 1, BLOCK, TILE), lambda i: (0, i, 0, 0))
    weight = pl.BlockSpec((TILE, BLOCK, BLOCK), lambda i: (i, 0, 0))
    shape = jax.ShapeDtypeStruct((own, own, part), BF16)
    v_shape = jax.ShapeDtypeStruct((own, BLOCK, part), BF16)
    kernel, extra = gated(functools.partial(units_forward_kernel, half), 6, gates)
    out = pl.pallas_call(
        kernel,
        grid=(own // TILE,),
        in_specs=[piece] * 4 + [gains, weight] + extra,
        out_specs=[full] + [piece] * 4,
        out_shape=[v_shape] + [shape] * 4,
        compiler_params=pltpu.CompilerParams(vmem_limit_bytes=VMEM_LIMIT),
        cost_estimate=cost(2 * own * BLOCK * BLOCK * part, left, v_shape, *u, *u),
        name="units_forward",
    )(*u, gain, left, *gates)
    return out[0], out[1:]


def units_backward(e, u, gain, left, half, *gates):
    own, part = u[0].shape[0], u[0].shape[2]
    piece = pl.BlockSpec((TILE, own, part), lambda i: (i, 0, 0))
    gains = pl.BlockSpec((2, 1, BLOCK, TILE), lambda i: (0, i, 0, 0))
    weight = pl.BlockSpec((TILE, BLOCK, BLOCK), lambda i: (i, 0, 0))
    shape = jax.ShapeDtypeStruct((own, own, part), BF16)
    kernel, extra = gated(functools.partial(units_backward_kernel, half), 10, gates)
    out = pl.pallas_call(
        kernel,
        grid=(own // TILE,),
        in_specs=[piece] * 8 + [gains, weight] + extra,
        out_specs=[piece] * 4 + [gains],
        out_shape=[shape] * 4 + [jax.ShapeDtypeStruct(gain.shape, F32)],
        compiler_params=pltpu.CompilerParams(vmem_limit_bytes=VMEM_LIMIT),
        cost_estimate=cost(2 * own * BLOCK * BLOCK * part, left, *u, *u, *u),
        name="units_backward",
    )(*e, *u, gain, left, *gates)
    return out[:4], out[4]


def gather_rows(pieces, scratch, half):
    for hop in range(4):
        turned = jnp.swapaxes(pieces[hop][...], 0, 1)
        for g in range(pieces[hop].shape[0] // half):
            start = half * (4 * g + hop)
            scratch[:, start : start + half, :] = turned[:, half * g : half * g + half, :]


def scatter_rows(scratch, pieces, half):
    for hop in range(4):
        for g in range(pieces[hop].shape[0] // half):
            start = half * (4 * g + hop)
            pieces[hop][half * g : half * g + half] = jnp.swapaxes(
                scratch[:, start : start + half, :], 0, 1
            )


def error_of(grad, before):
    logistic = jax.nn.sigmoid(before)
    return (grad * logistic * (1.0 + before * (1.0 - logistic))).astype(BF16)


def first_kernel(half, h_ref, right_ref, *refs):
    u, scratch = refs[:4], refs[4]
    for b in range(h_ref.shape[0]):
        out = lax.dot_general(
            right_ref[b], h_ref[b], (((0,), (0,)), ((), ())), preferred_element_type=F32
        )
        scratch[b] = out.astype(BF16)
    scatter_rows(scratch, u, half)


def middle_kernel(half, *refs):
    t, (h_ref, right_ref), (act_ref, next_ref), u = refs[:4], refs[4:6], refs[6:8], refs[8:12]
    scratch = refs[12]
    gather_rows(t, act_ref, half)
    for b in range(h_ref.shape[0]):
        height = (h_ref[b].astype(F32) + jax.nn.silu(act_ref[b].astype(F32))).astype(BF16)
        next_ref[b] = height
        out = lax.dot_general(
            right_ref[b], height, (((0,), (0,)), ((), ())), preferred_element_type=F32
        )
        scratch[b] = out.astype(BF16)
    scatter_rows(scratch, u, half)


def last_kernel(half, *refs):
    t, (h_ref, g_ref), next_ref, e = refs[:4], refs[4:6], refs[6], refs[7:11]
    act, scratch = refs[11:13]
    gather_rows(t, act, half)
    for b in range(h_ref.shape[0]):
        before = act[b].astype(F32)
        next_ref[b] = (h_ref[b].astype(F32) + jax.nn.silu(before)).astype(BF16)
        scratch[b] = error_of(g_ref[b].astype(F32), before)
    scatter_rows(scratch, e, half)


def back_kernel(half, *refs):
    du, (g_ref, right_ref, act_ref), (rows_ref, next_ref), e = refs[:4], refs[4:7], refs[7:9], refs[9:13]
    scratch = refs[13]
    gather_rows(du, rows_ref, half)
    for b in range(g_ref.shape[0]):
        term = jnp.dot(right_ref[b], rows_ref[b], preferred_element_type=F32)
        grad = (g_ref[b].astype(F32) + term).astype(BF16)
        next_ref[b] = grad
        scratch[b] = error_of(grad.astype(F32), act_ref[b].astype(F32))
    scatter_rows(scratch, e, half)


def final_kernel(half, *refs):
    du, (g_ref, right_ref), (rows_ref, next_ref) = refs[:4], refs[4:6], refs[6:8]
    gather_rows(du, rows_ref, half)
    for b in range(g_ref.shape[0]):
        term = jnp.dot(right_ref[b], rows_ref[b], preferred_element_type=F32)
        next_ref[b] = (g_ref[b].astype(F32) + term).astype(BF16)


def rows_call(kernel, half, ins, outs, scratches, *gates):
    own, part = 4 * half, 128
    rows = 16
    specs = {
        "p": pl.BlockSpec((own, rows, part), lambda i: (0, i, 0)),
        "r": pl.BlockSpec((rows, BLOCK, part), lambda i: (i, 0, 0)),
        "w": pl.BlockSpec((rows, BLOCK, BLOCK), lambda i: (i, 0, 0)),
    }
    shapes = {"p": (own, own, part), "r": (own, BLOCK, part)}
    out_shape = [jax.ShapeDtypeStruct(shapes[kind], BF16) for kind in outs]
    kinds = [kind for kind, _ in ins]
    arrays = [array for _, array in ins]
    flops = 2 * own * BLOCK * BLOCK * part if "w" in kinds else 0
    run, extra = gated(functools.partial(kernel, half), len(ins), gates)
    return pl.pallas_call(
        run,
        grid=(own // rows,),
        in_specs=[specs[kind] for kind in kinds] + extra,
        out_specs=[specs[kind] for kind in outs],
        out_shape=out_shape,
        scratch_shapes=[pltpu.VMEM((rows, BLOCK, part), BF16)] * scratches,
        compiler_params=pltpu.CompilerParams(vmem_limit_bytes=VMEM_LIMIT),
        cost_estimate=cost(flops, *arrays, *out_shape),
        name=kernel.__name__,
    )(*arrays, *gates)


def left_sum_kernel(half, where, *refs):
    v, e, out_ref = refs[:2], (refs[2:6], refs[6:10]), refs[10]
    for i in range(out_ref.shape[1]):
        total = 0.0
        for q in range(2):
            total += lax.dot_general(
                v[q][i], join(e[q], i, half), (((1,), (1,)), ((), ())), preferred_element_type=F32
            )
        out_ref[0, i] = total.astype(BF16)


def right_sum_kernel(half, where, *refs):
    h, du, out_ref = refs[:2], refs[2:4], refs[4]
    for i in range(out_ref.shape[1]):
        total = 0.0
        for q in range(2):
            total += lax.dot_general(
                h[q][i], du[q][i], (((1,), (1,)), ((), ())), preferred_element_type=F32
            )
        out_ref[0, i] = total.astype(BF16)


def sum_call(kernel, where, other, half, arrays, *gates):
    quarter = half // 2
    chans = arrays[0].shape[0] // half
    out_shape = jax.ShapeDtypeStruct((chans, quarter, BLOCK, BLOCK), BF16)

    def tile(g, w):
        return (2 * g + (w[3] ^ other), 0, 0)

    run, extra = gated(functools.partial(kernel, half), 1 + len(arrays), gates)
    return pl.pallas_call(
        run,
        out_shape=out_shape,
        grid_spec=pltpu.PrefetchScalarGridSpec(
            num_scalar_prefetch=1,
            grid=(chans,),
            in_specs=[pl.BlockSpec((quarter,) + a.shape[1:], tile) for a in arrays] + extra,
            out_specs=pl.BlockSpec((1, quarter, BLOCK, BLOCK), lambda g, w: (g, 0, 0, 0)),
        ),
        compiler_params=pltpu.CompilerParams(vmem_limit_bytes=VMEM_LIMIT),
        cost_estimate=cost(4 * chans * quarter * BLOCK * BLOCK * 128, *arrays),
        name=kernel.__name__,
    )(where, *arrays, *gates)


def weave_kernel(where, mine_ref, other_ref, out_ref):
    @pl.when(pl.program_id(1) == where[3])
    def _():
        out_ref[0, 0] = mine_ref[0]

    @pl.when(pl.program_id(1) != where[3])
    def _():
        out_ref[0, 0] = other_ref[0]


def weave(where, mine, other, *gates):
    block = (1,) + mine.shape[1:]
    spec = pl.BlockSpec(block, lambda g, y, w: (g, 0, 0, 0))
    kernel, extra = gated(weave_kernel, 3, gates)
    return pl.pallas_call(
        kernel,
        out_shape=jax.ShapeDtypeStruct(mine.shape[:1] + (2,) + mine.shape[1:], mine.dtype),
        grid_spec=pltpu.PrefetchScalarGridSpec(
            num_scalar_prefetch=1,
            grid=(mine.shape[0], 2),
            in_specs=[spec, spec] + extra,
            out_specs=pl.BlockSpec((1,) + block, lambda g, y, w: (g, y, 0, 0, 0)),
        ),
        cost_estimate=pl.CostEstimate(flops=0, bytes_accessed=8 * mine.size, transcendentals=0),
        name="weave",
    )(where, mine, other, *gates)


def prepare_kernel(half, where, factor_ref, out_ref):
    mask = 2 * half * where[0] + half * where[1]
    rows = lax.broadcasted_iota(jnp.int32, (BLOCK, BLOCK), 0)
    columns = lax.broadcasted_iota(jnp.int32, (BLOCK, BLOCK), 1)
    swap = jnp.where(rows == (columns ^ mask), 1.0, 0.0).astype(BF16)
    for i in range(out_ref.shape[0]):
        turned = jnp.dot(swap, factor_ref[0, i].astype(BF16), preferred_element_type=F32)
        out_ref[i] = jnp.dot(
            turned.astype(BF16), swap, preferred_element_type=F32
        ).astype(BF16)


def prepare(where, factor, layer, half, *gates):
    kernel, extra = gated(functools.partial(prepare_kernel, half), 2, gates)
    block = (1, half // 2) + factor.shape[2:]
    whole = factor.shape[1] == block[1]
    spec = pl.BlockSpec(block, lambda i, w: (layer, 0 if whole else 2 * w[1] + w[3], 0, 0))
    return pl.pallas_call(
        kernel,
        out_shape=jax.ShapeDtypeStruct(block[1:], BF16),
        grid_spec=pltpu.PrefetchScalarGridSpec(
            num_scalar_prefetch=1,
            grid=(1,),
            in_specs=[spec] + extra,
            out_specs=pl.BlockSpec(block[1:], lambda i, w: (0, 0, 0)),
        ),
        cost_estimate=pl.CostEstimate(flops=2**29, bytes_accessed=2**22, transcendentals=0),
        name="prepare",
    )(where, factor, *gates)


def copy_kernel(array_ref, out_ref):
    out_ref[...] = array_ref[...]


def copy_after(array, *gates):
    kernel, extra = gated(copy_kernel, 1, gates)
    spec = pl.BlockSpec((1,) + array.shape[1:], lambda g: (g, 0, 0, 0))
    return pl.pallas_call(
        kernel,
        out_shape=jax.ShapeDtypeStruct(array.shape, BF16),
        grid=array.shape[:1],
        in_specs=[spec] + extra,
        out_specs=spec,
        cost_estimate=pl.CostEstimate(flops=0, bytes_accessed=4 * array.size, transcendentals=0),
        name="copy_after",
    )(array, *gates)


def total_kernel(keep_ref, got_ref, out_ref):
    out_ref[...] = (keep_ref[...].astype(F32) + got_ref[...].astype(F32)).astype(BF16)


def total_of(keep, got, *gates):
    kernel, extra = gated(total_kernel, 2, gates)
    spec = pl.BlockSpec((1,) + keep.shape[1:], lambda g: (g, 0, 0, 0))
    return pl.pallas_call(
        kernel,
        out_shape=jax.ShapeDtypeStruct(keep.shape, BF16),
        grid=keep.shape[:1],
        in_specs=[spec, spec] + extra,
        out_specs=spec,
        cost_estimate=pl.CostEstimate(flops=0, bytes_accessed=6 * keep.size, transcendentals=0),
        name="total_of",
    )(keep, got, *gates)


def after(value, *others):
    return lax.optimization_barrier((value,) + others)[0]


def planes(features, cotangent, right_factor, left_factor, mixing):
    blocks = right_factor.shape[1]
    samples = features.shape[1]
    chans, samps = lax.axis_size("chan"), lax.axis_size("samp")
    half, quarter, part = blocks // 2, blocks // 4, samples // chans
    own = chans * half
    chan, own_x, samp = lax.axis_index("chan"), lax.axis_index("bfly"), lax.axis_index("samp")
    row, core = samp // 2, samp % 2
    where = jnp.stack([own_x, core, chan, row]).astype(jnp.int32)

    def over_chan(values, distance):
        return lax.ppermute(values, "chan", [(i, i ^ distance) for i in range(chans)])

    def over_samp(values, distance):
        return lax.ppermute(values, "samp", [(i, i ^ distance) for i in range(samps)])

    def in_plane(values, dx, dc):
        if dx == 0 and dc == 0:
            return values
        route = [(i, i ^ (dx * samps + dc)) for i in range(2 * samps)]
        return lax.ppermute(values, ("bfly", "samp"), route)

    def enter(array, *gates):
        pieces = split(where, array.reshape(blocks, BLOCK, samples), chans, *gates)
        mine, other = pieces[0], over_samp(pieces[1], 1)
        chunks, arrived = [], []
        for core_of in range(2):
            chunk = jnp.zeros((chans, half, BLOCK, part), BF16)
            for distance in range(chans):
                piece = jnp.where(core == core_of, mine[distance], other[distance])
                if distance:
                    piece = over_chan(piece, distance)
                    arrived.append(piece)
                chunk = lax.dynamic_update_index_in_dim(chunk, piece, chan ^ distance, 0)
            chunks.append(chunk.reshape(own, BLOCK, part))
        return pieces, chunks, arrived[: chans - 1]

    def leave_planes(chunks):
        arrived = []
        for chunk in chunks:
            chunk = chunk.reshape(chans, half, BLOCK, part)
            arrived.append([])
            for distance in range(chans):
                piece = lax.dynamic_index_in_dim(chunk, chan ^ distance, 0, keepdims=False)
                arrived[-1].append(over_chan(piece, distance) if distance else piece)
        return arrived

    def leave_chip(arrived, *gates):
        first, second = (jnp.stack(pieces) for pieces in arrived)
        keep = jnp.where(core == 0, first, second)
        got = over_samp(jnp.where(core == 0, second, first), 1)
        return merge(where, jnp.stack([keep, got]), *gates).reshape(blocks * BLOCK, samples)

    def gather_row(mine, *gates):
        return weave(where, mine, over_samp(mine, 2), *gates).reshape(own, BLOCK, BLOCK)

    def sum_factor(kernel, arrays, *gates):
        send = sum_call(kernel, where, 1, half, arrays, *gates)
        keep = sum_call(kernel, where, 0, half, arrays, send)
        return keep, send, over_samp(send, 2)

    def spread_factor(parts, *gates):
        total = total_of(parts[0], parts[2], *gates)
        return lax.psum_scatter(total, "chan", scatter_dimension=0, tiled=False)

    def finish_factor(total, *gates):
        total = prepare(where, total[None], 0, half, *gates)
        total = lax.all_gather(total, "samp")
        whole = total.reshape(2, 2, quarter, BLOCK, BLOCK)
        return total, jnp.swapaxes(whole, 0, 1).reshape(blocks, BLOCK, BLOCK).astype(F32)

    def swap_pieces(pieces):
        return [in_plane(piece, dx, dc) for piece, (dx, dc) in zip(pieces, HOPS)]

    both = range(2)
    ready = prepare(where, right_factor, 0, half)
    right_mine = lax.all_gather(ready, "chan")
    entered, features_in, arrival = enter(features, ready)
    heights = [features_in]
    ready = prepare(where, left_factor, 0, half, entered)
    left_mine = lax.all_gather(ready, "chan")
    left_other = over_samp(left_mine, 2)
    rights_in = [gather_row(copy_after(right_mine, *arrival)), None]
    gains = lax.all_gather(after(mixing, ready), ROW_AXES, axis=2, tiled=True)
    gains = gains.reshape(LAYERS, 2, chans, 2, 2, half, BLOCK)
    gains = jnp.where(own_x == 1, gains[:, :, :, ::-1], gains)
    gains = jnp.where(core == 1, gains[:, :, :, :, ::-1], gains)
    gains = gains.reshape(LAYERS, 2, BLOCK, chans, 4, half)
    gains = lax.dynamic_index_in_dim(gains, 2 * own_x + core, 4, keepdims=False)
    gains = gains.reshape(LAYERS, 2, BLOCK, own // TILE, TILE).swapaxes(2, 3)

    mixed_u, mixed_v, act = [[None] * 2 for _ in range(LAYERS)], [[None] * 2 for _ in range(LAYERS)], [None] * 2
    outer, sent = [None] * 2, [None] * 2
    for q in both:
        ins = [("r", heights[0][q]), ("w", rights_in[0])]
        gates = [] if q == 0 else [sent[0][0], left_other, *mixed_u[0][0][1:]]
        sent[q] = rows_call(first_kernel, half, ins, "pppp", 1, *gates)
        mixed_u[0][q] = swap_pieces(sent[q])
    first = sent[:]
    lefts_in = [weave(where, left_mine, left_other, first[0][0]).reshape(own, BLOCK, BLOCK), None]
    right_mine = lax.all_gather(prepare(where, right_factor, 1, half, first[0][0]), "chan")
    left_mine = lax.all_gather(prepare(where, left_factor, 1, half, first[1][0]), "chan")
    for q in both:
        gates = [first[1][0]] if q == 0 else [sent[0][0]]
        mixed_v[0][q], sent[q] = units_forward(mixed_u[0][q], gains[0], lefts_in[0], half, *gates)
        outer[q] = swap_pieces(sent[q])
    rights_in[1] = gather_row(right_mine, sent[0][0])
    _, grad, _ = enter(cotangent, sent[0][0])
    heights.append([None] * 2)
    last = sent[1][0]
    for q in both:
        ins = [("p", p) for p in outer[q]] + [("r", heights[0][q]), ("w", rights_in[1])]
        gates = [last] if q == 0 else [sent[0][0]]
        out = rows_call(middle_kernel, half, ins, "rrpppp", 1, *gates)
        act[q], heights[1][q] = out[:2]
        sent[q] = out[2:]
        mixed_u[1][q] = swap_pieces(out[2:])
    lefts_in[1] = gather_row(left_mine, sent[0][0])
    last = sent[1][0]
    for q in both:
        gates = [last] if q == 0 else [sent[0][0]]
        mixed_v[1][q], sent[q] = units_forward(mixed_u[1][q], gains[1], lefts_in[1], half, *gates)
        outer[q] = swap_pieces(sent[q])
    error, final = [None] * 2, [None] * 2
    last = sent[1][0]
    for q in both:
        ins = [("p", p) for p in outer[q]] + [("r", heights[1][q]), ("r", grad[q])]
        gates = [last] if q == 0 else [final[0]]
        out = rows_call(last_kernel, half, ins, "rpppp", 2, *gates)
        final[q] = out[0]
        error[q] = swap_pieces(out[1:])
    out_parts = leave_planes(final)
    mix = [None] * LAYERS
    grad_u = [None] * 2
    for q in both:
        gates = [final[1]] if q == 0 else [sent[0][0], out_parts[0][1]]
        sent[q], mix_q = units_backward(error[q], mixed_u[1][q], gains[1], lefts_in[1], half, *gates)
        mix[1] = mix_q if q == 0 else mix[1] + mix_q
        grad_u[q] = swap_pieces(sent[q])
    left_1 = sum_factor(left_sum_kernel, mixed_v[1] + error[0] + error[1], sent[1][0])
    rows = [None] * 2
    error = [None] * 2
    last = sent[1][0]
    for q in both:
        ins = [("p", p) for p in grad_u[q]]
        ins += [("r", grad[q]), ("w", rights_in[1]), ("r", act[q])]
        gates = [last, left_1[1], out_parts[0][2]] if q == 0 else [sent[0][0], out_parts[0][3]]
        out = rows_call(back_kernel, half, ins, "rrpppp", 1, *gates)
        rows[q], grad[q] = out[:2]
        sent[q] = out[2:]
        error[q] = swap_pieces(out[2:])
    left_1 = spread_factor(left_1, sent[1][0])
    right_1 = sum_factor(right_sum_kernel, heights[1] + rows)
    for q in both:
        gates = [right_1[1], out_parts[1][1]] if q == 0 else [sent[0][0], out_parts[1][2]]
        sent[q], mix_q = units_backward(error[q], mixed_u[0][q], gains[0], lefts_in[0], half, *gates)
        mix[0] = mix_q if q == 0 else mix[0] + mix_q
        grad_u[q] = swap_pieces(sent[q])
    right_1 = spread_factor(right_1, sent[1][0])
    left_0 = sum_factor(left_sum_kernel, mixed_v[0] + error[0] + error[1], sent[1][0])
    left_1 = finish_factor(left_1, sent[1][0])
    rows, in_parts = [None] * 2, []
    for q in both:
        ins = [("p", p) for p in grad_u[q]] + [("r", grad[q]), ("w", rights_in[0])]
        gates = [left_0[1], sent[1][0], out_parts[1][3]] if q == 0 else [grad[0], left_1[0], *in_parts[0][1:]]
        rows[q], grad[q] = rows_call(final_kernel, half, ins, "rr", 0, *gates)
        in_parts += leave_planes([grad[q]])
    output = leave_chip(out_parts, rows[0])
    left_0 = spread_factor(left_0, rows[0])
    right_0 = sum_factor(right_sum_kernel, heights[0] + rows)
    right_1 = finish_factor(right_1, rows[0])
    left_0 = finish_factor(left_0, right_0[1])
    right_0 = spread_factor(right_0, *in_parts[1][1:])
    right_0 = finish_factor(right_0, left_0[0], right_1[0], output)
    feature_grad = leave_chip(in_parts)
    mix = jnp.stack(mix).swapaxes(2, 3).reshape(LAYERS, 2, chans, 2, 2, half, own)
    mix = jnp.where(own_x == 1, mix[:, :, :, ::-1], mix)
    mix = jnp.where(core == 1, mix[:, :, :, :, ::-1], mix)
    mix = lax.psum_scatter(mix, "chan", scatter_dimension=2, tiled=False)
    mix = lax.all_gather(mix, ("bfly", "samp")).reshape((2, 2, 2) + mix.shape)
    mix = mix[:, 0] + mix[:, 1]
    mix = lax.dynamic_index_in_dim(mix, own_x, 4, keepdims=False)
    mix = mix.reshape(2, 2, LAYERS, 2, blocks, chans, half)
    mix = mix.transpose(2, 3, 4, 5, 0, 1, 6).reshape(LAYERS, 2, blocks, BLOCK)
    grad_right_0, grad_right_1 = right_0[1], right_1[1]
    grad_left_0, grad_left_1 = left_0[1], left_1[1]
    rights = jnp.stack([grad_right_0, grad_right_1])
    return (output, feature_grad, rights, jnp.stack([grad_left_0, grad_left_1]), mix)


def solution(mesh):
    sizes = dict(mesh.shape)
    fits = sizes["chan"] == 4 and sizes["bfly"] == 2 and sizes["samp"] == 4
    local = planes if fits else stationary
    rows = P(ROW_AXES, "samp")
    factors = P(None, ROW_AXES, None, None)
    gains = P(None, None, ROW_AXES, None)
    return jax.shard_map(
        local,
        mesh=mesh,
        in_specs=(rows, rows, factors, factors, gains),
        out_specs=(rows, rows, factors, factors, gains),
        check_vma=False,
    )
```
